32 devices in a mesh: seq: 8 (over z, y), neur: 4 (over x, core).
Axes of the slice: x: 2, y: 2, z: 4, core: 2. Of those that a mesh axis runs over, the one named last changes fastest.
Arguments:
- tokens: bfloat16 [8, 704, 2000], P('seq', None, 'neur'), may hold values from -8 to 8
- w_first: bfloat16 [2000, 2000], P(None, 'neur'), may hold values from -0.125 to 0.125
- gain_first: float32 [2000], P('neur'), may hold values from 0.5 to 1.5
- shift_first: float32 [2000], P('neur'), may hold values from -0.5 to 0.5
- decay_first: float32 [2000], P('neur'), may hold values from 0 to 0.999
- w_second: bfloat16 [2000, 2000], P(None, 'neur'), may hold values from -0.125 to 0.125
- gain_second: float32 [2000], P('neur'), may hold values from 0.5 to 1.5
- shift_second: float32 [2000], P('neur'), may hold values from -0.5 to 0.5
- decay_second: float32 [2000], P('neur'), may hold values from 0 to 0.999
- cotangent: bfloat16 [8, 704, 2000], P('seq', None, 'neur'), may hold values from -6 to 6
- running_mean: float32 [2, 2000], P(None, 'neur'), may hold values from -6 to 6
- running_var: float32 [2, 2000], P(None, 'neur'), may hold values from 0.5 to 2
Outputs:
- first_out: bfloat16 [8, 704, 2000], P('seq', None, 'neur')
- second_out: bfloat16 [8, 704, 2000], P('seq', None, 'neur')
- input_grad: float32 [8, 704, 2000], P('seq', None, 'neur')
- grad_w_first: float32 [2000, 2000], P(None, 'neur')
- grad_w_second: float32 [2000, 2000], P(None, 'neur')
- grad_gain: float32 [2, 2000], P(None, 'neur')
- grad_shift: float32 [2, 2000], P(None, 'neur')
- grad_decay: float32 [2, 2000], P(None, 'neur')
- new_mean: float32 [2, 2000], P(None, 'neur')
- new_var: float32 [2, 2000], P(None, 'neur')
The draws below stay inside these ranges and needn't reach their ends.
All inputs are finite; a program needn't handle non-finite values.
Results may differ from the reference program's by a relative error of at most 0.0053.
Values may be sent and summed in bfloat16 or wider, within the bound.
No kernel may reach another device: no remote copies, remote signals or barrier semaphores. Data moves between devices by JAX's collectives and lax.ppermute only.
A program may use at most 128 MiB of HBM per device.

```python
import math
import jax
import jax.numpy as jnp
from jax import lax

D_IN = 2000
HID = 2000
LEN = 704
SEQS = 8


def draw_tokens(key, part):
    key = jax.random.fold_in(key, 11)
    first_key = jax.random.fold_in(key, 0)
    ramp = 3.0 ** (jnp.arange(SEQS, dtype=jnp.float32) / max(SEQS - 1, 1))
    values = jax.random.normal(first_key, (SEQS, LEN, D_IN), jnp.float32)
    values = values * ramp[:, None, None]
    return jnp.clip(values, -8.0, 8.0).astype(jnp.bfloat16)


def decay_values(key, upper_exponent):
    exponent = jax.random.uniform(key, (HID,), jnp.float32, -3.0, upper_exponent)
    return jnp.clip(1.0 - 10.0 ** exponent, 0.0, 0.999)


def draw_decay_first(key, part):
    key = jax.random.fold_in(key, 23)
    return decay_values(key, 0.0)


def draw_decay_second(key, part):
    key = jax.random.fold_in(key, 37)
    return decay_values(key, 0.0)


def shard_levels(stream_key, extent, pieces, low, top_value):
    loudness, own = 1.0, jax.random.fold_in(stream_key, 6)
    for dim, blocks in pieces:
        steps = jnp.exp(jax.random.uniform(jax.random.fold_in(own, dim), (blocks,), jnp.float32, low / len(pieces), top_value / len(pieces)))
        loudness = loudness * jnp.repeat(steps, extent[dim] // blocks).reshape([-1 if axis == dim else 1 for axis in range(len(extent))])
    return loudness


def gaussian(rng, extent, spread, limit, cuts=(), kind=jnp.bfloat16):
    entries = spread * jax.random.normal(rng, extent, jnp.float32)
    if cuts:
        entries = entries * shard_levels(rng, extent, cuts, -0.22, 0.18)
    return jnp.clip(entries, -limit, limit).astype(kind)


def setup_inputs(seed: int = 0) -> dict:
    arg_keys = jax.random.split(jax.random.key(seed), 13)
    tokens = draw_tokens(jax.random.fold_in(arg_keys[12], 71), 0)
    w_first = gaussian(arg_keys[1], (D_IN, HID), D_IN ** -0.5, 0.125, ((1, 4),))
    gain_first = jnp.clip(1.0 + 0.1 * jax.random.normal(arg_keys[2], (HID,), jnp.float32), 0.5, 1.5)
    shift_first = jnp.clip(jax.random.uniform(arg_keys[3], (HID,), jnp.float32, -0.5, 0.5) * shard_levels(arg_keys[3], (HID,), ((0, 4),), -0.4, 0.0), -0.5, 0.5)
    decay_first = draw_decay_first(jax.random.fold_in(arg_keys[12], 71), 0)
    w_second = gaussian(arg_keys[5], (HID, HID), HID ** -0.5, 0.125, ((1, 4),))
    gain_second = jnp.clip(1.0 + 0.1 * jax.random.normal(arg_keys[6], (HID,), jnp.float32), 0.5, 1.5)
    shift_second = jnp.clip(jax.random.uniform(arg_keys[7], (HID,), jnp.float32, -0.5, 0.5) * shard_levels(arg_keys[7], (HID,), ((0, 4),), -0.4, 0.0), -0.5, 0.5)
    decay_second = draw_decay_second(jax.random.fold_in(arg_keys[12], 71), 0)
    cotangent = gaussian(arg_keys[9], (SEQS, LEN, HID), 1.0, 6.0, ((0, 8), (2, 4)))
    running_mean = gaussian(arg_keys[10], (2, HID), 1.0, 6.0, ((1, 4),), jnp.float32)
    running_var = jnp.clip(jnp.exp(math.log(2.0) - 1.3862944 * jax.random.uniform(arg_keys[11], (2, HID), jnp.float32) ** shard_levels(arg_keys[11], (2, HID), ((1, 4),), -0.2, 0.2)), 0.5, 2.0)
    return {"tokens": tokens, "w_first": w_first, "gain_first": gain_first, "shift_first": shift_first, "decay_first": decay_first, "w_second": w_second, "gain_second": gain_second, "shift_second": shift_second, "decay_second": decay_second, "cotangent": cotangent, "running_mean": running_mean, "running_var": running_var}


EPSILON = 1e-05
MOMENTUM = 0.1

@jax.custom_vjp
def lower_limit(v):
    return lax.optimization_barrier(v.astype(jnp.bfloat16)).astype(jnp.float32)

@jax.custom_vjp
def lower_limit_reverse(v):
    return v

def low_keep(v):
    return (lower_limit(v), None)

def low_pass(kept, grad):
    return (grad,)

def back_keep(v):
    return (v, None)

def back_low(kept, grad):
    return (lower_limit(grad),)
lower_limit.defvjp(low_keep, low_pass)
lower_limit_reverse.defvjp(back_keep, back_low)

def layer(input_pixels, input_weight, gain, shift, decay):
    projected_input = lower_limit_reverse(jnp.einsum('rcz,zq->rcq', lower_limit(input_pixels), input_weight, precision=lax.Precision.HIGHEST))
    batch_mean = lax.optimization_barrier(jnp.mean(projected_input, axis=(0, 1)))
    centered = projected_input - batch_mean
    batch_var = lax.optimization_barrier(jnp.mean(centered * centered, axis=(0, 1)))
    normalized = centered * lax.rsqrt(batch_var + EPSILON)
    driven = jnp.swapaxes(gain * normalized + shift, 0, 1)

    def advance(state, drive):
        after = jax.nn.softplus(drive + decay * state)
        return (after, after)
    _, states = lax.scan(jax.checkpoint(advance), jnp.zeros(driven.shape[1:], driven.dtype), driven)
    return (jnp.swapaxes(states, 0, 1), batch_mean, batch_var)

def forward(tokens, w_first, gain_first, shift_first, decay_first, w_second, gain_second, shift_second, decay_second):
    first, mean_one, var_one = layer(tokens, w_first, gain_first, shift_first, decay_first)
    second, mean_two, var_two = layer(first, w_second, gain_second, shift_second, decay_second)
    return ((first, second), (jnp.stack([mean_one, mean_two]), jnp.stack([var_one, var_two])))

def reference(tokens, w_first, gain_first, shift_first, decay_first, w_second, gain_second, shift_second, decay_second, cotangent, running_mean, running_var):
    primals = (tokens.astype(jnp.float32), w_first.astype(jnp.float32), gain_first, shift_first, decay_first, w_second.astype(jnp.float32), gain_second, shift_second, decay_second)
    outputs, pullback, stats = jax.vjp(forward, *primals, has_aux=True)
    first, second = outputs
    grads = pullback((jnp.zeros_like(first), cotangent.astype(jnp.float32)))
    means, variances = stats
    total_count = SEQS * LEN
    new_mean = (1.0 - MOMENTUM) * running_mean + MOMENTUM * means
    new_var = (1.0 - MOMENTUM) * running_var + MOMENTUM * variances * (total_count / (total_count - 1.0))
    return (first.astype(jnp.bfloat16), second.astype(jnp.bfloat16), grads[0], grads[1], grads[5], jnp.stack([grads[2], grads[6]]), jnp.stack([grads[3], grads[7]]), jnp.stack([grads[4], grads[8]]), new_mean, new_var)
```

```python
import functools
import math

import jax
import jax.numpy as jnp
from jax import lax
from jax.experimental import pallas as pl
from jax.experimental.pallas import tpu as pltpu
from jax.sharding import PartitionSpec as P

EPSILON = 1e-05
MOMENTUM = 0.1
LANE = 128
CHUNKS = 32
GROUPS = CHUNKS // 8
TOLERANCE = 1e-5
LOG2E = math.log2(math.e)
LN2 = math.log(2.0)
F32 = jnp.float32
BF16 = jnp.bfloat16
VMEM_BYTES = 50 * 1024 * 1024


def call(kernel, outs, scratch=(), flops=0, nbytes=0):
    return pl.pallas_call(
        kernel,
        out_shape=outs,
        scratch_shapes=list(scratch),
        compiler_params=pltpu.CompilerParams(vmem_limit_bytes=VMEM_BYTES),
        cost_estimate=pl.CostEstimate(flops=flops, bytes_accessed=nbytes, transcendentals=0),
    )


def shape(*dims, dtype=F32):
    return jax.ShapeDtypeStruct(dims, dtype)


def tiles_of(width):
    return [(j, j * LANE, min(LANE, width - j * LANE)) for j in range(-(-width // LANE))]


def dot(a, b):
    return jnp.dot(a, b, preferred_element_type=F32)


def dot_nt(a, b):
    return lax.dot_general(a, b, (((1,), (1,)), ((), ())), preferred_element_type=F32)


def block_kernel(w_ref, out_ref, mate_ref):
    here = lax.axis_index("neur")
    blocks, width, _ = out_ref.shape
    real = w_ref.shape[0] // blocks
    out_ref[...] = jnp.zeros(out_ref.shape, BF16)
    for b in range(blocks):
        out_ref[b, :real, : w_ref.shape[1]] = w_ref[b * real : (b + 1) * real, :]
    for i, k in enumerate((1, 3)):
        mate_ref[i] = out_ref[here ^ k]


def means_of(x_ref):
    length = x_ref.shape[0]
    return dot(jnp.ones((16, length), BF16), x_ref[...])[:1] * (1.0 / length)


def project_early(own_ref, mate_ref, w_ref, part_ref, means_ref):
    here = lax.axis_index("neur")
    k = own_ref.shape[1]
    means_ref[...] = jnp.zeros(means_ref.shape, F32)
    means_ref[0:1, :k] = means_of(own_ref)
    means_ref[1:2, :k] = means_of(mate_ref)
    for c in range(0, part_ref.shape[1], 256):
        part_ref[:, c : c + 256] = dot(own_ref[...], w_ref[here, :k, c : c + 256]) + dot(
            mate_ref[...], w_ref[here ^ 1, :k, c : c + 256]
        )


def project_late(part_ref, means_ref, far_ref, cross_ref, w_ref, proj_ref, stats_ref):
    here = lax.axis_index("neur")
    k = far_ref.shape[1]
    peers, _, width = stats_ref.shape
    far, cross = means_of(far_ref), means_of(cross_ref)
    for p in range(peers):
        stats_ref[p, 2:4, :] = means_ref[0:2, :]
        stats_ref[p, 4:8, :] = jnp.zeros((4, width), F32)
        stats_ref[p, 4:5, :k] = far
        stats_ref[p, 5:6, :k] = cross
    length = proj_ref.shape[0]
    for c in range(0, part_ref.shape[1], 256):
        y = (
            part_ref[:, c : c + 256]
            + dot(far_ref[...], w_ref[here ^ 2, :k, c : c + 256])
            + dot(cross_ref[...], w_ref[here ^ 3, :k, c : c + 256])
        )
        proj_ref[:, c : c + 256] = y
        mean = jnp.sum(y, axis=0, keepdims=True) * (1.0 / length)
        off = y - mean
        spread = jnp.sum(off * off, axis=0, keepdims=True)
        for p in range(stats_ref.shape[0]):
            stats_ref[p, 0:1, c : c + 256] = mean
            stats_ref[p, 1:2, c : c + 256] = spread


def merged(stats_ref, length, sum_ref):
    peers = stats_ref.shape[0]
    means = [stats_ref[p, 0:1, :] for p in range(peers)]
    mean = sum(means[1:], means[0]) * (1.0 / peers)
    total = None
    for p in range(peers):
        off = means[p] - mean
        term = stats_ref[p, 1:2, :] + off * off * float(length)
        total = term if total is None else total + term
    var = total * (1.0 / (peers * length))
    inverse = lax.rsqrt(var + EPSILON)
    features = stats_ref[0, 2:6, :]
    for p in range(1, peers):
        features = features + stats_ref[p, 2:6, :]
    sum_ref[0:1, :] = mean
    sum_ref[1:2, :] = var
    sum_ref[2:3, :] = inverse
    sum_ref[3:4, :] = jnp.zeros_like(mean)
    sum_ref[4:8, :] = features * (1.0 / peers)
    return mean, var, inverse


def spread_rows(row, tiles):
    return [jnp.broadcast_to(row[:, c : c + LANE], (8, LANE)) for _, c, _ in tiles]


def load_step(ref, step, tiles, lead=0):
    steps = (ref.shape[1] - lead) // CHUNKS
    return [
        ref[j, pl.ds(lead + step + g * 8 * steps, 8, stride=steps), :]
        for j, _, _ in tiles
        for g in range(GROUPS)
    ]


def store_step(ref, step, tiles, values, lead=0):
    steps = (ref.shape[1] - lead) // CHUNKS
    i = 0
    for j, _, _ in tiles:
        for g in range(GROUPS):
            ref[j, pl.ds(lead + step + g * 8 * steps, 8, stride=steps), :] = values[i]
            i += 1


def load_edges(ref, tiles):
    return [ref[g * 8 : g * 8 + 8, c : c + LANE] for _, c, _ in tiles for g in range(GROUPS)]


def store_edges(ref, tiles, values):
    i = 0
    for _, c, _ in tiles:
        for g in range(GROUPS):
            ref[g * 8 : g * 8 + 8, c : c + LANE] = values[i]
            i += 1


def power(x, n):
    out = None
    while n:
        if n & 1:
            out = x if out is None else out * x
        x = x * x
        n >>= 1
    return out


def run_chunks(drive_ref, state_ref, start, decay, tiles, steps, store):
    u2 = [d * LOG2E for d in decay for _ in range(GROUPS)]

    def body(step, carry):
        state, slope = carry
        drive = load_step(drive_ref, step, tiles)
        before = [d + u * s for d, u, s in zip(drive, u2, state)]
        soft = [jnp.log(1.0 + jnp.exp2(b)) for b in before]
        state = [jnp.where(b > 25.0, b * LN2, s) for b, s in zip(before, soft)]
        slope = [a + (b - s * LOG2E) for a, b, s in zip(slope, before, state)]
        if store:
            store_step(state_ref, step, tiles, state, lead=8)
        return state, slope

    zero = [jnp.zeros((8, LANE), F32) for _ in start]
    state, slope = lax.fori_loop(0, steps, body, (start, zero))
    top = [power(d, steps) for d in decay for _ in range(GROUPS)]
    return state, [t * jnp.exp2(a) for t, a in zip(top, slope)]


def run_line(drive_ref, decay, tiles, steps):
    u = [d for d in decay for _ in range(GROUPS)]

    def body(step, line):
        return [d + a * s for d, a, s in zip(load_step(drive_ref, step, tiles), u, line)]

    line = lax.fori_loop(0, steps, body, [jnp.zeros((8, LANE), F32) for _ in u])
    return [a * LN2 for a in line]


def solve(drive_ref, state_ref, decay_row, tiles, edges):
    from_zero, zero_slope, line_end, start_ref, end_ref, slope_ref = edges
    steps = drive_ref.shape[1] // CHUNKS
    decay = spread_rows(decay_row, tiles)
    width = start_ref.shape[1]
    top = power(decay_row, steps)

    end, slope = run_chunks(drive_ref, state_ref, [jnp.zeros((8, LANE), F32)] * (len(tiles) * GROUPS), decay, tiles, steps, False)
    store_edges(from_zero, tiles, end)
    store_edges(zero_slope, tiles, slope)
    store_edges(line_end, tiles, run_line(drive_ref, decay, tiles, steps))

    def sweep(newton):
        first = jnp.zeros((1, width), F32)
        old = first
        start_ref[0:1, :] = first
        worst = None
        for c in range(CHUNKS - 1):
            at = pl.ds(c, 1)
            value = jnp.maximum(
                from_zero[at, :] + zero_slope[at, :] * first, line_end[at, :] + top * first
            )
            if newton:
                reached = end_ref[at, :]
                value = jnp.maximum(value, reached + slope_ref[at, :] * (first - old))
                old = start_ref[c + 1 : c + 2, :]
                miss = jnp.abs(reached - old) - TOLERANCE * jnp.maximum(old, 1.0)
                worst = miss if worst is None else jnp.maximum(worst, miss)
            start_ref[c + 1 : c + 2, :] = value
            first = value
        return worst

    sweep(False)

    def again(carry):
        count, worst = carry
        return jnp.logical_and(worst > 0.0, count < CHUNKS + 1)

    def newton(carry):
        count, _ = carry
        end, slope = run_chunks(
            drive_ref, state_ref, load_edges(start_ref, tiles), decay, tiles, steps, True
        )
        store_edges(end_ref, tiles, end)
        store_edges(slope_ref, tiles, slope)
        return count + 1, jnp.max(sweep(True))

    lax.while_loop(again, newton, (jnp.int32(0), jnp.float32(1.0)))


def run_back(grad_ref, sigma_ref, start, decay, tiles, steps, store):
    u = [d for d in decay for _ in range(GROUPS)]

    def body(i, carry):
        z, prod = carry
        step = steps - 1 - i
        gs = load_step(grad_ref, step, tiles)
        sig = load_step(sigma_ref, step, tiles)
        z = [s * (g + a * v) for s, g, a, v in zip(sig, gs, u, z)]
        if store:
            store_step(grad_ref, step, tiles, z)
            return z, prod
        return z, [p * (s * a) for p, s, a in zip(prod, sig, u)]

    ones = [] if store else [jnp.ones((8, LANE), F32) for _ in start]
    return lax.fori_loop(0, steps, body, (start, ones))


def solve_back(grad_ref, sigma_ref, decay_row, tiles, edges):
    _, _, _, start_ref, end_ref, slope_ref = edges
    steps = grad_ref.shape[1] // CHUNKS
    decay = spread_rows(decay_row, tiles)
    zero = [jnp.zeros((8, LANE), F32)] * (len(tiles) * GROUPS)
    end, slope = run_back(grad_ref, sigma_ref, zero, decay, tiles, steps, False)
    store_edges(end_ref, tiles, end)
    store_edges(slope_ref, tiles, slope)
    value = jnp.zeros((1, start_ref.shape[1]), F32)
    for c in range(CHUNKS - 1, -1, -1):
        start_ref[c : c + 1, :] = value
        value = end_ref[c : c + 1, :] + slope_ref[c : c + 1, :] * value
    run_back(grad_ref, sigma_ref, load_edges(start_ref, tiles), decay, tiles, steps, True)


BLOCK = 88


def row_blocks(length, body):
    @pl.loop(0, length // BLOCK)
    def _(i):
        body(pl.ds(pl.multiple_of(i * BLOCK, 8), BLOCK))


def fill_drive(proj_ref, drive_ref, mean, inverse, gain, shift, tiles):
    scale = inverse * gain * LOG2E
    offset = shift * LOG2E

    def body(rows):
        for j, c, _ in tiles:
            at = slice(c, c + LANE)
            drive_ref[j, rows, :] = (proj_ref[rows, at] - mean[:, at]) * scale[:, at] + offset[:, at]

    row_blocks(proj_ref.shape[0], body)


def fill_sigma(drive_ref, prev_ref, decay_row, tiles, length):
    u2 = decay_row * LOG2E

    def body(i, _):
        for j, c, _w in tiles:
            rows = pl.ds(pl.multiple_of(i * BLOCK, 8), BLOCK)
            before = drive_ref[j, rows, :] + u2[:, c : c + LANE] * prev_ref[j, pl.ds(i * BLOCK + 7, BLOCK), :]
            drive_ref[j, rows, :] = 1.0 / (1.0 + jnp.exp2(-before))
        return 0

    lax.fori_loop(0, length // BLOCK, body, 0)


def finish_back(grad_ref, state_ref, proj_ref, mean, inverse, tiles, gb_ref, sums_ref):
    length, width = proj_ref.shape
    zero = tuple(jnp.zeros((1, LANE), F32) for _ in tiles)

    def body(i, carry):
        shift, gain, decay = (list(x) for x in carry)
        rows = pl.ds(pl.multiple_of(i * BLOCK, 8), BLOCK)
        for j, c, _w in tiles:
            at = slice(c, c + LANE)
            gb = grad_ref[j, rows, :]
            gb_ref[rows, at] = gb
            shift[j] = shift[j] + jnp.sum(gb, axis=0, keepdims=True)
            gain[j] = gain[j] + jnp.sum(gb * (proj_ref[rows, at] - mean[:, at]), axis=0, keepdims=True)
            decay[j] = decay[j] + jnp.sum(
                gb * state_ref[j, pl.ds(i * BLOCK + 7, BLOCK), :], axis=0, keepdims=True
            )
        return tuple(shift), tuple(gain), tuple(decay)

    shift, gain, decay = lax.fori_loop(0, length // BLOCK, body, (zero, zero, zero))
    for j, c, _ in tiles:
        at = slice(c, c + LANE)
        scaled = gain[j] * inverse[:, at]
        for p in range(sums_ref.shape[0]):
            sums_ref[p, 0:1, at] = shift[j]
            sums_ref[p, 1:2, at] = scaled
            sums_ref[p, 2:3, at] = decay[j]


def clear(state_ref, tiles):
    for j, _, _ in tiles:
        state_ref[j, 0:8, :] = jnp.zeros((8, LANE), F32)


def put_states(state_ref, out_ref, tiles, wide_ref=None):
    def body(i, _):
        rows = pl.ds(pl.multiple_of(i * 16, 16), 16)
        for j, c, w in tiles:
            s = state_ref[j, pl.ds(pl.multiple_of(8 + i * 16, 8), 16), :]
            out_ref[rows, c : c + w] = s[:, :w].astype(BF16)
            if wide_ref is not None:
                wide_ref[rows, c : c + LANE] = s
        return 0

    lax.fori_loop(0, out_ref.shape[0] // 16, body, 0)


def forward_kernel(stats_ref, proj_ref, par_ref, out_ref, wide_ref, sum_ref, drive, state, *edges):
    length, width = proj_ref.shape
    tiles = tiles_of(width)
    outs = tiles_of(out_ref.shape[1])
    mean, var, inverse = merged(stats_ref, length, sum_ref)
    gain, shift, decay = par_ref[0:1, :], par_ref[1:2, :], par_ref[2:3, :]
    fill_drive(proj_ref, drive, mean, inverse, gain, shift, tiles)
    clear(state, tiles)
    solve(drive, state, decay, tiles, edges)
    put_states(state, out_ref, outs, wide_ref)


def turn_kernel(
    stats_ref,
    proj_ref,
    par_ref,
    cot_ref,
    first_ref,
    rmean_ref,
    rvar_ref,
    out_ref,
    gb_ref,
    sums_ref,
    sum_ref,
    nmean_ref,
    nvar_ref,
    drive,
    state,
    grad,
    *edges,
):
    length, width = proj_ref.shape
    tiles = tiles_of(width)
    outs = tiles_of(out_ref.shape[1])
    mean, var, inverse = merged(stats_ref, length, sum_ref)
    gain, shift, decay = par_ref[0:1, :], par_ref[1:2, :], par_ref[2:3, :]
    real = out_ref.shape[1]
    count = float(stats_ref.shape[0] * length)
    for row, m, v in ((0, first_ref[0:1, :], first_ref[1:2, :]), (1, mean, var)):
        nmean_ref[row : row + 1, :] = (1.0 - MOMENTUM) * rmean_ref[row : row + 1, :] + MOMENTUM * m[:, :real]
        nvar_ref[row : row + 1, :] = (1.0 - MOMENTUM) * rvar_ref[row : row + 1, :] + (
            MOMENTUM * v[:, :real]
        ) * (count / (count - 1.0))
    fill_drive(proj_ref, drive, mean, inverse, gain, shift, tiles)
    clear(state, tiles)
    solve(drive, state, decay, tiles, edges)
    put_states(state, out_ref, outs)
    fill_sigma(drive, state, decay, tiles, length)
    for j, _, w in outs:
        if w < LANE:
            grad[j] = jnp.zeros(grad.shape[1:], F32)

    def load_cot(i, _):
        rows = pl.ds(pl.multiple_of(i * 16, 16), 16)
        for j, c, w in outs:
            grad[j, rows, :w] = cot_ref[rows, c : c + w].astype(F32)
        return 0

    lax.fori_loop(0, length // 16, load_cot, 0)
    solve_back(grad, drive, decay, tiles, edges)
    finish_back(grad, state, proj_ref, mean, inverse, tiles, gb_ref, sums_ref)


def back_kernel(
    keep_ref, got_ref, proj_ref, wide_ref, sum_ref, par_ref, gb_ref, sums_ref, drive, state, grad, *edges
):
    length, width = proj_ref.shape
    tiles = tiles_of(width)
    mean, inverse = sum_ref[0:1, :], sum_ref[2:3, :]
    gain, shift, decay = par_ref[0:1, :], par_ref[1:2, :], par_ref[2:3, :]
    fill_drive(proj_ref, drive, mean, inverse, gain, shift, tiles)
    clear(state, tiles)

    def load(i, _):
        rows = pl.ds(pl.multiple_of(i * 16, 16), 16)
        for j, c, _w in tiles:
            at = slice(c, c + LANE)
            grad[j, rows, :] = keep_ref[rows, at] + got_ref[rows, at].astype(F32)
            state[j, pl.ds(pl.multiple_of(8 + i * 16, 8), 16), :] = wide_ref[rows, at]
        return 0

    lax.fori_loop(0, length // 16, load, 0)
    fill_sigma(drive, state, decay, tiles, length)
    solve_back(grad, drive, decay, tiles, edges)
    finish_back(grad, state, proj_ref, mean, inverse, tiles, gb_ref, sums_ref)


def total_of(sums_ref):
    peers = sums_ref.shape[0]
    out = sums_ref[0]
    for p in range(1, peers):
        out = out + sums_ref[p]
    return out


def grad_kernel(sums_ref, gb_ref, proj_ref, sum_ref, par_ref, g_ref, total_ref):
    length, _ = proj_ref.shape
    total = total_of(sums_ref)
    total_ref[...] = total
    count = float(sums_ref.shape[0] * length)
    mean, inverse = sum_ref[0:1, :], sum_ref[2:3, :]
    scale = par_ref[0:1, :] * inverse
    base = total[0:1, :] * (1.0 / count)
    lean = total[1:2, :] * (1.0 / count) * inverse

    def body(i, summed):
        rows = pl.ds(pl.multiple_of(i * 16, 16), 16)
        g = scale * (gb_ref[rows, :] - base - (proj_ref[rows, :] - mean) * lean)
        g_ref[rows, :] = g.astype(BF16)
        return summed + (g[:8] + g[8:])

    summed = lax.fori_loop(0, length // 16, body, jnp.zeros((8, g_ref.shape[1]), F32))
    total_ref[7:8, :] = jnp.sum(summed, axis=0, keepdims=True)


def send_kernel(g_ref, mate_ref, w_ref, wmate_ref, out_ref):
    here = lax.axis_index("neur")
    for c in range(0, out_ref.shape[1], 256):
        at = slice(c, c + 256)
        out_ref[:, at] = (
            dot_nt(g_ref[...], w_ref[here ^ 2, at, :]) + dot_nt(mate_ref[...], wmate_ref[1, at, :])
        ).astype(BF16)


def keep_kernel(g_ref, mate_ref, w_ref, wmate_ref, out_ref):
    here = lax.axis_index("neur")
    for c in range(0, out_ref.shape[1], 256):
        at = slice(c, c + 256)
        out_ref[:, at] = dot_nt(g_ref[...], w_ref[here, at, :]) + dot_nt(
            mate_ref[...], wmate_ref[0, at, :]
        )


def outer(a, b):
    return lax.dot_general(
        a, b, (((0,), (0,)), ((), ())), precision=lax.Precision.HIGHEST, preferred_element_type=F32
    )


def weight_kernel(own_ref, mate_ref, far_ref, cross_ref, g_ref, sum_ref, total_ref, *refs):
    outs, hold = refs[:-1], refs[-1]
    place = lax.axis_index("seq") & 7
    half, width = outs[0].shape
    alone = lax.broadcasted_iota(jnp.int32, (8, width), 0) == 0
    summed = jnp.where(alone, total_ref[7:8, :], 0.0)
    for k, x_ref in enumerate((own_ref, mate_ref, far_ref, cross_ref)):
        real = x_ref.shape[1]
        mean = jnp.where(alone, sum_ref[4 + k : 5 + k, :], 0.0)[:, :real]
        part = lax.dot_general(
            x_ref[...], g_ref[...], (((0,), (0,)), ((), ())), preferred_element_type=F32
        )
        part = (part - outer(mean, summed)).astype(BF16)
        hold[(2 * k) ^ place] = part[:half]
        rest = part[half:]
        hold[(2 * k + 1) ^ place, : rest.shape[0], :] = rest
    for r, out in enumerate(outs):
        out[...] = hold[r]


def spread_kernel(*refs):
    shares, out_ref, hold = refs[:-2], refs[-2], refs[-1]
    place, here = lax.axis_index("seq") & 7, lax.axis_index("neur")
    for r, share in enumerate(shares):
        hold[r] = share[...]
    half = shares[0].shape[0]
    block = out_ref.shape[0] // 4
    width = out_ref.shape[1]
    for b in range(4):
        for h in range(2):
            low, high = b * block + h * half, min(b * block + h * half + half, (b + 1) * block)
            which = (((here ^ b) * 2) + h) ^ place
            out_ref[low:high, :] = hold[which, : high - low, :width].astype(F32)


def half_sum(a, b):
    return (a.astype(F32) + b.astype(F32)).astype(BF16)


def swap(x, bit, axis="seq"):
    n = lax.axis_size(axis)
    return lax.ppermute(x, axis, [(i, i ^ bit) for i in range(n)])


def reduce_shares(shares):
    part = {(r >> 2 & 1, r >> 1 & 1, r & 1): v for r, v in enumerate(shares)}
    got = {q: swap(part[(1,) + q], 4) for q in ((1, 1), (1, 0), (0, 1), (0, 0))}
    mine = {q: half_sum(part[(0,) + q], v) for q, v in got.items()}
    first = half_sum(mine[(0, 1)], swap(mine[(1, 1)], 2))
    last = half_sum(mine[(0, 0)], swap(mine[(1, 0)], 2))
    return half_sum(last, swap(first, 1))


def gather_shares(v):
    out = {0: v}
    out[1] = swap(v, 1)
    out[2] = swap(v, 2)
    out[4] = swap(v, 4)
    out[3] = swap(out[1], 2)
    out[6] = swap(out[2], 4)
    out[5] = swap(out[1], 4)
    out[7] = swap(out[3], 4)
    return [out[r] for r in range(8)]


def per_device(devices_seq, *args):
    (
        tokens,
        w_first,
        gain_first,
        shift_first,
        decay_first,
        w_second,
        gain_second,
        shift_second,
        decay_second,
        cotangent,
        running_mean,
        running_var,
    ) = args
    _, length, real = tokens.shape
    width = -(-real // LANE) * LANE
    tiles = len(tiles_of(width))
    peers = devices_seq
    here = lax.axis_index("neur")
    tokens, cotangent = tokens[0], cotangent[0]

    def blocks(w):
        return call(
            block_kernel,
            [shape(4, width, width, dtype=BF16), shape(2, width, width, dtype=BF16)],
            nbytes=5 << 20,
        )(w)

    def params(*rows):
        return jnp.pad(jnp.stack(rows), ((0, 5), (0, width - real)))

    scans = [
        pltpu.VMEM((tiles, length, LANE), F32),
        pltpu.VMEM((tiles, length + 8, LANE), F32),
    ]
    grads = [pltpu.VMEM((tiles, length, LANE), F32)]
    edges = [pltpu.VMEM((CHUNKS, width), F32)] * 6
    big = 2 * length * real * real

    def share(stats):
        return lax.all_to_all(stats, "seq", 0, 0, tiled=True)

    def project(own, make):
        far = swap(own, 2, "neur")
        mate = swap(own, 1, "neur")
        w4, ready = make()
        part, means = call(
            project_early, [shape(length, width), shape(8, width)], flops=2 * big, nbytes=4 << 20
        )(own, mate, w4)
        far, part, ready = lax.optimization_barrier((far, part, ready))
        cross = swap(far, 1, "neur")
        proj, stats = call(
            project_late, [shape(length, width), shape(peers, 8, width)], flops=2 * big, nbytes=6 << 20
        )(part, means, far, cross, w4)
        return (own, mate, far, cross), proj, share(stats), ready

    def back(sums, gb, proj, summary, par, w4, wm):
        g, total = call(
            grad_kernel, [shape(length, width, dtype=BF16), shape(8, width)], nbytes=5 << 20
        )(share(sums), gb, proj, summary, par)
        mate = swap(g, 1, "neur")
        send = call(send_kernel, shape(length, width, dtype=BF16), flops=2 * big, nbytes=4 << 20)(
            g, mate, w4, wm
        )
        got = swap(send, 2, "neur")
        keep = call(keep_kernel, shape(length, width), flops=2 * big, nbytes=4 << 20)(g, mate, w4, wm)
        return g, total, keep, got

    def weights(x, g, summary, total):
        half = width // 2
        shares = call(
            weight_kernel,
            [shape(half, width, dtype=BF16)] * 8,
            [pltpu.VMEM((8, half, width), BF16)],
            flops=4 * big,
            nbytes=6 << 20,
        )(*x, g, summary, total)
        if peers == 8:
            shares = gather_shares(reduce_shares(shares))
        else:
            place = lax.axis_index("seq")
            order = jnp.stack([lax.dynamic_index_in_dim(jnp.stack(shares), (place & 7) ^ r, 0, False) for r in range(8)])
            whole = lax.psum(order, "seq")
            shares = [lax.dynamic_index_in_dim(whole, (place & 7) ^ r, 0, False) for r in range(8)]
        return call(
            spread_kernel,
            shape(4 * real, real),
            [pltpu.VMEM((8, half, width), BF16)],
            nbytes=6 << 20,
        )(*shares)

    def prepare():
        first, first_give = blocks(w_first)
        second, second_give = blocks(w_second)
        return first, (
            first,
            second,
            swap(first_give, 1, "neur"),
            swap(second_give, 1, "neur"),
            params(gain_first, shift_first, decay_first),
            params(gain_second, shift_second, decay_second),
        )

    first_x, first_proj, first_stats, ready = project(tokens, prepare)
    first_w, second_w, first_mate, second_mate, first_par, second_par = ready
    first_out, first_wide, first_sum = call(
        forward_kernel,
        [shape(length, real, dtype=BF16), shape(length, width), shape(8, width)],
        scans + edges,
        nbytes=8 << 20,
    )(first_stats, first_proj, first_par)

    second_x, second_proj, second_stats, _ = project(first_out, lambda: (second_w, ()))
    second_out, second_gb, second_sums, second_sum, new_mean, new_var = call(
        turn_kernel,
        [
            shape(length, real, dtype=BF16),
            shape(length, width),
            shape(peers, 8, width),
            shape(8, width),
            shape(2, real),
            shape(2, real),
        ],
        scans + grads + edges,
        nbytes=12 << 20,
    )(second_stats, second_proj, second_par, cotangent, first_sum, running_mean, running_var)

    second_g, second_total, keep, got = back(
        second_sums, second_gb, second_proj, second_sum, second_par, second_w, second_mate
    )
    grad_w_second = weights(second_x, second_g, second_sum, second_total)
    first_gb, first_sums = call(
        back_kernel,
        [shape(length, width), shape(peers, 8, width)],
        scans + grads + edges,
        nbytes=10 << 20,
    )(keep, got, first_proj, first_wide, first_sum, first_par)
    first_g, first_total, keep, got = back(
        first_sums, first_gb, first_proj, first_sum, first_par, first_w, first_mate
    )
    grad_w_first = weights(first_x, first_g, first_sum, first_total)
    input_grad = (keep + got.astype(F32))[:, :real]

    def pair(row):
        return jnp.stack([first_total[row, :real], second_total[row, :real]])

    return (
        first_out[None],
        second_out[None],
        input_grad[None],
        grad_w_first,
        grad_w_second,
        pair(1),
        pair(0),
        pair(2),
        new_mean,
        new_var,
    )


def solution(mesh):
    rows, line, flat = P("seq", None, "neur"), P("neur"), P(None, "neur")
    return jax.shard_map(
        functools.partial(per_device, mesh.shape["seq"]),
        mesh=mesh,
        in_specs=(rows, flat, line, line, line, flat, line, line, line, rows, flat, flat),
        out_specs=(rows, rows, rows) + (flat,) * 7,
        check_vma=False,
    )
```

```python
import functools
import math

import jax
import jax.numpy as jnp
from jax import lax
from jax.experimental import pallas as pl
from jax.experimental.pallas import tpu as pltpu
from jax.sharding import PartitionSpec as P

EPSILON = 1e-05
MOMENTUM = 0.1
LANE = 128
CHUNKS = 32
GROUPS = CHUNKS // 8
TOLERANCE = 1e-5
LOG2E = math.log2(math.e)
LN2 = math.log(2.0)
F32 = jnp.float32
BF16 = jnp.bfloat16
VMEM_BYTES = 50 * 1024 * 1024


def call(kernel, outs, scratch=(), flops=0, nbytes=0):
    return pl.pallas_call(
        kernel,
        out_shape=outs,
        scratch_shapes=list(scratch),
        compiler_params=pltpu.CompilerParams(vmem_limit_bytes=VMEM_BYTES),
        cost_estimate=pl.CostEstimate(flops=1, bytes_accessed=1, transcendentals=0),
    )


def shape(*dims, dtype=F32):
    return jax.ShapeDtypeStruct(dims, dtype)


def tiles_of(width):
    return [(j, j * LANE, min(LANE, width - j * LANE)) for j in range(-(-width // LANE))]


def dot(a, b):
    return jnp.dot(a, b, preferred_element_type=F32)


def dot_nt(a, b):
    return lax.dot_general(a, b, (((1,), (1,)), ((), ())), preferred_element_type=F32)


def block_kernel(w_ref, out_ref, mate_ref):
    here = lax.axis_index("neur")
    blocks, width, _ = out_ref.shape
    real = w_ref.shape[0] // blocks
    out_ref[...] = jnp.zeros(out_ref.shape, BF16)
    for b in range(blocks):
        out_ref[b, :real, : w_ref.shape[1]] = w_ref[b * real : (b + 1) * real, :]
    for i, k in enumerate((1, 3)):
        mate_ref[i] = out_ref[here ^ k]


def means_of(x_ref):
    length = x_ref.shape[0]
    return dot(jnp.ones((16, length), BF16), x_ref[...])[:1] * (1.0 / length)


def project_early(own_ref, mate_ref, w_ref, part_ref, means_ref):
    here = lax.axis_index("neur")
    k = own_ref.shape[1]
    means_ref[...] = jnp.zeros(means_ref.shape, F32)
    means_ref[0:1, :k] = means_of(own_ref)
    means_ref[1:2, :k] = means_of(mate_ref)
    for c in range(0, part_ref.shape[1], 256):
        part_ref[:, c : c + 256] = dot(own_ref[...], w_ref[here, :k, c : c + 256]) + dot(
            mate_ref[...], w_ref[here ^ 1, :k, c : c + 256]
        )


def project_late(part_ref, means_ref, far_ref, cross_ref, w_ref, proj_ref, stats_ref):
    here = lax.axis_index("neur")
    k = far_ref.shape[1]
    peers, _, width = stats_ref.shape
    far, cross = means_of(far_ref), means_of(cross_ref)
    for p in range(peers):
        stats_ref[p, 2:4, :] = means_ref[0:2, :]
        stats_ref[p, 4:8, :] = jnp.zeros((4, width), F32)
        stats_ref[p, 4:5, :k] = far
        stats_ref[p, 5:6, :k] = cross
    length = proj_ref.shape[0]
    for c in range(0, part_ref.shape[1], 256):
        y = (
            part_ref[:, c : c + 256]
            + dot(far_ref[...], w_ref[here ^ 2, :k, c : c + 256])
            + dot(cross_ref[...], w_ref[here ^ 3, :k, c : c + 256])
        )
        proj_ref[:, c : c + 256] = y
        mean = jnp.sum(y, axis=0, keepdims=True) * (1.0 / length)
        off = y - mean
        spread = jnp.sum(off * off, axis=0, keepdims=True)
        for p in range(stats_ref.shape[0]):
            stats_ref[p, 0:1, c : c + 256] = mean
            stats_ref[p, 1:2, c : c + 256] = spread


def merged(stats_ref, length, sum_ref):
    peers = stats_ref.shape[0]
    means = [stats_ref[p, 0:1, :] for p in range(peers)]
    mean = sum(means[1:], means[0]) * (1.0 / peers)
    total = None
    for p in range(peers):
        off = means[p] - mean
        term = stats_ref[p, 1:2, :] + off * off * float(length)
        total = term if total is None else total + term
    var = total * (1.0 / (peers * length))
    inverse = lax.rsqrt(var + EPSILON)
    features = stats_ref[0, 2:6, :]
    for p in range(1, peers):
        features = features + stats_ref[p, 2:6, :]
    sum_ref[0:1, :] = mean
    sum_ref[1:2, :] = var
    sum_ref[2:3, :] = inverse
    sum_ref[3:4, :] = jnp.zeros_like(mean)
    sum_ref[4:8, :] = features * (1.0 / peers)
    return mean, var, inverse


def spread_rows(row, tiles):
    return [jnp.broadcast_to(row[:, c : c + LANE], (8, LANE)) for _, c, _ in tiles]


def load_step(ref, step, tiles, lead=0):
    steps = (ref.shape[1] - lead) // CHUNKS
    return [
        ref[j, pl.ds(lead + step + g * 8 * steps, 8, stride=steps), :]
        for j, _, _ in tiles
        for g in range(GROUPS)
    ]


def store_step(ref, step, tiles, values, lead=0):
    steps = (ref.shape[1] - lead) // CHUNKS
    i = 0
    for j, _, _ in tiles:
        for g in range(GROUPS):
            ref[j, pl.ds(lead + step + g * 8 * steps, 8, stride=steps), :] = values[i]
            i += 1


def load_edges(ref, tiles):
    return [ref[g * 8 : g * 8 + 8, c : c + LANE] for _, c, _ in tiles for g in range(GROUPS)]


def store_edges(ref, tiles, values):
    i = 0
    for _, c, _ in tiles:
        for g in range(GROUPS):
            ref[g * 8 : g * 8 + 8, c : c + LANE] = values[i]
            i += 1


def power(x, n):
    out = None
    while n:
        if n & 1:
            out = x if out is None else out * x
        x = x * x
        n >>= 1
    return out


def run_chunks(drive_ref, state_ref, start, decay, tiles, steps, store):
    u2 = [d * LOG2E for d in decay for _ in range(GROUPS)]

    def body(step, carry):
        state, slope = carry
        drive = load_step(drive_ref, step, tiles)
        before = [d + u * s for d, u, s in zip(drive, u2, state)]
        soft = [jnp.log(1.0 + jnp.exp2(b)) for b in before]
        state = [jnp.where(b > 25.0, b * LN2, s) for b, s in zip(before, soft)]
        slope = [a + (b - s * LOG2E) for a, b, s in zip(slope, before, state)]
        if store:
            store_step(state_ref, step, tiles, state, lead=8)
        return state, slope

    zero = [jnp.zeros((8, LANE), F32) for _ in start]
    state, slope = lax.fori_loop(0, steps, body, (start, zero))
    top = [power(d, steps) for d in decay for _ in range(GROUPS)]
    return state, [t * jnp.exp2(a) for t, a in zip(top, slope)]


def run_line(drive_ref, decay, tiles, steps):
    u = [d for d in decay for _ in range(GROUPS)]

    def body(step, line):
        return [d + a * s for d, a, s in zip(load_step(drive_ref, step, tiles), u, line)]

    line = lax.fori_loop(0, steps, body, [jnp.zeros((8, LANE), F32) for _ in u])
    return [a * LN2 for a in line]


def solve(drive_ref, state_ref, decay_row, tiles, edges):
    from_zero, zero_slope, line_end, start_ref, end_ref, slope_ref = edges
    steps = drive_ref.shape[1] // CHUNKS
    decay = spread_rows(decay_row, tiles)
    width = start_ref.shape[1]
    top = power(decay_row, steps)

    end, slope = run_chunks(drive_ref, state_ref, [jnp.zeros((8, LANE), F32)] * (len(tiles) * GROUPS), decay, tiles, steps, False)
    store_edges(from_zero, tiles, end)
    store_edges(zero_slope, tiles, slope)
    store_edges(line_end, tiles, run_line(drive_ref, decay, tiles, steps))

    def sweep(newton):
        first = jnp.zeros((1, width), F32)
        old = first
        start_ref[0:1, :] = first
        worst = None
        for c in range(CHUNKS - 1):
            at = pl.ds(c, 1)
            value = jnp.maximum(
                from_zero[at, :] + zero_slope[at, :] * first, line_end[at, :] + top * first
            )
            if newton:
                reached = end_ref[at, :]
                value = jnp.maximum(value, reached + slope_ref[at, :] * (first - old))
                old = start_ref[c + 1 : c + 2, :]
                miss = jnp.abs(reached - old) - TOLERANCE * jnp.maximum(old, 1.0)
                worst = miss if worst is None else jnp.maximum(worst, miss)
            start_ref[c + 1 : c + 2, :] = value
            first = value
        return worst

    sweep(False)

    def again(carry):
        count, worst = carry
        return jnp.logical_and(worst > 0.0, count < CHUNKS + 1)

    def newton(carry):
        count, _ = carry
        end, slope = run_chunks(
            drive_ref, state_ref, load_edges(start_ref, tiles), decay, tiles, steps, True
        )
        store_edges(end_ref, tiles, end)
        store_edges(slope_ref, tiles, slope)
        return count + 1, jnp.max(sweep(True))

    lax.while_loop(again, newton, (jnp.int32(0), jnp.float32(1.0)))


def run_back(grad_ref, sigma_ref, start, decay, tiles, steps, store):
    u = [d for d in decay for _ in range(GROUPS)]

    def body(i, carry):
        z, prod = carry
        step = steps - 1 - i
        gs = load_step(grad_ref, step, tiles)
        sig = load_step(sigma_ref, step, tiles)
        z = [s * (g + a * v) for s, g, a, v in zip(sig, gs, u, z)]
        if store:
            store_step(grad_ref, step, tiles, z)
            return z, prod
        return z, [p * (s * a) for p, s, a in zip(prod, sig, u)]

    ones = [] if store else [jnp.ones((8, LANE), F32) for _ in start]
    return lax.fori_loop(0, steps, body, (start, ones))


def solve_back(grad_ref, sigma_ref, decay_row, tiles, edges):
    _, _, _, start_ref, end_ref, slope_ref = edges
    steps = grad_ref.shape[1] // CHUNKS
    decay = spread_rows(decay_row, tiles)
    zero = [jnp.zeros((8, LANE), F32)] * (len(tiles) * GROUPS)
    end, slope = run_back(grad_ref, sigma_ref, zero, decay, tiles, steps, False)
    store_edges(end_ref, tiles, end)
    store_edges(slope_ref, tiles, slope)
    value = jnp.zeros((1, start_ref.shape[1]), F32)
    for c in range(CHUNKS - 1, -1, -1):
        start_ref[c : c + 1, :] = value
        value = end_ref[c : c + 1, :] + slope_ref[c : c + 1, :] * value
    run_back(grad_ref, sigma_ref, load_edges(start_ref, tiles), decay, tiles, steps, True)


BLOCK = 88


def row_blocks(length, body):
    @pl.loop(0, length // BLOCK)
    def _(i):
        body(pl.ds(pl.multiple_of(i * BLOCK, 8), BLOCK))


def fill_drive(proj_ref, drive_ref, mean, inverse, gain, shift, tiles):
    scale = inverse * gain * LOG2E
    offset = shift * LOG2E

    def body(rows):
        for j, c, _ in tiles:
            at = slice(c, c + LANE)
            drive_ref[j, rows, :] = (proj_ref[rows, at] - mean[:, at]) * scale[:, at] + offset[:, at]

    row_blocks(proj_ref.shape[0], body)


def fill_sigma(drive_ref, prev_ref, decay_row, tiles, length):
    u2 = decay_row * LOG2E

    def body(i, _):
        for j, c, _w in tiles:
            rows = pl.ds(pl.multiple_of(i * BLOCK, 8), BLOCK)
            before = drive_ref[j, rows, :] + u2[:, c : c + LANE] * prev_ref[j, pl.ds(i * BLOCK + 7, BLOCK), :]
            drive_ref[j, rows, :] = 1.0 / (1.0 + jnp.exp2(-before))
        return 0

    lax.fori_loop(0, length // BLOCK, body, 0)


def finish_back(grad_ref, state_ref, proj_ref, mean, inverse, tiles, gb_ref, sums_ref):
    length, width = proj_ref.shape
    zero = tuple(jnp.zeros((1, LANE), F32) for _ in tiles)

    def body(i, carry):
        shift, gain, decay = (list(x) for x in carry)
        rows = pl.ds(pl.multiple_of(i * BLOCK, 8), BLOCK)
        for j, c, _w in tiles:
            at = slice(c, c + LANE)
            gb = grad_ref[j, rows, :]
            gb_ref[rows, at] = gb
            shift[j] = shift[j] + jnp.sum(gb, axis=0, keepdims=True)
            gain[j] = gain[j] + jnp.sum(gb * (proj_ref[rows, at] - mean[:, at]), axis=0, keepdims=True)
            decay[j] = decay[j] + jnp.sum(
                gb * state_ref[j, pl.ds(i * BLOCK + 7, BLOCK), :], axis=0, keepdims=True
            )
        return tuple(shift), tuple(gain), tuple(decay)

    shift, gain, decay = lax.fori_loop(0, length // BLOCK, body, (zero, zero, zero))
    for j, c, _ in tiles:
        at = slice(c, c + LANE)
        scaled = gain[j] * inverse[:, at]
        for p in range(sums_ref.shape[0]):
            sums_ref[p, 0:1, at] = shift[j]
            sums_ref[p, 1:2, at] = scaled
            sums_ref[p, 2:3, at] = decay[j]


def clear(state_ref, tiles):
    for j, _, _ in tiles:
        state_ref[j, 0:8, :] = jnp.zeros((8, LANE), F32)


def put_states(state_ref, out_ref, tiles, wide_ref=None):
    def body(i, _):
        rows = pl.ds(pl.multiple_of(i * 16, 16), 16)
        for j, c, w in tiles:
            s = state_ref[j, pl.ds(pl.multiple_of(8 + i * 16, 8), 16), :]
            out_ref[rows, c : c + w] = s[:, :w].astype(BF16)
            if wide_ref is not None:
                wide_ref[rows, c : c + LANE] = s
        return 0

    lax.fori_loop(0, out_ref.shape[0] // 16, body, 0)


def forward_kernel(stats_ref, proj_ref, par_ref, out_ref, wide_ref, sum_ref, drive, state, *edges):
    length, width = proj_ref.shape
    tiles = tiles_of(width)
    outs = tiles_of(out_ref.shape[1])
    mean, var, inverse = merged(stats_ref, length, sum_ref)
    gain, shift, decay = par_ref[0:1, :], par_ref[1:2, :], par_ref[2:3, :]
    fill_drive(proj_ref, drive, mean, inverse, gain, shift, tiles)
    clear(state, tiles)
    solve(drive, state, decay, tiles, edges)
    put_states(state, out_ref, outs, wide_ref)


def turn_kernel(
    stats_ref,
    proj_ref,
    par_ref,
    cot_ref,
    first_ref,
    rmean_ref,
    rvar_ref,
    out_ref,
    gb_ref,
    sums_ref,
    sum_ref,
    nmean_ref,
    nvar_ref,
    drive,
    state,
    grad,
    *edges,
):
    length, width = proj_ref.shape
    tiles = tiles_of(width)
    outs = tiles_of(out_ref.shape[1])
    mean, var, inverse = merged(stats_ref, length, sum_ref)
    gain, shift, decay = par_ref[0:1, :], par_ref[1:2, :], par_ref[2:3, :]
    real = out_ref.shape[1]
    count = float(stats_ref.shape[0] * length)
    for row, m, v in ((0, first_ref[0:1, :], first_ref[1:2, :]), (1, mean, var)):
        nmean_ref[row : row + 1, :] = (1.0 - MOMENTUM) * rmean_ref[row : row + 1, :] + MOMENTUM * m[:, :real]
        nvar_ref[row : row + 1, :] = (1.0 - MOMENTUM) * rvar_ref[row : row + 1, :] + (
            MOMENTUM * v[:, :real]
        ) * (count / (count - 1.0))
    fill_drive(proj_ref, drive, mean, inverse, gain, shift, tiles)
    clear(state, tiles)
    solve(drive, state, decay, tiles, edges)
    put_states(state, out_ref, outs)
    fill_sigma(drive, state, decay, tiles, length)
    for j, _, w in outs:
        if w < LANE:
            grad[j] = jnp.zeros(grad.shape[1:], F32)

    def load_cot(i, _):
        rows = pl.ds(pl.multiple_of(i * 16, 16), 16)
        for j, c, w in outs:
            grad[j, rows, :w] = cot_ref[rows, c : c + w].astype(F32)
        return 0

    lax.fori_loop(0, length // 16, load_cot, 0)
    solve_back(grad, drive, decay, tiles, edges)
    finish_back(grad, state, proj_ref, mean, inverse, tiles, gb_ref, sums_ref)


def back_kernel(
    keep_ref, got_ref, proj_ref, wide_ref, sum_ref, par_ref, gb_ref, sums_ref, drive, state, grad, *edges
):
    length, width = proj_ref.shape
    tiles = tiles_of(width)
    mean, inverse = sum_ref[0:1, :], sum_ref[2:3, :]
    gain, shift, decay = par_ref[0:1, :], par_ref[1:2, :], par_ref[2:3, :]
    fill_drive(proj_ref, drive, mean, inverse, gain, shift, tiles)
    clear(state, tiles)

    def load(i, _):
        rows = pl.ds(pl.multiple_of(i * 16, 16), 16)
        for j, c, _w in tiles:
            at = slice(c, c + LANE)
            grad[j, rows, :] = keep_ref[rows, at] + got_ref[rows, at].astype(F32)
            state[j, pl.ds(pl.multiple_of(8 + i * 16, 8), 16), :] = wide_ref[rows, at]
        return 0

    lax.fori_loop(0, length // 16, load, 0)
    fill_sigma(drive, state, decay, tiles, length)
    solve_back(grad, drive, decay, tiles, edges)
    finish_back(grad, state, proj_ref, mean, inverse, tiles, gb_ref, sums_ref)


def total_of(sums_ref):
    peers = sums_ref.shape[0]
    out = sums_ref[0]
    for p in range(1, peers):
        out = out + sums_ref[p]
    return out


def grad_kernel(sums_ref, gb_ref, proj_ref, sum_ref, par_ref, g_ref, total_ref):
    length, _ = proj_ref.shape
    total = total_of(sums_ref)
    total_ref[...] = total
    count = float(sums_ref.shape[0] * length)
    mean, inverse = sum_ref[0:1, :], sum_ref[2:3, :]
    scale = par_ref[0:1, :] * inverse
    base = total[0:1, :] * (1.0 / count)
    lean = total[1:2, :] * (1.0 / count) * inverse

    def body(i, summed):
        rows = pl.ds(pl.multiple_of(i * 16, 16), 16)
        g = scale * (gb_ref[rows, :] - base - (proj_ref[rows, :] - mean) * lean)
        g_ref[rows, :] = g.astype(BF16)
        return summed + (g[:8] + g[8:])

    summed = lax.fori_loop(0, length // 16, body, jnp.zeros((8, g_ref.shape[1]), F32))
    total_ref[7:8, :] = jnp.sum(summed, axis=0, keepdims=True)


def send_kernel(g_ref, mate_ref, w_ref, wmate_ref, out_ref):
    here = lax.axis_index("neur")
    for c in range(0, out_ref.shape[1], 256):
        at = slice(c, c + 256)
        out_ref[:, at] = (
            dot_nt(g_ref[...], w_ref[here ^ 2, at, :]) + dot_nt(mate_ref[...], wmate_ref[1, at, :])
        ).astype(BF16)


def keep_kernel(g_ref, mate_ref, w_ref, wmate_ref, out_ref):
    here = lax.axis_index("neur")
    for c in range(0, out_ref.shape[1], 256):
        at = slice(c, c + 256)
        out_ref[:, at] = dot_nt(g_ref[...], w_ref[here, at, :]) + dot_nt(
            mate_ref[...], wmate_ref[0, at, :]
        )


def outer(a, b):
    return lax.dot_general(
        a, b, (((0,), (0,)), ((), ())), precision=lax.Precision.HIGHEST, preferred_element_type=F32
    )


def weight_kernel(own_ref, mate_ref, far_ref, cross_ref, g_ref, sum_ref, total_ref, *refs):
    outs, hold = refs[:-1], refs[-1]
    place = seat()
    half, width = outs[0].shape
    alone = lax.broadcasted_iota(jnp.int32, (8, width), 0) == 0
    summed = jnp.where(alone, total_ref[7:8, :], 0.0)
    for k, x_ref in enumerate((own_ref, mate_ref, far_ref, cross_ref)):
        real = x_ref.shape[1]
        mean = jnp.where(alone, sum_ref[4 + k : 5 + k, :], 0.0)[:, :real]
        part = lax.dot_general(
            x_ref[...], g_ref[...], (((0,), (0,)), ((), ())), preferred_element_type=F32
        )
        part = (part - outer(mean, summed)).astype(BF16)
        hold[(2 * k) ^ place] = part[:half]
        rest = part[half:]
        hold[(2 * k + 1) ^ place, : rest.shape[0], :] = rest
    for r, out in enumerate(outs):
        out[...] = hold[r]


def spread_kernel(*refs):
    shares, out_ref, hold = refs[:-2], refs[-2], refs[-1]
    place, here = seat(), lax.axis_index("neur")
    for r, share in enumerate(shares):
        hold[r] = share[...]
    half = shares[0].shape[0]
    block = out_ref.shape[0] // 4
    width = out_ref.shape[1]
    for b in range(4):
        for h in range(2):
            low, high = b * block + h * half, min(b * block + h * half + half, (b + 1) * block)
            which = (((here ^ b) * 2) + h) ^ place
            out_ref[low:high, :] = hold[which, : high - low, :width].astype(F32)


def half_sum(a, b):
    return (a.astype(F32) + b.astype(F32)).astype(BF16)


def swap(x, bit, axis="seq"):
    n = lax.axis_size(axis)
    return lax.ppermute(x, axis, [(i, i ^ bit) for i in range(n)])


LEVEL = {4: 1, 2: 2, 1: 4}


def seat():
    place = lax.axis_index("seq")
    return ((place & 1) << 2) | (place & 2) | ((place >> 2) & 1)


def reduce_shares(shares):
    part = {(r >> 2 & 1, r >> 1 & 1, r & 1): v for r, v in enumerate(shares)}
    got = {q: swap(part[(1,) + q], LEVEL[4]) for q in ((1, 1), (1, 0), (0, 1), (0, 0))}
    mine = {q: half_sum(part[(0,) + q], v) for q, v in got.items()}
    first = half_sum(mine[(0, 1)], swap(mine[(1, 1)], LEVEL[2]))
    last = half_sum(mine[(0, 0)], swap(mine[(1, 0)], LEVEL[2]))
    return half_sum(last, swap(first, LEVEL[1]))


def gather_shares(v):
    out = {0: v}
    out[1] = swap(v, LEVEL[1])
    out[2] = swap(v, LEVEL[2])
    out[4] = swap(v, LEVEL[4])
    out[3] = swap(out[1], LEVEL[2])
    out[6] = swap(out[2], LEVEL[4])
    out[5] = swap(out[1], LEVEL[4])
    out[7] = swap(out[3], LEVEL[4])
    return [out[r] for r in range(8)]


def per_device(devices_seq, *args):
    (
        tokens,
        w_first,
        gain_first,
        shift_first,
        decay_first,
        w_second,
        gain_second,
        shift_second,
        decay_second,
        cotangent,
        running_mean,
        running_var,
    ) = args
    _, length, real = tokens.shape
    width = -(-real // LANE) * LANE
    tiles = len(tiles_of(width))
    peers = devices_seq
    here = lax.axis_index("neur")
    tokens, cotangent = tokens[0], cotangent[0]

    def blocks(w):
        return call(
            block_kernel,
            [shape(4, width, width, dtype=BF16), shape(2, width, width, dtype=BF16)],
            nbytes=5 << 20,
        )(w)

    def params(*rows):
        return jnp.pad(jnp.stack(rows), ((0, 5), (0, width - real)))

    scans = [
        pltpu.VMEM((tiles, length, LANE), F32),
        pltpu.VMEM((tiles, length + 8, LANE), F32),
    ]
    grads = [pltpu.VMEM((tiles, length, LANE), F32)]
    edges = [pltpu.VMEM((CHUNKS, width), F32)] * 6
    big = 2 * length * real * real

    def share(stats):
        return lax.all_to_all(stats, "seq", 0, 0, tiled=True)

    def project(own, make):
        far = swap(own, 2, "neur")
        mate = swap(own, 1, "neur")
        w4, ready = make()
        part, means = call(
            project_early, [shape(length, width), shape(8, width)], flops=2 * big, nbytes=4 << 20
        )(own, mate, w4)
        far, part, ready = lax.optimization_barrier((far, part, ready))
        cross = swap(far, 1, "neur")
        proj, stats = call(
            project_late, [shape(length, width), shape(peers, 8, width)], flops=2 * big, nbytes=6 << 20
        )(part, means, far, cross, w4)
        return (own, mate, far, cross), proj, share(stats), ready

    def back(sums, gb, proj, summary, par, w4, wm):
        g, total = call(
            grad_kernel, [shape(length, width, dtype=BF16), shape(8, width)], nbytes=5 << 20
        )(share(sums), gb, proj, summary, par)
        mate = swap(g, 1, "neur")
        send = call(send_kernel, shape(length, width, dtype=BF16), flops=2 * big, nbytes=4 << 20)(
            g, mate, w4, wm
        )
        got = swap(send, 2, "neur")
        keep = call(keep_kernel, shape(length, width), flops=2 * big, nbytes=4 << 20)(g, mate, w4, wm)
        return g, total, keep, got

    def weights(x, g, summary, total):
        half = width // 2
        shares = call(
            weight_kernel,
            [shape(half, width, dtype=BF16)] * 8,
            [pltpu.VMEM((8, half, width), BF16)],
            flops=4 * big,
            nbytes=6 << 20,
        )(*x, g, summary, total)
        if peers == 8:
            shares = gather_shares(reduce_shares(shares))
        else:
            place = lax.axis_index("seq")
            order = jnp.stack([lax.dynamic_index_in_dim(jnp.stack(shares), (place & 7) ^ r, 0, False) for r in range(8)])
            whole = lax.psum(order, "seq")
            shares = [lax.dynamic_index_in_dim(whole, (place & 7) ^ r, 0, False) for r in range(8)]
        return call(
            spread_kernel,
            shape(4 * real, real),
            [pltpu.VMEM((8, half, width), BF16)],
            nbytes=6 << 20,
        )(*shares)

    def prepare():
        first, first_give = blocks(w_first)
        second, second_give = blocks(w_second)
        return first, (
            first,
            second,
            swap(first_give, 1, "neur"),
            swap(second_give, 1, "neur"),
            params(gain_first, shift_first, decay_first),
            params(gain_second, shift_second, decay_second),
        )

    first_x, first_proj, first_stats, ready = project(tokens, prepare)
    first_w, second_w, first_mate, second_mate, first_par, second_par = ready
    first_out, first_wide, first_sum = call(
        forward_kernel,
        [shape(length, real, dtype=BF16), shape(length, width), shape(8, width)],
        scans + edges,
        nbytes=8 << 20,
    )(first_stats, first_proj, first_par)

    second_x, second_proj, second_stats, _ = project(first_out, lambda: (second_w, ()))
    second_out, second_gb, second_sums, second_sum, new_mean, new_var = call(
        turn_kernel,
        [
            shape(length, real, dtype=BF16),
            shape(length, width),
            shape(peers, 8, width),
            shape(8, width),
            shape(2, real),
            shape(2, real),
        ],
        scans + grads + edges,
        nbytes=12 << 20,
    )(second_stats, second_proj, second_par, cotangent, first_sum, running_mean, running_var)

    second_g, second_total, keep, got = back(
        second_sums, second_gb, second_proj, second_sum, second_par, second_w, second_mate
    )
    grad_w_second = weights(second_x, second_g, second_sum, second_total)
    first_gb, first_sums = call(
        back_kernel,
        [shape(length, width), shape(peers, 8, width)],
        scans + grads + edges,
        nbytes=10 << 20,
    )(keep, got, first_proj, first_wide, first_sum, first_par)
    first_g, first_total, keep, got = back(
        first_sums, first_gb, first_proj, first_sum, first_par, first_w, first_mate
    )
    grad_w_first = weights(first_x, first_g, first_sum, first_total)
    input_grad = (keep + got.astype(F32))[:, :real]

    def pair(row):
        return jnp.stack([first_total[row, :real], second_total[row, :real]])

    return (
        first_out[None],
        second_out[None],
        input_grad[None],
        grad_w_first,
        grad_w_second,
        pair(1),
        pair(0),
        pair(2),
        new_mean,
        new_var,
    )


def solution(mesh):
    rows, line, flat = P("seq", None, "neur"), P("neur"), P(None, "neur")
    return jax.shard_map(
        functools.partial(per_device, mesh.shape["seq"]),
        mesh=mesh,
        in_specs=(rows, flat, line, line, line, flat, line, line, line, rows, flat, flat),
        out_specs=(rows, rows, rows) + (flat,) * 7,
        check_vma=False,
    )
```

```python
import functools
import math

import jax
import jax.numpy as jnp
from jax import lax
from jax.experimental import pallas as pl
from jax.experimental.pallas import tpu as pltpu
from jax.sharding import PartitionSpec as P

EPSILON = 1e-05
MOMENTUM = 0.1
LANE = 128
CHUNKS = 32
GROUPS = CHUNKS // 8
TOLERANCE = 1e-5
LOG2E = math.log2(math.e)
LN2 = math.log(2.0)
F32 = jnp.float32
BF16 = jnp.bfloat16
VMEM_BYTES = 16 * 1024 * 1024


def call(kernel, outs, scratch=(), **specs):
    return pl.pallas_call(
        kernel,
        **specs,
        out_shape=outs,
        scratch_shapes=list(scratch),
        compiler_params=pltpu.CompilerParams(vmem_limit_bytes=VMEM_BYTES),
    )


def shape(*dims, dtype=F32):
    return jax.ShapeDtypeStruct(dims, dtype)


def tiles_of(width):
    return [(j, j * LANE, min(LANE, width - j * LANE)) for j in range(-(-width // LANE))]


def dot(a, b):
    return jnp.dot(a, b, preferred_element_type=F32)


def dot_nt(a, b):
    return lax.dot_general(a, b, (((1,), (1,)), ((), ())), preferred_element_type=F32)


def block_kernel(w_ref, gain_ref, shift_ref, decay_ref, out_ref, mate_ref, par_ref):
    here = lax.axis_index("neur")
    blocks, width, _ = out_ref.shape
    real = w_ref.shape[0] // blocks
    out_ref[...] = jnp.zeros(out_ref.shape, BF16)
    for b in range(blocks):
        out_ref[b, :real, : w_ref.shape[1]] = w_ref[b * real : (b + 1) * real, :]
    for i, k in enumerate((1, 3)):
        mate_ref[i] = out_ref[here ^ k]
    par_ref[...] = jnp.zeros(par_ref.shape, F32)
    for i, row_ref in enumerate((gain_ref, shift_ref, decay_ref)):
        par_ref[i : i + 1, : row_ref.shape[1]] = row_ref[...]


def means_of(x_ref):
    length = x_ref.shape[0]
    return dot(jnp.ones((16, length), BF16), x_ref[...])[:1] * (1.0 / length)


def project_early(own_ref, mate_ref, w_ref, part_ref, means_ref):
    here = lax.axis_index("neur")
    k = own_ref.shape[1]
    means_ref[...] = jnp.zeros(means_ref.shape, F32)
    means_ref[0:1, :k] = means_of(own_ref)
    means_ref[1:2, :k] = means_of(mate_ref)
    for c in range(0, part_ref.shape[1], 256):
        part_ref[:, c : c + 256] = dot(own_ref[...], w_ref[here, :k, c : c + 256]) + dot(
            mate_ref[...], w_ref[here ^ 1, :k, c : c + 256]
        )


def project_late(part_ref, means_ref, far_ref, cross_ref, w_ref, proj_ref, stats_ref):
    here = lax.axis_index("neur")
    k = far_ref.shape[1]
    peers, _, width = stats_ref.shape
    far, cross = means_of(far_ref), means_of(cross_ref)
    for p in range(peers):
        stats_ref[p, 2:4, :] = means_ref[0:2, :]
        stats_ref[p, 4:8, :] = jnp.zeros((4, width), F32)
        stats_ref[p, 4:5, :k] = far
        stats_ref[p, 5:6, :k] = cross
    length = proj_ref.shape[0]
    for c in range(0, part_ref.shape[1], 256):
        y = (
            part_ref[:, c : c + 256]
            + dot(far_ref[...], w_ref[here ^ 2, :k, c : c + 256])
            + dot(cross_ref[...], w_ref[here ^ 3, :k, c : c + 256])
        )
        proj_ref[:, c : c + 256] = y
        mean = jnp.sum(y, axis=0, keepdims=True) * (1.0 / length)
        off = y - mean
        spread = jnp.sum(off * off, axis=0, keepdims=True)
        for p in range(stats_ref.shape[0]):
            stats_ref[p, 0:1, c : c + 256] = mean
            stats_ref[p, 1:2, c : c + 256] = spread


def merged(stats_ref, length, sum_ref):
    peers = stats_ref.shape[0]
    means = [stats_ref[p, 0:1, :] for p in range(peers)]
    mean = sum(means[1:], means[0]) * (1.0 / peers)
    total = None
    for p in range(peers):
        off = means[p] - mean
        term = stats_ref[p, 1:2, :] + off * off * float(length)
        total = term if total is None else total + term
    var = total * (1.0 / (peers * length))
    inverse = lax.rsqrt(var + EPSILON)
    features = stats_ref[0, 2:6, :]
    for p in range(1, peers):
        features = features + stats_ref[p, 2:6, :]
    sum_ref[0:1, :] = mean
    sum_ref[1:2, :] = var
    sum_ref[2:3, :] = inverse
    sum_ref[3:4, :] = stats_ref[lax.axis_index("seq"), 0:1, :]
    sum_ref[4:8, :] = features * (1.0 / peers)
    return mean, var, inverse


def spread_rows(row, tiles):
    return [jnp.broadcast_to(row[:, c : c + LANE], (8, LANE)) for _, c, _ in tiles]


def load_step(ref, step, tiles, lead=0):
    steps = (ref.shape[1] - lead) // CHUNKS
    return [
        ref[j, pl.ds(lead + step + g * 8 * steps, 8, stride=steps), :]
        for j, _, _ in tiles
        for g in range(GROUPS)
    ]


def store_step(ref, step, tiles, values, lead=0):
    steps = (ref.shape[1] - lead) // CHUNKS
    i = 0
    for j, _, _ in tiles:
        for g in range(GROUPS):
            ref[j, pl.ds(lead + step + g * 8 * steps, 8, stride=steps), :] = values[i]
            i += 1


def rows_before(x, k, fill):
    at = lax.broadcasted_iota(jnp.int32, x.shape, 0)
    return jnp.where(at >= k, pltpu.roll(x, k, axis=0), fill)


def rows_after(x, k, fill):
    at = lax.broadcasted_iota(jnp.int32, x.shape, 0)
    return jnp.where(at < 8 - k, pltpu.roll(x, 8 - k, axis=0), fill)


def whole_row(x, i):
    return jnp.broadcast_to(x[i : i + 1, :], x.shape)


def chain(base, slope, floor=None, back=False):
    shifted, last, first = (rows_after, 0, 7) if back else (rows_before, 7, 0)
    starts = [None] * GROUPS
    carry = jnp.zeros((8, LANE), F32)
    for g in reversed(range(GROUPS)) if back else range(GROUPS):
        b, q, f = base[g], slope[g], None if floor is None else floor[g]
        for k in (1, 2, 4):
            early = shifted(b, k, 0.0)
            if f is not None:
                f = jnp.maximum(f, b + q * shifted(f, k, 0.0))
            b = b + q * early
            q = q * shifted(q, k, 1.0)
        ends = b + q * carry
        if f is not None:
            ends = jnp.maximum(ends, f)
        starts[g] = jnp.where(
            lax.broadcasted_iota(jnp.int32, ends.shape, 0) == first, carry, shifted(ends, 1, 0.0)
        )
        carry = whole_row(ends, last)
    return starts


def by_tile(tiles, run, *lists):
    out = []
    for n in range(len(tiles)):
        out += run(*(x[n * GROUPS : (n + 1) * GROUPS] for x in lists))
    return out


def handed_on(ends):
    out, carry = [], jnp.zeros((8, LANE), F32)
    for x in ends:
        out.append(jnp.where(lax.broadcasted_iota(jnp.int32, x.shape, 0) == 0, carry, rows_before(x, 1, 0.0)))
        carry = whole_row(x, 7)
    return out


def power(x, n):
    out = None
    while n:
        if n & 1:
            out = x if out is None else out * x
        x = x * x
        n >>= 1
    return out


def softplus2(before):
    return [jnp.where(b > 25.0, b * LN2, jnp.log(1.0 + jnp.exp2(b))) for b in before]


def run_bounds(drive_ref, decay, tiles, steps):
    u = [d for d in decay for _ in range(GROUPS)]
    u2 = [d * LOG2E for d in u]

    def body(step, carry):
        state, line = carry
        drive = load_step(drive_ref, step, tiles)
        line = [d + a * v for d, a, v in zip(drive, u, line)]
        state = softplus2([d + a * v for d, a, v in zip(drive, u2, state)])
        return state, line

    zero = [jnp.zeros((8, LANE), F32) for _ in u]
    state, line = lax.fori_loop(0, steps, body, (zero, zero), unroll=11)
    return state, [a * LN2 for a in line]


def run_chunks(drive_ref, state_ref, start, decay, tiles, steps):
    u2 = [d * LOG2E for d in decay for _ in range(GROUPS)]

    def body(step, carry):
        state, slope = carry
        drive = load_step(drive_ref, step, tiles)
        before = [d + u * s for d, u, s in zip(drive, u2, state)]
        state = softplus2(before)
        slope = [a + (b - s * LOG2E) for a, b, s in zip(slope, before, state)]
        store_step(state_ref, step, tiles, state, lead=8)
        return state, slope

    zero = [jnp.zeros((8, LANE), F32) for _ in start]
    state, slope = lax.fori_loop(0, steps, body, (start, zero), unroll=True)
    top = [power(d, steps) for d in decay for _ in range(GROUPS)]
    return state, [t * jnp.exp2(a) for t, a in zip(top, slope)]


def solve(drive_ref, state_ref, decay_row, tiles):
    steps = drive_ref.shape[1] // CHUNKS
    decay = spread_rows(decay_row, tiles)
    top = [power(d, steps) for d in decay for _ in range(GROUPS)]
    low, line = run_bounds(drive_ref, decay, tiles, steps)
    start = by_tile(tiles, lambda f, b, q: chain(b, q, f), low, line, top)

    def again(carry):
        count, worst, _ = carry
        return jnp.logical_and(worst > 0.0, count < CHUNKS + 1)

    def newton(carry):
        count, _, start = carry
        end, slope = run_chunks(drive_ref, state_ref, start, decay, tiles, steps)
        miss = [e - s for e, s in zip(by_tile(tiles, handed_on, end), start)]
        worst = None
        for m, s in zip(miss, start):
            over = jnp.abs(m) - TOLERANCE * jnp.maximum(s, 1.0)
            worst = over if worst is None else jnp.maximum(worst, over)

        def step(miss, slope, start):
            after = [
                jnp.where(
                    lax.broadcasted_iota(jnp.int32, m.shape, 0) == 7,
                    whole_row(miss[g + 1], 0) if g + 1 < GROUPS else 0.0,
                    rows_after(m, 1, 0.0),
                )
                for g, m in enumerate(miss)
            ]
            return [s + c for s, c in zip(start, chain(after, slope))]

        return count + 1, jnp.max(worst), by_tile(tiles, step, miss, slope, start)

    lax.while_loop(again, newton, (jnp.int32(0), jnp.float32(1.0), start))


def run_back(grad_ref, sigma_ref, start, decay, tiles, steps, store):
    u = [d for d in decay for _ in range(GROUPS)]

    def body(i, carry):
        z, prod = carry
        step = steps - 1 - i
        gs = load_step(grad_ref, step, tiles)
        sig = load_step(sigma_ref, step, tiles)
        z = [s * (g + a * v) for s, g, a, v in zip(sig, gs, u, z)]
        if store:
            store_step(grad_ref, step, tiles, z)
            return z, prod
        return z, [p * (s * a) for p, s, a in zip(prod, sig, u)]

    ones = [] if store else [jnp.ones((8, LANE), F32) for _ in start]
    return lax.fori_loop(0, steps, body, (start, ones), unroll=11)


def solve_back(grad_ref, sigma_ref, decay_row, tiles):
    steps = grad_ref.shape[1] // CHUNKS
    decay = spread_rows(decay_row, tiles)
    zero = [jnp.zeros((8, LANE), F32)] * (len(tiles) * GROUPS)
    end, slope = run_back(grad_ref, sigma_ref, zero, decay, tiles, steps, False)
    start = by_tile(tiles, lambda b, q: chain(b, q, back=True), end, slope)
    run_back(grad_ref, sigma_ref, start, decay, tiles, steps, True)


BLOCK = 88


def row_blocks(length, body):
    @pl.loop(0, length // BLOCK)
    def _(i):
        body(pl.ds(pl.multiple_of(i * BLOCK, 8), BLOCK))


def fill_drive(proj_ref, drive_ref, mean, inverse, gain, shift, tiles):
    scale = inverse * gain * LOG2E
    offset = shift * LOG2E

    def body(rows):
        for j, c, _ in tiles:
            at = slice(c, c + LANE)
            drive_ref[j, rows, :] = (proj_ref[rows, at] - mean[:, at]) * scale[:, at] + offset[:, at]

    row_blocks(proj_ref.shape[0], body)


def fill_sigma(drive_ref, prev_ref, decay_row, tiles, length):
    u2 = decay_row * LOG2E

    def body(i, _):
        for j, c, _w in tiles:
            rows = pl.ds(pl.multiple_of(i * BLOCK, 8), BLOCK)
            before = drive_ref[j, rows, :] + u2[:, c : c + LANE] * prev_ref[j, pl.ds(i * BLOCK + 7, BLOCK), :]
            drive_ref[j, rows, :] = 1.0 / (1.0 + jnp.exp2(-before))
        return 0

    lax.fori_loop(0, length // BLOCK, body, 0)


def finish_back(grad_ref, state_ref, proj_ref, mean, inverse, tiles, gb_ref, sums_ref):
    length, width = proj_ref.shape
    zero = tuple(jnp.zeros((1, LANE), F32) for _ in tiles)

    def body(i, carry):
        shift, gain, decay = (list(x) for x in carry)
        rows = pl.ds(pl.multiple_of(i * BLOCK, 8), BLOCK)
        for j, c, _w in tiles:
            at = slice(c, c + LANE)
            gb = grad_ref[j, rows, :]
            gb_ref[rows, at] = gb
            shift[j] = shift[j] + jnp.sum(gb, axis=0, keepdims=True)
            gain[j] = gain[j] + jnp.sum(gb * (proj_ref[rows, at] - mean[:, at]), axis=0, keepdims=True)
            decay[j] = decay[j] + jnp.sum(
                gb * state_ref[j, pl.ds(i * BLOCK + 7, BLOCK), :], axis=0, keepdims=True
            )
        return tuple(shift), tuple(gain), tuple(decay)

    shift, gain, decay = lax.fori_loop(0, length // BLOCK, body, (zero, zero, zero))
    for j, c, _ in tiles:
        at = slice(c, c + LANE)
        scaled = gain[j] * inverse[:, at]
        for p in range(sums_ref.shape[0]):
            sums_ref[p, 0:1, at] = shift[j]
            sums_ref[p, 1:2, at] = scaled
            sums_ref[p, 2:3, at] = decay[j]


def clear(state_ref, tiles):
    for j, _, _ in tiles:
        state_ref[j, 0:8, :] = jnp.zeros((8, LANE), F32)


def put_states(state_ref, out_ref, tiles, wide_ref=None):
    def body(i, _):
        rows = pl.ds(pl.multiple_of(i * 16, 16), 16)
        for j, c, w in tiles:
            s = state_ref[j, pl.ds(pl.multiple_of(8 + i * 16, 8), 16), :]
            out_ref[rows, c : c + w] = s[:, :w].astype(BF16)
            if wide_ref is not None:
                wide_ref[rows, c : c + LANE] = s
        return 0

    lax.fori_loop(0, out_ref.shape[0] // 16, body, 0, unroll=4)


def forward_kernel(stats_ref, proj_ref, par_ref, out_ref, wide_ref, sum_ref, drive, state):
    length, width = proj_ref.shape
    tiles = tiles_of(width)
    outs = tiles_of(out_ref.shape[1])
    mean, var, inverse = merged(stats_ref, length, sum_ref)
    gain, shift, decay = par_ref[0:1, :], par_ref[1:2, :], par_ref[2:3, :]
    fill_drive(proj_ref, drive, mean, inverse, gain, shift, tiles)
    clear(state, tiles)
    solve(drive, state, decay, tiles)
    put_states(state, out_ref, outs, wide_ref)


def turn_kernel(
    stats_ref,
    proj_ref,
    par_ref,
    first_ref,
    cot_hbm,
    rmean_hbm,
    rvar_hbm,
    out_ref,
    gb_ref,
    sums_ref,
    sum_ref,
    nmean_ref,
    nvar_ref,
    drive,
    state,
    grad,
    cot_ref,
    rmean_ref,
    rvar_ref,
    arrived,
):
    copies = [
        pltpu.make_async_copy(a, b, arrived.at[i])
        for i, (a, b) in enumerate(
            ((cot_hbm, cot_ref), (rmean_hbm, rmean_ref), (rvar_hbm, rvar_ref))
        )
    ]
    for copy in copies:
        copy.start()
    length, width = proj_ref.shape
    tiles = tiles_of(width)
    outs = tiles_of(out_ref.shape[1])
    mean, var, inverse = merged(stats_ref, length, sum_ref)
    gain, shift, decay = par_ref[0:1, :], par_ref[1:2, :], par_ref[2:3, :]
    real = out_ref.shape[1]
    count = float(stats_ref.shape[0] * length)
    fill_drive(proj_ref, drive, mean, inverse, gain, shift, tiles)
    clear(state, tiles)
    solve(drive, state, decay, tiles)
    put_states(state, out_ref, outs)
    fill_sigma(drive, state, decay, tiles, length)
    for copy in copies:
        copy.wait()
    for row, m, v in ((0, first_ref[0:1, :], first_ref[1:2, :]), (1, mean, var)):
        nmean_ref[row : row + 1, :] = (1.0 - MOMENTUM) * rmean_ref[row : row + 1, :] + MOMENTUM * m[:, :real]
        nvar_ref[row : row + 1, :] = (1.0 - MOMENTUM) * rvar_ref[row : row + 1, :] + (
            MOMENTUM * v[:, :real]
        ) * (count / (count - 1.0))
    for j, _, w in outs:
        if w < LANE:
            grad[j] = jnp.zeros(grad.shape[1:], F32)

    def load_cot(i, _):
        rows = pl.ds(pl.multiple_of(i * 16, 16), 16)
        for j, c, w in outs:
            grad[j, rows, :w] = cot_ref[rows, c : c + w].astype(F32)
        return 0

    lax.fori_loop(0, length // 16, load_cot, 0, unroll=4)
    solve_back(grad, drive, decay, tiles)
    finish_back(grad, state, proj_ref, mean, inverse, tiles, gb_ref, sums_ref)


def back_kernel(
    keep_ref, got_ref, proj_ref, wide_ref, sum_ref, par_ref, gb_ref, sums_ref, drive, state, grad
):
    length, width = proj_ref.shape
    tiles = tiles_of(width)
    mean, inverse = sum_ref[0:1, :], sum_ref[2:3, :]
    gain, shift, decay = par_ref[0:1, :], par_ref[1:2, :], par_ref[2:3, :]
    fill_drive(proj_ref, drive, mean, inverse, gain, shift, tiles)
    clear(state, tiles)

    def load(i, _):
        rows = pl.ds(pl.multiple_of(i * 16, 16), 16)
        for j, c, _w in tiles:
            at = slice(c, c + LANE)
            grad[j, rows, :] = keep_ref[rows, at] + got_ref[rows, at].astype(F32)
            state[j, pl.ds(pl.multiple_of(8 + i * 16, 8), 16), :] = wide_ref[rows, at]
        return 0

    lax.fori_loop(0, length // 16, load, 0, unroll=4)
    fill_sigma(drive, state, decay, tiles, length)
    solve_back(grad, drive, decay, tiles)
    finish_back(grad, state, proj_ref, mean, inverse, tiles, gb_ref, sums_ref)


def total_of(sums_ref):
    peers = sums_ref.shape[0]
    out = sums_ref[0]
    for p in range(1, peers):
        out = out + sums_ref[p]
    return out


def grad_kernel(sums_ref, gb_ref, proj_ref, sum_ref, par_ref, g_ref, total_ref):
    length, _ = proj_ref.shape
    total = total_of(sums_ref)
    total_ref[...] = total
    count = float(sums_ref.shape[0] * length)
    mean, inverse = sum_ref[0:1, :], sum_ref[2:3, :]
    scale = par_ref[0:1, :] * inverse
    base = total[0:1, :] * (1.0 / count)
    lean = total[1:2, :] * (1.0 / count) * inverse

    total_ref[7:8, :] = scale * (
        sums_ref[lax.axis_index("seq"), 0:1, :]
        - length * base
        - length * (sum_ref[3:4, :] - mean) * lean
    )

    def body(i, _):
        rows = pl.ds(pl.multiple_of(i * 16, 16), 16)
        g_ref[rows, :] = (
            scale * (gb_ref[rows, :] - base - (proj_ref[rows, :] - mean) * lean)
        ).astype(BF16)
        return 0

    lax.fori_loop(0, length // 16, body, 0, unroll=4)


def send_kernel(g_ref, mate_ref, w_ref, wmate_ref, out_ref):
    here = lax.axis_index("neur")
    for c in range(0, out_ref.shape[1], 256):
        at = slice(c, c + 256)
        out_ref[:, at] = (
            dot_nt(g_ref[...], w_ref[here ^ 2, at, :]) + dot_nt(mate_ref[...], wmate_ref[1, at, :])
        ).astype(BF16)


def keep_kernel(g_ref, mate_ref, w_ref, wmate_ref, out_ref):
    here = lax.axis_index("neur")
    for c in range(0, out_ref.shape[1], 256):
        at = slice(c, c + 256)
        out_ref[:, at] = dot_nt(g_ref[...], w_ref[here, at, :]) + dot_nt(
            mate_ref[...], wmate_ref[0, at, :]
        )


def split(row):
    high = row.astype(BF16)
    return high, (row - high.astype(F32)).astype(BF16)


def dot_tn(a, b):
    return lax.dot_general(a, b, (((0,), (0,)), ((), ())), preferred_element_type=F32)


def outer(a, b):
    (a_high, a_low), (b_high, b_low) = split(a), split(b)
    return dot_tn(
        jnp.concatenate([a_high, a_high, a_low, a_low]), jnp.concatenate([b_high, b_low, b_high, b_low])
    )


def weight_kernel(parted, own_ref, mate_ref, far_ref, cross_ref, g_ref, sum_ref, total_ref, *refs):
    outs, hold = (refs[:-1], refs[-1]) if parted else ((), refs[0])
    place = seat() if parted else 0
    _, half, width = hold.shape
    for k, x_ref in enumerate((own_ref, mate_ref, far_ref, cross_ref)):
        real = x_ref.shape[1]
        mean = sum_ref[4 + k : 5 + k, :real]
        part = (dot_tn(x_ref[...], g_ref[...]) - outer(mean, total_ref[7:8, :])).astype(BF16)
        hold[(2 * k) ^ place] = part[:half]
        rest = part[half:]
        hold[(2 * k + 1) ^ place, : rest.shape[0], :] = rest
        if not parted:
            hold[2 * k + 1, rest.shape[0] :, :] = jnp.zeros((half - rest.shape[0], width), BF16)
    count = hold.shape[0] // len(outs) if outs else 0
    for r, out in enumerate(outs):
        out[...] = hold[r] if count == 1 else hold[r * count : (r + 1) * count]


def halve_kernel(keep_ref, got_ref, mine_ref, give_ref):
    count = mine_ref.shape[0]
    for i in range(2 * count):
        value = wide_sum(keep_ref[i], got_ref[i])
        if i < count:
            mine_ref[i] = value
        else:
            give_ref[i - count] = value.astype(BF16)


def spread_kernel(parted, *refs):
    if parted:
        shares, out_ref, hold = refs[:-2], refs[-2], refs[-1]
        for r, share in enumerate(shares):
            hold[r] = share[...]
    else:
        hold, out_ref = refs
    place, here = seat() if parted else 0, lax.axis_index("neur")
    half = hold.shape[1]
    block = out_ref.shape[0] // 4
    width = out_ref.shape[1]
    for b in range(4):
        for h in range(2):
            low, high = b * block + h * half, min(b * block + h * half + half, (b + 1) * block)
            which = (((here ^ b) * 2) + h) ^ place
            out_ref[low:high, :] = hold[which, : high - low, :width].astype(F32)


def wide_sum(a, b):
    return a.astype(F32) + b.astype(F32)


def half_sum(a, b):
    return wide_sum(a, b).astype(BF16)


def swap(x, bit, axis="seq"):
    n = lax.axis_size(axis)
    return lax.ppermute(x, axis, [(i, i ^ bit) for i in range(n)])


LEVEL = {4: 1, 2: 2, 1: 4}


def seat():
    place = lax.axis_index("seq")
    return ((place & 1) << 2) | (place & 2) | ((place >> 2) & 1)


def send_shares(shares):
    part = {(r >> 2 & 1, r >> 1 & 1, r & 1): v for r, v in enumerate(shares)}
    return part, {q: swap(part[(1,) + q], LEVEL[4]) for q in ((1, 1), (1, 0), (0, 1), (0, 0))}


def halve_shares(part, got):
    mine = {q: wide_sum(part[(0,) + q], v) for q, v in got.items()}
    away, near = (swap(mine[(1, i)].astype(BF16), LEVEL[2]) for i in (1, 0))
    return {i: mine[(0, i)] for i in (0, 1)}, away, near


def quarter_shares(mine, away, near):
    return wide_sum(mine[0], near), swap(half_sum(mine[1], away), LEVEL[1])


def gather_shares(v):
    out = {0: v}
    out[4] = swap(v, LEVEL[4])
    out[2] = swap(v, LEVEL[2])
    out[1] = swap(v, LEVEL[1])
    out[2], out[4] = lax.optimization_barrier((out[2], out[4]))
    out[6] = swap(out[2], LEVEL[4])
    out[5] = swap(out[1], LEVEL[4])
    out[3] = swap(out[1], LEVEL[2])
    out[3], out[6] = lax.optimization_barrier((out[3], out[6]))
    out[7] = swap(out[3], LEVEL[4])
    return [out[r] for r in range(8)]


def per_device(devices_seq, *args):
    (
        tokens,
        w_first,
        gain_first,
        shift_first,
        decay_first,
        w_second,
        gain_second,
        shift_second,
        decay_second,
        cotangent,
        running_mean,
        running_var,
    ) = args
    _, length, real = tokens.shape
    width = -(-real // LANE) * LANE
    tiles = len(tiles_of(width))
    peers = devices_seq
    here = lax.axis_index("neur")
    tokens, cotangent = tokens[0], cotangent[0]

    scans = [
        pltpu.VMEM((tiles, length, LANE), F32),
        pltpu.VMEM((tiles, length + 8, LANE), F32),
    ]
    grads = [pltpu.VMEM((tiles, length, LANE), F32)]

    def share(stats):
        return lax.all_to_all(stats, "seq", 0, 0, tiled=True)

    def project(own, w, rows, *gives):
        far = swap(own, 2, "neur")
        mate = swap(own, 1, "neur")
        w = lax.optimization_barrier((w, own))[0]
        w4, give, par = call(
            block_kernel,
            [shape(4, width, width, dtype=BF16), shape(2, width, width, dtype=BF16), shape(8, width)],
        )(w, *(row[None] for row in rows))
        part, means = call(project_early, [shape(length, width), shape(8, width)])(own, mate, w4)
        gives = [swap(lax.optimization_barrier((g, own))[0], 1, "neur") for g in gives + (give,)] if gives else give
        far, part, par, gives = lax.optimization_barrier((far, part, par, gives))
        cross = swap(far, 1, "neur")
        proj, stats = call(project_late, [shape(length, width), shape(peers, 8, width)])(
            part, means, far, cross, w4
        )
        return (own, mate, far, cross), proj, share(stats), w4, gives, par

    def gradient(sums, gb, proj, summary, par):
        return call(grad_kernel, [shape(length, width, dtype=BF16), shape(8, width)])(
            sums, gb, proj, summary, par
        )

    def send(g, mate, w4, wm):
        out = call(send_kernel, shape(length, width, dtype=BF16))(g, mate, w4, wm)
        out, g, mate = lax.optimization_barrier((out, g, mate))
        got = swap(out, 2, "neur")
        keep = call(keep_kernel, shape(length, width))(g, mate, w4, wm)
        return out, keep, got

    half = width // 2

    def parts_shape(*lead):
        return shape(*lead, half, width, dtype=BF16)

    def weight_parts(fine, *operands):
        if peers != 8:
            return call(functools.partial(weight_kernel, False), parts_shape(8))(*operands)
        return call(
            functools.partial(weight_kernel, True),
            [parts_shape()] * 8 if fine else [parts_shape(4)] * 2,
            [pltpu.VMEM((8, half, width), BF16)],
        )(*operands)

    def weights(shares):
        if peers != 8:
            return call(functools.partial(spread_kernel, False), shape(4 * real, real))(shares)
        return call(
            functools.partial(spread_kernel, True),
            shape(4 * real, real),
            [pltpu.VMEM((8, half, width), BF16)],
        )(*gather_shares(shares))

    def together(*values):
        return lax.optimization_barrier(values)

    first_x, first_proj, first_stats, first_w, give, first_par = project(
        tokens, w_first, (gain_first, shift_first, decay_first)
    )
    first_out, first_wide, first_sum = call(
        forward_kernel,
        [shape(length, real, dtype=BF16), shape(length, width), shape(8, width)],
        scans)(first_stats, first_proj, first_par)

    second_x, second_proj, second_stats, second_w, (first_mate, second_mate), second_par = project(
        first_out, w_second, (gain_second, shift_second, decay_second), give
    )
    second_out, second_gb, second_sums, second_sum, new_mean, new_var = call(
        turn_kernel,
        [
            shape(length, real, dtype=BF16),
            shape(length, width),
            shape(peers, 8, width),
            shape(8, width),
            shape(2, real),
            shape(2, real),
        ],
        scans
        + grads
        + [
            pltpu.VMEM((length, real), BF16),
            pltpu.VMEM((2, real), F32),
            pltpu.VMEM((2, real), F32),
            pltpu.SemaphoreType.DMA((3,)),
        ],
        in_specs=[pl.BlockSpec(memory_space=pltpu.VMEM)] * 4 + [pl.BlockSpec(memory_space=pl.ANY)] * 3,
    )(second_stats, second_proj, second_par, first_sum, cotangent, running_mean, running_var)

    def after(x, *earlier):
        return lax.optimization_barrier((x, earlier))[0]

    second_sums = share(second_sums)
    second_g, second_total = gradient(second_sums, second_gb, second_proj, second_sum, second_par)
    mate = swap(second_g, 1, "neur")
    second_parts = weight_parts(False, *second_x, second_g, second_sum, second_total)
    mate, second_parts = together(mate, second_parts)
    out, keep, got = send(second_g, mate, second_w, second_mate)
    if peers == 8:
        parcel = swap(second_parts[1], LEVEL[4])
    first_gb, first_sums = call(
        back_kernel, [shape(length, width), shape(peers, 8, width)], scans + grads
    )(keep, got, first_proj, first_wide, first_sum, first_par)
    if peers == 8:
        mine, give = call(halve_kernel, [shape(2, half, width), parts_shape(2)])(
            second_parts[0], after(parcel, first_gb)
        )
        parcel = swap(give, LEVEL[2])
    first_sums = share(first_sums)
    first_g, first_total = gradient(first_sums, first_gb, first_proj, first_sum, first_par)
    mate = swap(first_g, 1, "neur")
    first_parts = weight_parts(True, *first_x, first_g, first_sum, first_total)
    mate, first_parts = together(mate, first_parts)
    out, keep, got = send(first_g, mate, first_w, first_mate)
    if peers == 8:
        part, parcels = send_shares(first_parts)
        mine, give = call(halve_kernel, [shape(1, half, width), parts_shape(1)])(
            mine, after(parcel, first_parts)
        )
        second_share = half_sum(*after((mine[0], swap(give[0], LEVEL[1])), keep))
        first_share = half_sum(*quarter_shares(*halve_shares(part, parcels)))
    else:
        second_share, first_share = lax.psum((second_parts, first_parts), "seq")
    grad_w_first = weights(first_share)
    grad_w_second = weights(second_share)
    input_grad = (keep + got.astype(F32))[:, :real]

    def pair(row):
        return jnp.stack([first_total[row, :real], second_total[row, :real]])

    return (
        first_out[None],
        second_out[None],
        input_grad[None],
        grad_w_first,
        grad_w_second,
        pair(1),
        pair(0),
        pair(2),
        new_mean,
        new_var,
    )


def solution(mesh):
    rows, line, flat = P("seq", None, "neur"), P("neur"), P(None, "neur")
    return jax.shard_map(
        functools.partial(per_device, mesh.shape["seq"]),
        mesh=mesh,
        in_specs=(rows, flat, line, line, line, flat, line, line, line, rows, flat, flat),
        out_specs=(rows, rows, rows) + (flat,) * 7,
        check_vma=False,
    )
```

```python
import functools
import math

import jax
import jax.numpy as jnp
from jax import lax
from jax.experimental import pallas as pl
from jax.experimental.pallas import tpu as pltpu
from jax.sharding import PartitionSpec as P

EPSILON = 1e-05
MOMENTUM = 0.1
LANE = 128
CHUNKS = 32
GROUPS = CHUNKS // 8
TOLERANCE = 1e-5
LOG2E = math.log2(math.e)
LN2 = math.log(2.0)
F32 = jnp.float32
BF16 = jnp.bfloat16
VMEM_BYTES = 16 * 1024 * 1024


def call(kernel, outs, scratch=(), **specs):
    return pl.pallas_call(
        kernel,
        **specs,
        out_shape=outs,
        scratch_shapes=list(scratch),
        compiler_params=pltpu.CompilerParams(vmem_limit_bytes=VMEM_BYTES),
    )


def shape(*dims, dtype=F32):
    return jax.ShapeDtypeStruct(dims, dtype)


def tiles_of(width):
    return [(j, j * LANE, min(LANE, width - j * LANE)) for j in range(-(-width // LANE))]


def dot(a, b):
    return jnp.dot(a, b, preferred_element_type=F32)


def dot_nt(a, b):
    return lax.dot_general(a, b, (((1,), (1,)), ((), ())), preferred_element_type=F32)


def block_kernel(w_ref, gain_ref, shift_ref, decay_ref, out_ref, mate_ref, par_ref):
    here = lax.axis_index("neur")
    blocks, width, _ = out_ref.shape
    real = w_ref.shape[0] // blocks
    out_ref[...] = jnp.zeros(out_ref.shape, BF16)
    for b in range(blocks):
        out_ref[b, :real, : w_ref.shape[1]] = w_ref[b * real : (b + 1) * real, :]
    for i, k in enumerate((1, 3)):
        mate_ref[i] = out_ref[here ^ k]
    par_ref[...] = jnp.zeros(par_ref.shape, F32)
    for i, row_ref in enumerate((gain_ref, shift_ref, decay_ref)):
        par_ref[i : i + 1, : row_ref.shape[1]] = row_ref[...]


def means_of(x_ref):
    length = x_ref.shape[0]
    return dot(jnp.ones((16, length), BF16), x_ref[...])[:1] * (1.0 / length)


def project_early(own_ref, mate_ref, w_ref, part_ref, means_ref):
    here = lax.axis_index("neur")
    k = own_ref.shape[1]
    means_ref[...] = jnp.zeros(means_ref.shape, F32)
    means_ref[0:1, :k] = means_of(own_ref)
    means_ref[1:2, :k] = means_of(mate_ref)
    for c in range(0, part_ref.shape[1], 256):
        part_ref[:, c : c + 256] = dot(own_ref[...], w_ref[here, :k, c : c + 256]) + dot(
            mate_ref[...], w_ref[here ^ 1, :k, c : c + 256]
        )


def project_late(part_ref, means_ref, far_ref, cross_ref, w_ref, proj_ref, stats_ref):
    here = lax.axis_index("neur")
    k = far_ref.shape[1]
    peers, _, width = stats_ref.shape
    far, cross = means_of(far_ref), means_of(cross_ref)
    for p in range(peers):
        stats_ref[p, 2:4, :] = means_ref[0:2, :]
        stats_ref[p, 4:8, :] = jnp.zeros((4, width), F32)
        stats_ref[p, 4:5, :k] = far
        stats_ref[p, 5:6, :k] = cross
    length = proj_ref.shape[0]
    for c in range(0, part_ref.shape[1], 256):
        y = (
            part_ref[:, c : c + 256]
            + dot(far_ref[...], w_ref[here ^ 2, :k, c : c + 256])
            + dot(cross_ref[...], w_ref[here ^ 3, :k, c : c + 256])
        )
        proj_ref[:, c : c + 256] = y
        mean = jnp.sum(y, axis=0, keepdims=True) * (1.0 / length)
        off = y - mean
        spread = jnp.sum(off * off, axis=0, keepdims=True)
        for p in range(stats_ref.shape[0]):
            stats_ref[p, 0:1, c : c + 256] = mean
            stats_ref[p, 1:2, c : c + 256] = spread


def merged(stats_ref, length, sum_ref):
    peers = stats_ref.shape[0]
    means = [stats_ref[p, 0:1, :] for p in range(peers)]
    mean = sum(means[1:], means[0]) * (1.0 / peers)
    total = None
    for p in range(peers):
        off = means[p] - mean
        term = stats_ref[p, 1:2, :] + off * off * float(length)
        total = term if total is None else total + term
    var = total * (1.0 / (peers * length))
    inverse = lax.rsqrt(var + EPSILON)
    features = stats_ref[0, 2:6, :]
    for p in range(1, peers):
        features = features + stats_ref[p, 2:6, :]
    sum_ref[0:1, :] = mean
    sum_ref[1:2, :] = var
    sum_ref[2:3, :] = inverse
    sum_ref[3:4, :] = stats_ref[lax.axis_index("seq"), 0:1, :]
    sum_ref[4:8, :] = features * (1.0 / peers)
    return mean, var, inverse


def spread_rows(row, tiles):
    return [jnp.broadcast_to(row[:, c : c + LANE], (8, LANE)) for _, c, _ in tiles]


def load_step(ref, step, tiles, lead=0):
    steps = (ref.shape[1] - lead) // CHUNKS
    return [
        ref[j, pl.ds(lead + step + g * 8 * steps, 8, stride=steps), :]
        for j, _, _ in tiles
        for g in range(GROUPS)
    ]


def store_step(ref, step, tiles, values, lead=0):
    steps = (ref.shape[1] - lead) // CHUNKS
    i = 0
    for j, _, _ in tiles:
        for g in range(GROUPS):
            ref[j, pl.ds(lead + step + g * 8 * steps, 8, stride=steps), :] = values[i]
            i += 1


def rows_before(x, k, fill):
    at = lax.broadcasted_iota(jnp.int32, x.shape, 0)
    return jnp.where(at >= k, pltpu.roll(x, k, axis=0), fill)


def rows_after(x, k, fill):
    at = lax.broadcasted_iota(jnp.int32, x.shape, 0)
    return jnp.where(at < 8 - k, pltpu.roll(x, 8 - k, axis=0), fill)


def whole_row(x, i):
    return jnp.broadcast_to(x[i : i + 1, :], x.shape)


def chain(base, slope, floor=None, back=False):
    shifted, last, first = (rows_after, 0, 7) if back else (rows_before, 7, 0)
    starts = [None] * GROUPS
    carry = jnp.zeros((8, LANE), F32)
    for g in reversed(range(GROUPS)) if back else range(GROUPS):
        b, q, f = base[g], slope[g], None if floor is None else floor[g]
        for k in (1, 2, 4):
            early = shifted(b, k, 0.0)
            if f is not None:
                f = jnp.maximum(f, b + q * shifted(f, k, 0.0))
            b = b + q * early
            q = q * shifted(q, k, 1.0)
        ends = b + q * carry
        if f is not None:
            ends = jnp.maximum(ends, f)
        starts[g] = jnp.where(
            lax.broadcasted_iota(jnp.int32, ends.shape, 0) == first, carry, shifted(ends, 1, 0.0)
        )
        carry = whole_row(ends, last)
    return starts


def by_tile(tiles, run, *lists):
    out = []
    for n in range(len(tiles)):
        out += run(*(x[n * GROUPS : (n + 1) * GROUPS] for x in lists))
    return out


def handed_on(ends):
    out, carry = [], jnp.zeros((8, LANE), F32)
    for x in ends:
        out.append(jnp.where(lax.broadcasted_iota(jnp.int32, x.shape, 0) == 0, carry, rows_before(x, 1, 0.0)))
        carry = whole_row(x, 7)
    return out


def power(x, n):
    out = None
    while n:
        if n & 1:
            out = x if out is None else out * x
        x = x * x
        n >>= 1
    return out


def softplus2(before):
    return [jnp.where(b > 25.0, b * LN2, jnp.log(1.0 + jnp.exp2(b))) for b in before]


def run_bounds(drive_ref, decay, tiles, steps):
    u = [d for d in decay for _ in range(GROUPS)]
    u2 = [d * LOG2E for d in u]

    def body(step, carry):
        state, line = carry
        drive = load_step(drive_ref, step, tiles)
        line = [d + a * v for d, a, v in zip(drive, u, line)]
        state = softplus2([d + a * v for d, a, v in zip(drive, u2, state)])
        return state, line

    zero = [jnp.zeros((8, LANE), F32) for _ in u]
    state, line = lax.fori_loop(0, steps, body, (zero, zero), unroll=11)
    return state, [a * LN2 for a in line]


def run_chunks(drive_ref, state_ref, start, decay, tiles, steps):
    u2 = [d * LOG2E for d in decay for _ in range(GROUPS)]

    def body(step, carry):
        state, slope = carry
        drive = load_step(drive_ref, step, tiles)
        before = [d + u * s for d, u, s in zip(drive, u2, state)]
        state = softplus2(before)
        slope = [a + (b - s * LOG2E) for a, b, s in zip(slope, before, state)]
        store_step(state_ref, step, tiles, state, lead=8)
        return state, slope

    zero = [jnp.zeros((8, LANE), F32) for _ in start]
    state, slope = lax.fori_loop(0, steps, body, (start, zero), unroll=True)
    top = [power(d, steps) for d in decay for _ in range(GROUPS)]
    return state, [t * jnp.exp2(a) for t, a in zip(top, slope)]


def solve(drive_ref, state_ref, decay_row, tiles):
    steps = drive_ref.shape[1] // CHUNKS
    decay = spread_rows(decay_row, tiles)
    top = [power(d, steps) for d in decay for _ in range(GROUPS)]
    low, line = run_bounds(drive_ref, decay, tiles, steps)
    start = by_tile(tiles, lambda f, b, q: chain(b, q, f), low, line, top)

    def again(carry):
        count, worst, _ = carry
        return jnp.logical_and(worst > 0.0, count < CHUNKS + 1)

    def newton(carry):
        count, _, start = carry
        end, slope = run_chunks(drive_ref, state_ref, start, decay, tiles, steps)
        miss = [e - s for e, s in zip(by_tile(tiles, handed_on, end), start)]
        worst = None
        for m, s in zip(miss, start):
            over = jnp.abs(m) - TOLERANCE * jnp.maximum(s, 1.0)
            worst = over if worst is None else jnp.maximum(worst, over)

        def step(miss, slope, start):
            after = [
                jnp.where(
                    lax.broadcasted_iota(jnp.int32, m.shape, 0) == 7,
                    whole_row(miss[g + 1], 0) if g + 1 < GROUPS else 0.0,
                    rows_after(m, 1, 0.0),
                )
                for g, m in enumerate(miss)
            ]
            return [s + c for s, c in zip(start, chain(after, slope))]

        return count + 1, jnp.max(worst), by_tile(tiles, step, miss, slope, start)

    lax.while_loop(again, newton, (jnp.int32(0), jnp.float32(1.0), start))


def run_back(grad_ref, sigma_ref, start, decay, tiles, steps, store):
    u = [d for d in decay for _ in range(GROUPS)]

    def body(i, carry):
        z, prod = carry
        step = steps - 1 - i
        gs = load_step(grad_ref, step, tiles)
        sig = load_step(sigma_ref, step, tiles)
        z = [s * (g + a * v) for s, g, a, v in zip(sig, gs, u, z)]
        if store:
            store_step(grad_ref, step, tiles, z)
            return z, prod
        return z, [p * (s * a) for p, s, a in zip(prod, sig, u)]

    ones = [] if store else [jnp.ones((8, LANE), F32) for _ in start]
    return lax.fori_loop(0, steps, body, (start, ones), unroll=11)


def solve_back(grad_ref, sigma_ref, decay_row, tiles):
    steps = grad_ref.shape[1] // CHUNKS
    decay = spread_rows(decay_row, tiles)
    zero = [jnp.zeros((8, LANE), F32)] * (len(tiles) * GROUPS)
    end, slope = run_back(grad_ref, sigma_ref, zero, decay, tiles, steps, False)
    start = by_tile(tiles, lambda b, q: chain(b, q, back=True), end, slope)
    run_back(grad_ref, sigma_ref, start, decay, tiles, steps, True)


BLOCK = 88


def row_blocks(length, body):
    @pl.loop(0, length // BLOCK)
    def _(i):
        body(pl.ds(pl.multiple_of(i * BLOCK, 8), BLOCK))


def fill_drive(proj_ref, drive_ref, mean, inverse, gain, shift, tiles):
    scale = inverse * gain * LOG2E
    offset = shift * LOG2E

    def body(rows):
        for j, c, _ in tiles:
            at = slice(c, c + LANE)
            drive_ref[j, rows, :] = (proj_ref[rows, at] - mean[:, at]) * scale[:, at] + offset[:, at]

    row_blocks(proj_ref.shape[0], body)


def fill_sigma(drive_ref, prev_ref, decay_row, tiles, length):
    u2 = decay_row * LOG2E

    def body(i, _):
        for j, c, _w in tiles:
            rows = pl.ds(pl.multiple_of(i * BLOCK, 8), BLOCK)
            before = drive_ref[j, rows, :] + u2[:, c : c + LANE] * prev_ref[j, pl.ds(i * BLOCK + 7, BLOCK), :]
            drive_ref[j, rows, :] = 1.0 / (1.0 + jnp.exp2(-before))
        return 0

    lax.fori_loop(0, length // BLOCK, body, 0)


def finish_back(grad_ref, state_ref, proj_ref, mean, inverse, tiles, gb_ref, sums_ref):
    length, width = proj_ref.shape
    zero = tuple(jnp.zeros((1, LANE), F32) for _ in tiles)

    def body(i, carry):
        shift, gain, decay = (list(x) for x in carry)
        rows = pl.ds(pl.multiple_of(i * BLOCK, 8), BLOCK)
        for j, c, _w in tiles:
            at = slice(c, c + LANE)
            gb = grad_ref[j, rows, :]
            gb_ref[rows, at] = gb
            shift[j] = shift[j] + jnp.sum(gb, axis=0, keepdims=True)
            gain[j] = gain[j] + jnp.sum(gb * (proj_ref[rows, at] - mean[:, at]), axis=0, keepdims=True)
            decay[j] = decay[j] + jnp.sum(
                gb * state_ref[j, pl.ds(i * BLOCK + 7, BLOCK), :], axis=0, keepdims=True
            )
        return tuple(shift), tuple(gain), tuple(decay)

    shift, gain, decay = lax.fori_loop(0, length // BLOCK, body, (zero, zero, zero))
    for j, c, _ in tiles:
        at = slice(c, c + LANE)
        scaled = gain[j] * inverse[:, at]
        for p in range(sums_ref.shape[0]):
            sums_ref[p, 0:1, at] = shift[j]
            sums_ref[p, 1:2, at] = scaled
            sums_ref[p, 2:3, at] = decay[j]


def clear(state_ref, tiles):
    for j, _, _ in tiles:
        state_ref[j, 0:8, :] = jnp.zeros((8, LANE), F32)


def put_states(state_ref, out_ref, tiles, wide_ref=None):
    def body(i, _):
        rows = pl.ds(pl.multiple_of(i * 16, 16), 16)
        for j, c, w in tiles:
            s = state_ref[j, pl.ds(pl.multiple_of(8 + i * 16, 8), 16), :]
            out_ref[rows, c : c + w] = s[:, :w].astype(BF16)
            if wide_ref is not None:
                wide_ref[rows, c : c + LANE] = s
        return 0

    lax.fori_loop(0, out_ref.shape[0] // 16, body, 0, unroll=4)


def forward_kernel(stats_ref, proj_ref, par_ref, out_ref, wide_ref, sum_ref, norm_ref, total_ref, drive, state):
    length, width = proj_ref.shape
    tiles = tiles_of(width)
    outs = tiles_of(out_ref.shape[1])
    mean, var, inverse = merged(stats_ref, length, sum_ref)
    gain, shift, decay = par_ref[0:1, :], par_ref[1:2, :], par_ref[2:3, :]
    fill_drive(proj_ref, drive, mean, inverse, gain, shift, tiles)
    clear(state, tiles)
    solve(drive, state, decay, tiles)
    put_states(state, out_ref, outs, wide_ref)
    total_ref[...] = jnp.zeros(total_ref.shape, F32)
    total_ref[7:8, :] = length * (sum_ref[3:4, :] - mean) * inverse

    def put_norm(i, _):
        rows = pl.ds(pl.multiple_of(i * 16, 16), 16)
        norm_ref[rows, :] = ((proj_ref[rows, :] - mean) * inverse).astype(BF16)
        return 0

    lax.fori_loop(0, length // 16, put_norm, 0, unroll=4)


def turn_kernel(
    stats_ref,
    proj_ref,
    par_ref,
    first_ref,
    cot_hbm,
    rmean_hbm,
    rvar_hbm,
    out_ref,
    gb_ref,
    sums_ref,
    sum_ref,
    nmean_ref,
    nvar_ref,
    drive,
    state,
    grad,
    cot_ref,
    rmean_ref,
    rvar_ref,
    arrived,
):
    copies = [
        pltpu.make_async_copy(a, b, arrived.at[i])
        for i, (a, b) in enumerate(
            ((cot_hbm, cot_ref), (rmean_hbm, rmean_ref), (rvar_hbm, rvar_ref))
        )
    ]
    for copy in copies:
        copy.start()
    length, width = proj_ref.shape
    tiles = tiles_of(width)
    outs = tiles_of(out_ref.shape[1])
    mean, var, inverse = merged(stats_ref, length, sum_ref)
    gain, shift, decay = par_ref[0:1, :], par_ref[1:2, :], par_ref[2:3, :]
    real = out_ref.shape[1]
    count = float(stats_ref.shape[0] * length)
    fill_drive(proj_ref, drive, mean, inverse, gain, shift, tiles)
    clear(state, tiles)
    solve(drive, state, decay, tiles)
    put_states(state, out_ref, outs)
    fill_sigma(drive, state, decay, tiles, length)
    for copy in copies:
        copy.wait()
    for row, m, v in ((0, first_ref[0:1, :], first_ref[1:2, :]), (1, mean, var)):
        nmean_ref[row : row + 1, :] = (1.0 - MOMENTUM) * rmean_ref[row : row + 1, :] + MOMENTUM * m[:, :real]
        nvar_ref[row : row + 1, :] = (1.0 - MOMENTUM) * rvar_ref[row : row + 1, :] + (
            MOMENTUM * v[:, :real]
        ) * (count / (count - 1.0))
    for j, _, w in outs:
        if w < LANE:
            grad[j] = jnp.zeros(grad.shape[1:], F32)

    def load_cot(i, _):
        rows = pl.ds(pl.multiple_of(i * 16, 16), 16)
        for j, c, w in outs:
            grad[j, rows, :w] = cot_ref[rows, c : c + w].astype(F32)
        return 0

    lax.fori_loop(0, length // 16, load_cot, 0, unroll=4)
    solve_back(grad, drive, decay, tiles)
    finish_back(grad, state, proj_ref, mean, inverse, tiles, gb_ref, sums_ref)


def back_kernel(
    keep_ref, got_ref, proj_ref, wide_ref, sum_ref, par_ref, gb_ref, sums_ref, own_ref, drive, state, grad
):
    length, width = proj_ref.shape
    tiles = tiles_of(width)
    mean, inverse = sum_ref[0:1, :], sum_ref[2:3, :]
    gain, shift, decay = par_ref[0:1, :], par_ref[1:2, :], par_ref[2:3, :]
    fill_drive(proj_ref, drive, mean, inverse, gain, shift, tiles)
    clear(state, tiles)

    def load(i, _):
        rows = pl.ds(pl.multiple_of(i * 16, 16), 16)
        for j, c, _w in tiles:
            at = slice(c, c + LANE)
            grad[j, rows, :] = keep_ref[rows, at] + got_ref[rows, at].astype(F32)
            state[j, pl.ds(pl.multiple_of(8 + i * 16, 8), 16), :] = wide_ref[rows, at]
        return 0

    lax.fori_loop(0, length // 16, load, 0, unroll=4)
    fill_sigma(drive, state, decay, tiles, length)
    solve_back(grad, drive, decay, tiles)
    finish_back(grad, state, proj_ref, mean, inverse, tiles, gb_ref, sums_ref)
    scale = gain * inverse
    average = sums_ref[0, 0:1, :] * (1.0 / length)

    def put_own(i, _):
        rows = pl.ds(pl.multiple_of(i * 16, 16), 16)
        own_ref[rows, :] = (scale * (gb_ref[rows, :] - average)).astype(BF16)
        return 0

    lax.fori_loop(0, length // 16, put_own, 0, unroll=4)


def total_of(sums_ref):
    peers = sums_ref.shape[0]
    out = sums_ref[0]
    for p in range(1, peers):
        out = out + sums_ref[p]
    return out


def grad_kernel(sums_ref, gb_ref, proj_ref, sum_ref, par_ref, g_ref, total_ref):
    length, _ = proj_ref.shape
    total = total_of(sums_ref)
    total_ref[...] = total
    count = float(sums_ref.shape[0] * length)
    mean, inverse = sum_ref[0:1, :], sum_ref[2:3, :]
    scale = par_ref[0:1, :] * inverse
    base = total[0:1, :] * (1.0 / count)
    lean = total[1:2, :] * (1.0 / count) * inverse

    total_ref[7:8, :] = scale * (
        sums_ref[lax.axis_index("seq"), 0:1, :]
        - length * base
        - length * (sum_ref[3:4, :] - mean) * lean
    )

    def body(i, _):
        rows = pl.ds(pl.multiple_of(i * 16, 16), 16)
        g_ref[rows, :] = (
            scale * (gb_ref[rows, :] - base - (proj_ref[rows, :] - mean) * lean)
        ).astype(BF16)
        return 0

    lax.fori_loop(0, length // 16, body, 0, unroll=4)


def send_kernel(g_ref, mate_ref, w_ref, wmate_ref, out_ref):
    here = lax.axis_index("neur")
    for c in range(0, out_ref.shape[1], 256):
        at = slice(c, c + 256)
        out_ref[:, at] = (
            dot_nt(g_ref[...], w_ref[here ^ 2, at, :]) + dot_nt(mate_ref[...], wmate_ref[1, at, :])
        ).astype(BF16)


def keep_kernel(g_ref, mate_ref, w_ref, wmate_ref, out_ref):
    here = lax.axis_index("neur")
    for c in range(0, out_ref.shape[1], 256):
        at = slice(c, c + 256)
        out_ref[:, at] = dot_nt(g_ref[...], w_ref[here, at, :]) + dot_nt(
            mate_ref[...], wmate_ref[0, at, :]
        )


def split(row):
    high = row.astype(BF16)
    return high, (row - high.astype(F32)).astype(BF16)


def dot_tn(a, b):
    return lax.dot_general(a, b, (((0,), (0,)), ((), ())), preferred_element_type=F32)


def outer(a, b):
    (a_high, a_low), (b_high, b_low) = split(a), split(b)
    return dot_tn(
        jnp.concatenate([a_high, a_high, a_low, a_low]), jnp.concatenate([b_high, b_low, b_high, b_low])
    )


def weight_kernel(parted, own_ref, mate_ref, far_ref, cross_ref, g_ref, sum_ref, total_ref, *refs):
    outs, hold = (refs[:-1], refs[-1]) if parted else ((), refs[0])
    place = seat() if parted else 0
    _, half, width = hold.shape
    for k, x_ref in enumerate((own_ref, mate_ref, far_ref, cross_ref)):
        real = x_ref.shape[1]
        mean = sum_ref[4 + k : 5 + k, :real]
        part = (dot_tn(x_ref[...], g_ref[...]) - outer(mean, total_ref[7:8, :])).astype(BF16)
        hold[(2 * k) ^ place] = part[:half]
        rest = part[half:]
        hold[(2 * k + 1) ^ place, : rest.shape[0], :] = rest
        if not parted:
            hold[2 * k + 1, rest.shape[0] :, :] = jnp.zeros((half - rest.shape[0], width), BF16)
    if parted:
        left, right = slice(0, half), slice(half, width)
        for out, shares, at in zip(
            outs, ((0, 1, 2, 3), (4, 5, 6, 7), (0, 1, 4, 5), (2, 3, 6, 7)), (left, left, right, right)
        ):
            for i, r in enumerate(shares):
                out[i] = hold[r, :, at]


def halve_kernel(left_ref, got_left_ref, right_ref, got_right_ref, *outs):
    for n, (keep, got) in enumerate(((left_ref, got_left_ref), (right_ref, got_right_ref))):
        mine, give = outs[2 * n : 2 * n + 2]
        for i in range(2):
            mine[i] = wide_sum(keep[i], got[i])
            give[i] = half_sum(keep[i + 2], got[i + 2])


def settle_kernel(
    length,
    left_ref,
    got_left_ref,
    right_ref,
    got_right_ref,
    lean_left_ref,
    lean_got_left_ref,
    lean_right_ref,
    lean_got_right_ref,
    sums_ref,
    stats_ref,
    sum_ref,
    par_ref,
    *outs,
):
    peers = sums_ref.shape[0]
    total = total_of(sums_ref)
    base = total[0:1, :] * (1.0 / (peers * length))
    scale = par_ref[0:1, :] * sum_ref[2:3, :]
    lean = scale * total[1:2, :] * (1.0 / (peers * length))
    place, here = lax.axis_index("seq"), seat()
    half = left_ref.shape[1]
    for n, (keep, got, lean_keep, lean_got, other, shares, at) in enumerate((
        (left_ref, got_left_ref, lean_left_ref, lean_got_left_ref, place ^ LEVEL[4], (0, 1, 2, 3), slice(0, half)),
        (right_ref, got_right_ref, lean_right_ref, lean_got_right_ref, place ^ LEVEL[2], (0, 1, 4, 5), slice(half, 2 * half)),
    )):
        mine, give = outs[2 * n : 2 * n + 2]
        columns = [
            (scale * (sums_ref[p, 0:1, :] * (1.0 / length) - base) * length)[:, at] for p in (place, other)
        ]
        for i, r in enumerate(shares):
            share = here ^ r
            row, low = share >> 1, pl.multiple_of((share & 1) * half, 128)
            middle = sum_ref[pl.ds(4 + row, 1), pl.ds(low, half)]
            value = wide_sum(keep[i], got[i]) - lean[:, at] * wide_sum(lean_keep[i], lean_got[i])
            for p, column in zip((place, other), columns):
                value = value + outer(stats_ref[p, pl.ds(2 + row, 1), pl.ds(low, half)] - middle, column)
            if i < 2:
                mine[i] = value
            else:
                give[i - 2] = value.astype(BF16)


def quarter_kernel(left_ref, got_left_ref, right_ref, got_right_ref, mine_ref, give_ref):
    edge = left_ref.shape[2]
    for keep, got, at in (
        (left_ref, got_left_ref, slice(0, edge)),
        (right_ref, got_right_ref, slice(edge, 2 * edge)),
    ):
        mine_ref[:, at] = wide_sum(keep[0], got[0])
        give_ref[:, at] = half_sum(keep[1], got[1])


def spread_kernel(parted, *refs):
    if parted:
        shares, out_ref, hold = refs[:-2], refs[-2], refs[-1]
        for r, share in enumerate(shares):
            hold[r] = share[...]
    else:
        hold, out_ref = refs
    place, here = seat() if parted else 0, lax.axis_index("neur")
    half = hold.shape[1]
    block = out_ref.shape[0] // 4
    width = out_ref.shape[1]
    for b in range(4):
        for h in range(2):
            low, high = b * block + h * half, min(b * block + h * half + half, (b + 1) * block)
            which = (((here ^ b) * 2) + h) ^ place
            out_ref[low:high, :] = hold[which, : high - low, :width].astype(F32)


def wide_sum(a, b):
    return a.astype(F32) + b.astype(F32)


def half_sum(a, b):
    return wide_sum(a, b).astype(BF16)


def swap(x, bit, axis="seq"):
    n = lax.axis_size(axis)
    return lax.ppermute(x, axis, [(i, i ^ bit) for i in range(n)])


LEVEL = {4: 1, 2: 2, 1: 4}


def seat():
    place = lax.axis_index("seq")
    return ((place & 1) << 2) | (place & 2) | ((place >> 2) & 1)


def gather_first(v):
    return {0: v, 4: swap(v, LEVEL[4]), 2: swap(v, LEVEL[2]), 1: swap(v, LEVEL[1])}


def gather_rest(out):
    out = dict(out)
    out[2], out[4] = lax.optimization_barrier((out[2], out[4]))
    out[6] = swap(out[2], LEVEL[4])
    out[5] = swap(out[1], LEVEL[4])
    out[3] = swap(out[1], LEVEL[2])
    out[3], out[6] = lax.optimization_barrier((out[3], out[6]))
    out[7] = swap(out[3], LEVEL[4])
    return [out[r] for r in range(8)]


def per_device(devices_seq, *args):
    (
        tokens,
        w_first,
        gain_first,
        shift_first,
        decay_first,
        w_second,
        gain_second,
        shift_second,
        decay_second,
        cotangent,
        running_mean,
        running_var,
    ) = args
    _, length, real = tokens.shape
    width = -(-real // LANE) * LANE
    tiles = len(tiles_of(width))
    peers = devices_seq
    here = lax.axis_index("neur")
    tokens, cotangent = tokens[0], cotangent[0]

    scans = [
        pltpu.VMEM((tiles, length, LANE), F32),
        pltpu.VMEM((tiles, length + 8, LANE), F32),
    ]
    grads = [pltpu.VMEM((tiles, length, LANE), F32)]

    def share(stats):
        return lax.all_to_all(stats, "seq", 0, 0, tiled=True)

    def project(own, w, rows, *gives, aside=None):
        far = swap(own, 2, "neur")
        mate = swap(own, 1, "neur")
        w = lax.optimization_barrier((w, own))[0]
        w4, give, par = call(
            block_kernel,
            [shape(4, width, width, dtype=BF16), shape(2, width, width, dtype=BF16), shape(8, width)],
        )(w, *(row[None] for row in rows))
        part, means = call(project_early, [shape(length, width), shape(8, width)])(own, mate, w4)
        gives = [swap(lax.optimization_barrier((g, own))[0], 1, "neur") for g in gives + (give,)] if gives else give
        extra = aside(mate) if aside else ()
        far, part, par, gives, extra = lax.optimization_barrier((far, part, par, gives, extra))
        cross = swap(far, 1, "neur")
        proj, stats = call(project_late, [shape(length, width), shape(peers, 8, width)])(
            part, means, far, cross, w4
        )
        return (own, mate, far, cross), proj, share(stats), w4, gives, par, extra

    def gradient(sums, gb, proj, summary, par):
        return call(grad_kernel, [shape(length, width, dtype=BF16), shape(8, width)])(
            sums, gb, proj, summary, par
        )

    def send(g, mate, w4, wm):
        out = call(send_kernel, shape(length, width, dtype=BF16))(g, mate, w4, wm)
        out, g, mate = lax.optimization_barrier((out, g, mate))
        got = swap(out, 2, "neur")
        keep = call(keep_kernel, shape(length, width))(g, mate, w4, wm)
        return keep, got

    half = width // 2

    def parts_shape(*lead):
        return shape(*lead, half, width, dtype=BF16)

    def weight_parts(*operands):
        if peers != 8:
            return call(functools.partial(weight_kernel, False), parts_shape(8))(*operands)
        return call(
            functools.partial(weight_kernel, True),
            [shape(4, half, half, dtype=BF16)] * 4,
            [pltpu.VMEM((8, half, width), BF16)],
        )(*operands)

    def weights(shares):
        if peers != 8:
            return call(functools.partial(spread_kernel, False), shape(4 * real, real))(shares)
        return call(
            functools.partial(spread_kernel, True),
            shape(4 * real, real),
            [pltpu.VMEM((8, half, width), BF16)],
        )(*shares)

    def together(*values):
        return lax.optimization_barrier(values)

    first_x, first_proj, first_stats, first_w, give, first_par, _ = project(
        tokens, w_first, (gain_first, shift_first, decay_first)
    )
    first_out, first_wide, first_sum, first_norm, norm_total = call(
        forward_kernel,
        [
            shape(length, real, dtype=BF16),
            shape(length, width),
            shape(8, width),
            shape(length, width, dtype=BF16),
            shape(8, width),
        ],
        scans,
    )(first_stats, first_proj, first_par)

    def after(x, *earlier):
        return lax.optimization_barrier((x, earlier))[0]

    def leaning(mate):
        if peers != 8:
            return ()
        norm = after(first_norm, mate)
        left, give_left, right, give_right = weight_parts(*first_x, norm, first_sum, norm_total)
        return left, swap(give_left, LEVEL[4]), right, swap(give_right, LEVEL[2])

    second_x, second_proj, second_stats, second_w, (first_mate, second_mate), second_par, lean = project(
        first_out, w_second, (gain_second, shift_second, decay_second), give, aside=leaning
    )
    second_out, second_gb, second_sums, second_sum, new_mean, new_var = call(
        turn_kernel,
        [
            shape(length, real, dtype=BF16),
            shape(length, width),
            shape(peers, 8, width),
            shape(8, width),
            shape(2, real),
            shape(2, real),
        ],
        scans
        + grads
        + [
            pltpu.VMEM((length, real), BF16),
            pltpu.VMEM((2, real), F32),
            pltpu.VMEM((2, real), F32),
            pltpu.SemaphoreType.DMA((3,)),
        ],
        in_specs=[pl.BlockSpec(memory_space=pltpu.VMEM)] * 4 + [pl.BlockSpec(memory_space=pl.ANY)] * 3,
    )(second_stats, second_proj, second_par, first_sum, cotangent, running_mean, running_var)

    second_sums = share(second_sums)
    second_g, second_total = gradient(second_sums, second_gb, second_proj, second_sum, second_par)
    mate = swap(second_g, 1, "neur")
    pairs = [shape(2, half, half), shape(2, half, half, dtype=BF16)] * 2
    rest = [shape(half, width), parts_shape()]
    second_parts = weight_parts(*second_x, second_g, second_sum, second_total)
    mate, second_parts = together(mate, second_parts)
    keep, got = send(second_g, mate, second_w, second_mate)
    if peers == 8:
        left, give_left, right, give_right = second_parts
        parcel = after((swap(give_left, LEVEL[4]), swap(give_right, LEVEL[2])), keep)
        left, give_left, right, give_right = call(halve_kernel, pairs)(left, parcel[0], right, parcel[1])
        keep, got, left = together(keep, got, left)
        parcel = swap(give_left, LEVEL[2]), swap(give_right, LEVEL[4])
    first_gb, first_sums, first_own = call(
        back_kernel,
        [shape(length, width), shape(peers, 8, width), shape(length, width, dtype=BF16)],
        scans + grads,
    )(keep, got, first_proj, first_wide, first_sum, first_par)
    if peers == 8:
        second_mine, give = call(quarter_kernel, rest)(left, parcel[0], right, parcel[1])
        first_sums, second_mine, give = together(first_sums, second_mine, give)
        left, give_left, right, give_right = weight_parts(
            *first_x, first_own, first_sum, jnp.zeros((8, width), F32)
        )
        parcel = swap(give_left, LEVEL[4]), swap(give_right, LEVEL[2])
    first_sums = share(first_sums)
    if peers == 8:
        first_sums, last, parcel = together(first_sums, swap(give, LEVEL[1]), parcel)
    first_g, first_total = gradient(first_sums, first_gb, first_proj, first_sum, first_par)
    mate = swap(first_g, 1, "neur")
    if peers == 8:
        left, give_left, right, give_right = call(functools.partial(settle_kernel, length), pairs)(
            left, parcel[0], right, parcel[1], *lean, first_sums, first_stats, first_sum, first_par
        )
        parcel = swap(give_left, LEVEL[2]), swap(give_right, LEVEL[4])
        mate, left = together(mate, left)
        keep, got = send(first_g, mate, first_w, first_mate)
        second_share = gather_first(half_sum(second_mine, last))
        mine, give = call(quarter_kernel, rest)(left, parcel[0], right, parcel[1])
        keep, first_share = together(keep, half_sum(mine, swap(give, LEVEL[1])))
        second_share = gather_rest(second_share)
        first_share = gather_rest(gather_first(first_share))
    else:
        first_parts = weight_parts(*first_x, first_g, first_sum, first_total)
        keep, got = send(first_g, mate, first_w, first_mate)
        second_share, first_share = lax.psum((second_parts, first_parts), "seq")
    grad_w_first = weights(first_share)
    grad_w_second = weights(second_share)
    input_grad = (keep + got.astype(F32))[:, :real]

    def pair(row):
        return jnp.stack([first_total[row, :real], second_total[row, :real]])

    return (
        first_out[None],
        second_out[None],
        input_grad[None],
        grad_w_first,
        grad_w_second,
        pair(1),
        pair(0),
        pair(2),
        new_mean,
        new_var,
    )


def solution(mesh):
    rows, line, flat = P("seq", None, "neur"), P("neur"), P(None, "neur")
    return jax.shard_map(
        functools.partial(per_device, mesh.shape["seq"]),
        mesh=mesh,
        in_specs=(rows, flat, line, line, line, flat, line, line, line, rows, flat, flat),
        out_specs=(rows, rows, rows) + (flat,) * 7,
        check_vma=False,
    )
```

```python
import functools
import math

import jax
import jax.numpy as jnp
from jax import lax
from jax.experimental import pallas as pl
from jax.experimental.pallas import tpu as pltpu
from jax.sharding import PartitionSpec as P

EPSILON = 1e-05
MOMENTUM = 0.1
LANE = 128
CHUNKS = 32
GROUPS = CHUNKS // 8
TOLERANCE = 1e-5
LOG2E = math.log2(math.e)
LN2 = math.log(2.0)
F32 = jnp.float32
BF16 = jnp.bfloat16
VMEM_BYTES = 16 * 1024 * 1024


def call(kernel, outs, scratch=(), **specs):
    return pl.pallas_call(
        kernel,
        **specs,
        out_shape=outs,
        scratch_shapes=list(scratch),
        compiler_params=pltpu.CompilerParams(vmem_limit_bytes=VMEM_BYTES),
    )


def shape(*dims, dtype=F32):
    return jax.ShapeDtypeStruct(dims, dtype)


def tiles_of(width):
    return [(j, j * LANE, min(LANE, width - j * LANE)) for j in range(-(-width // LANE))]


def dot(a, b):
    return jnp.dot(a, b, preferred_element_type=F32)


def dot_nt(a, b):
    return lax.dot_general(a, b, (((1,), (1,)), ((), ())), preferred_element_type=F32)


def block_kernel(w_ref, gain_ref, shift_ref, decay_ref, out_ref, mate_ref, par_ref):
    here = lax.axis_index("neur")
    blocks, width, _ = out_ref.shape
    real = w_ref.shape[0] // blocks
    out_ref[...] = jnp.zeros(out_ref.shape, BF16)
    for b in range(blocks):
        out_ref[b, :real, : w_ref.shape[1]] = w_ref[b * real : (b + 1) * real, :]
    for i, k in enumerate((1, 3)):
        mate_ref[i] = out_ref[here ^ k]
    par_ref[...] = jnp.zeros(par_ref.shape, F32)
    for i, row_ref in enumerate((gain_ref, shift_ref, decay_ref)):
        par_ref[i : i + 1, : row_ref.shape[1]] = row_ref[...]


def means_of(x_ref):
    length = x_ref.shape[0]
    return dot(jnp.ones((16, length), BF16), x_ref[...])[:1] * (1.0 / length)


def project_early(own_ref, mate_ref, w_ref, part_ref, means_ref):
    here = lax.axis_index("neur")
    k = own_ref.shape[1]
    means_ref[...] = jnp.zeros(means_ref.shape, F32)
    means_ref[0:1, :k] = means_of(own_ref)
    means_ref[1:2, :k] = means_of(mate_ref)
    for c in range(0, part_ref.shape[1], 256):
        part_ref[:, c : c + 256] = dot(own_ref[...], w_ref[here, :k, c : c + 256]) + dot(
            mate_ref[...], w_ref[here ^ 1, :k, c : c + 256]
        )


def project_middle(part_ref, means_ref, far_ref, w_ref, out_ref, out_means_ref):
    here = lax.axis_index("neur")
    k = far_ref.shape[1]
    out_means_ref[...] = means_ref[...]
    out_means_ref[2:3, :k] = means_of(far_ref)
    for c in range(0, part_ref.shape[1], 256):
        out_ref[:, c : c + 256] = part_ref[:, c : c + 256] + dot(
            far_ref[...], w_ref[here ^ 2, :k, c : c + 256]
        )


def project_late(part_ref, means_ref, cross_ref, w_ref, proj_ref, stats_ref):
    here = lax.axis_index("neur")
    k = cross_ref.shape[1]
    peers, _, width = stats_ref.shape
    cross = means_of(cross_ref)
    for p in range(peers):
        stats_ref[p, 2:8, :] = means_ref[0:6, :]
        stats_ref[p, 5:6, :k] = cross
    length = proj_ref.shape[0]
    for c in range(0, part_ref.shape[1], 256):
        y = part_ref[:, c : c + 256] + dot(cross_ref[...], w_ref[here ^ 3, :k, c : c + 256])
        proj_ref[:, c : c + 256] = y
        mean = jnp.sum(y, axis=0, keepdims=True) * (1.0 / length)
        off = y - mean
        spread = jnp.sum(off * off, axis=0, keepdims=True)
        for p in range(stats_ref.shape[0]):
            stats_ref[p, 0:1, c : c + 256] = mean
            stats_ref[p, 1:2, c : c + 256] = spread


def merged(stats_ref, length, sum_ref):
    peers = stats_ref.shape[0]
    means = [stats_ref[p, 0:1, :] for p in range(peers)]
    mean = sum(means[1:], means[0]) * (1.0 / peers)
    total = None
    for p in range(peers):
        off = means[p] - mean
        term = stats_ref[p, 1:2, :] + off * off * float(length)
        total = term if total is None else total + term
    var = total * (1.0 / (peers * length))
    inverse = lax.rsqrt(var + EPSILON)
    features = stats_ref[0, 2:6, :]
    for p in range(1, peers):
        features = features + stats_ref[p, 2:6, :]
    sum_ref[0:1, :] = mean
    sum_ref[1:2, :] = var
    sum_ref[2:3, :] = inverse
    sum_ref[3:4, :] = stats_ref[lax.axis_index("seq"), 0:1, :]
    sum_ref[4:8, :] = features * (1.0 / peers)
    return mean, var, inverse


def spread_rows(row, tiles):
    return [jnp.broadcast_to(row[:, c : c + LANE], (8, LANE)) for _, c, _ in tiles]


def load_step(ref, step, tiles, lead=0):
    steps = (ref.shape[1] - lead) // CHUNKS
    return [
        ref[j, pl.ds(lead + step + g * 8 * steps, 8, stride=steps), :]
        for j, _, _ in tiles
        for g in range(GROUPS)
    ]


def store_step(ref, step, tiles, values, lead=0):
    steps = (ref.shape[1] - lead) // CHUNKS
    i = 0
    for j, _, _ in tiles:
        for g in range(GROUPS):
            ref[j, pl.ds(lead + step + g * 8 * steps, 8, stride=steps), :] = values[i]
            i += 1


def rows_before(x, k, fill):
    at = lax.broadcasted_iota(jnp.int32, x.shape, 0)
    return jnp.where(at >= k, pltpu.roll(x, k, axis=0), fill)


def rows_after(x, k, fill):
    at = lax.broadcasted_iota(jnp.int32, x.shape, 0)
    return jnp.where(at < 8 - k, pltpu.roll(x, 8 - k, axis=0), fill)


def whole_row(x, i):
    return jnp.broadcast_to(x[i : i + 1, :], x.shape)


def chain(base, slope, floor=None, back=False):
    shifted, last, first = (rows_after, 0, 7) if back else (rows_before, 7, 0)
    starts = [None] * GROUPS
    carry = jnp.zeros((8, LANE), F32)
    for g in reversed(range(GROUPS)) if back else range(GROUPS):
        b, q, f = base[g], slope[g], None if floor is None else floor[g]
        for k in (1, 2, 4):
            early = shifted(b, k, 0.0)
            if f is not None:
                f = jnp.maximum(f, b + q * shifted(f, k, 0.0))
            b = b + q * early
            q = q * shifted(q, k, 1.0)
        ends = b + q * carry
        if f is not None:
            ends = jnp.maximum(ends, f)
        starts[g] = jnp.where(
            lax.broadcasted_iota(jnp.int32, ends.shape, 0) == first, carry, shifted(ends, 1, 0.0)
        )
        carry = whole_row(ends, last)
    return starts


def by_tile(tiles, run, *lists):
    out = []
    for n in range(len(tiles)):
        out += run(*(x[n * GROUPS : (n + 1) * GROUPS] for x in lists))
    return out


def handed_on(ends):
    out, carry = [], jnp.zeros((8, LANE), F32)
    for x in ends:
        out.append(jnp.where(lax.broadcasted_iota(jnp.int32, x.shape, 0) == 0, carry, rows_before(x, 1, 0.0)))
        carry = whole_row(x, 7)
    return out


def power(x, n):
    out = None
    while n:
        if n & 1:
            out = x if out is None else out * x
        x = x * x
        n >>= 1
    return out


def softplus2(before):
    return [jnp.where(b > 25.0, b * LN2, jnp.log(1.0 + jnp.exp2(b))) for b in before]


def run_bounds(drive_ref, decay, tiles, steps):
    u = [d for d in decay for _ in range(GROUPS)]
    u2 = [d * LOG2E for d in u]

    def body(step, carry):
        state, line = carry
        drive = load_step(drive_ref, step, tiles)
        line = [d + a * v for d, a, v in zip(drive, u, line)]
        state = softplus2([d + a * v for d, a, v in zip(drive, u2, state)])
        return state, line

    zero = [jnp.zeros((8, LANE), F32) for _ in u]
    state, line = lax.fori_loop(0, steps, body, (zero, zero), unroll=11)
    return state, [a * LN2 for a in line]


def run_chunks(drive_ref, state_ref, start, decay, tiles, steps):
    u2 = [d * LOG2E for d in decay for _ in range(GROUPS)]

    def body(step, carry):
        state, slope = carry
        drive = load_step(drive_ref, step, tiles)
        before = [d + u * s for d, u, s in zip(drive, u2, state)]
        state = softplus2(before)
        slope = [a + (b - s * LOG2E) for a, b, s in zip(slope, before, state)]
        store_step(state_ref, step, tiles, state, lead=8)
        return state, slope

    zero = [jnp.zeros((8, LANE), F32) for _ in start]
    state, slope = lax.fori_loop(0, steps, body, (start, zero), unroll=True)
    top = [power(d, steps) for d in decay for _ in range(GROUPS)]
    return state, [t * jnp.exp2(a) for t, a in zip(top, slope)]


def solve(drive_ref, state_ref, decay_row, tiles):
    steps = drive_ref.shape[1] // CHUNKS
    decay = spread_rows(decay_row, tiles)
    top = [power(d, steps) for d in decay for _ in range(GROUPS)]
    low, line = run_bounds(drive_ref, decay, tiles, steps)
    start = by_tile(tiles, lambda f, b, q: chain(b, q, f), low, line, top)

    def again(carry):
        count, worst, _ = carry
        return jnp.logical_and(worst > 0.0, count < CHUNKS + 1)

    def newton(carry):
        count, _, start = carry
        end, slope = run_chunks(drive_ref, state_ref, start, decay, tiles, steps)
        miss = [e - s for e, s in zip(by_tile(tiles, handed_on, end), start)]
        worst = None
        for m, s in zip(miss, start):
            over = jnp.abs(m) - TOLERANCE * jnp.maximum(s, 1.0)
            worst = over if worst is None else jnp.maximum(worst, over)

        def step(miss, slope, start):
            after = [
                jnp.where(
                    lax.broadcasted_iota(jnp.int32, m.shape, 0) == 7,
                    whole_row(miss[g + 1], 0) if g + 1 < GROUPS else 0.0,
                    rows_after(m, 1, 0.0),
                )
                for g, m in enumerate(miss)
            ]
            return [s + c for s, c in zip(start, chain(after, slope))]

        return count + 1, jnp.max(worst), by_tile(tiles, step, miss, slope, start)

    lax.while_loop(again, newton, (jnp.int32(0), jnp.float32(1.0), start))


def run_back(grad_ref, sigma_ref, start, decay, tiles, steps, store):
    u = [d for d in decay for _ in range(GROUPS)]

    def body(i, carry):
        z, prod = carry
        step = steps - 1 - i
        gs = load_step(grad_ref, step, tiles)
        sig = load_step(sigma_ref, step, tiles)
        z = [s * (g + a * v) for s, g, a, v in zip(sig, gs, u, z)]
        if store:
            store_step(grad_ref, step, tiles, z)
            return z, prod
        return z, [p * (s * a) for p, s, a in zip(prod, sig, u)]

    ones = [] if store else [jnp.ones((8, LANE), F32) for _ in start]
    return lax.fori_loop(0, steps, body, (start, ones), unroll=11)


def solve_back(grad_ref, sigma_ref, decay_row, tiles):
    steps = grad_ref.shape[1] // CHUNKS
    decay = spread_rows(decay_row, tiles)
    zero = [jnp.zeros((8, LANE), F32)] * (len(tiles) * GROUPS)
    end, slope = run_back(grad_ref, sigma_ref, zero, decay, tiles, steps, False)
    start = by_tile(tiles, lambda b, q: chain(b, q, back=True), end, slope)
    run_back(grad_ref, sigma_ref, start, decay, tiles, steps, True)


BLOCK = 88


def row_blocks(length, body):
    @pl.loop(0, length // BLOCK)
    def _(i):
        body(pl.ds(pl.multiple_of(i * BLOCK, 8), BLOCK))


def fill_drive(proj_ref, drive_ref, mean, inverse, gain, shift, tiles):
    scale = inverse * gain * LOG2E
    offset = shift * LOG2E

    def body(rows):
        for j, c, _ in tiles:
            at = slice(c, c + LANE)
            drive_ref[j, rows, :] = (proj_ref[rows, at] - mean[:, at]) * scale[:, at] + offset[:, at]

    row_blocks(proj_ref.shape[0], body)


def fill_sigma(drive_ref, prev_ref, decay_row, tiles, length):
    u2 = decay_row * LOG2E

    def body(i, _):
        for j, c, _w in tiles:
            rows = pl.ds(pl.multiple_of(i * BLOCK, 8), BLOCK)
            before = drive_ref[j, rows, :] + u2[:, c : c + LANE] * prev_ref[j, pl.ds(i * BLOCK + 7, BLOCK), :]
            drive_ref[j, rows, :] = 1.0 / (1.0 + jnp.exp2(-before))
        return 0

    lax.fori_loop(0, length // BLOCK, body, 0)


def finish_back(grad_ref, state_ref, proj_ref, mean, inverse, tiles, gb_ref, sums_ref):
    length, width = proj_ref.shape
    zero = tuple(jnp.zeros((1, LANE), F32) for _ in tiles)

    def body(i, carry):
        shift, gain, decay = (list(x) for x in carry)
        rows = pl.ds(pl.multiple_of(i * BLOCK, 8), BLOCK)
        for j, c, _w in tiles:
            at = slice(c, c + LANE)
            gb = grad_ref[j, rows, :]
            gb_ref[rows, at] = gb
            shift[j] = shift[j] + jnp.sum(gb, axis=0, keepdims=True)
            gain[j] = gain[j] + jnp.sum(gb * (proj_ref[rows, at] - mean[:, at]), axis=0, keepdims=True)
            decay[j] = decay[j] + jnp.sum(
                gb * state_ref[j, pl.ds(i * BLOCK + 7, BLOCK), :], axis=0, keepdims=True
            )
        return tuple(shift), tuple(gain), tuple(decay)

    shift, gain, decay = lax.fori_loop(0, length // BLOCK, body, (zero, zero, zero))
    for j, c, _ in tiles:
        at = slice(c, c + LANE)
        scaled = gain[j] * inverse[:, at]
        for p in range(sums_ref.shape[0]):
            sums_ref[p, 0:1, at] = shift[j]
            sums_ref[p, 1:2, at] = scaled
            sums_ref[p, 2:3, at] = decay[j]


def clear(state_ref, tiles):
    for j, _, _ in tiles:
        state_ref[j, 0:8, :] = jnp.zeros((8, LANE), F32)


def put_states(state_ref, out_ref, tiles, wide_ref=None):
    def body(i, _):
        rows = pl.ds(pl.multiple_of(i * 16, 16), 16)
        for j, c, w in tiles:
            s = state_ref[j, pl.ds(pl.multiple_of(8 + i * 16, 8), 16), :]
            out_ref[rows, c : c + w] = s[:, :w].astype(BF16)
            if wide_ref is not None:
                wide_ref[rows, c : c + LANE] = s
        return 0

    lax.fori_loop(0, out_ref.shape[0] // 16, body, 0, unroll=4)


def forward_kernel(stats_ref, proj_ref, par_ref, out_ref, wide_ref, sum_ref, drive, state):
    length, width = proj_ref.shape
    tiles = tiles_of(width)
    outs = tiles_of(out_ref.shape[1])
    mean, var, inverse = merged(stats_ref, length, sum_ref)
    gain, shift, decay = par_ref[0:1, :], par_ref[1:2, :], par_ref[2:3, :]
    fill_drive(proj_ref, drive, mean, inverse, gain, shift, tiles)
    clear(state, tiles)
    solve(drive, state, decay, tiles)
    put_states(state, out_ref, outs, wide_ref)


def norm_kernel(proj_ref, sum_ref, norm_ref, total_ref):
    length = proj_ref.shape[0]
    mean, inverse = sum_ref[0:1, :], sum_ref[2:3, :]
    total_ref[...] = jnp.zeros(total_ref.shape, F32)
    total_ref[7:8, :] = length * (sum_ref[3:4, :] - mean) * inverse

    def body(i, _):
        rows = pl.ds(pl.multiple_of(i * 16, 16), 16)
        norm_ref[rows, :] = ((proj_ref[rows, :] - mean) * inverse).astype(BF16)
        return 0

    lax.fori_loop(0, length // 16, body, 0, unroll=4)


def turn_kernel(
    stats_ref,
    proj_ref,
    par_ref,
    first_ref,
    cot_hbm,
    rmean_hbm,
    rvar_hbm,
    out_ref,
    gb_ref,
    sums_ref,
    sum_ref,
    nmean_ref,
    nvar_ref,
    drive,
    state,
    grad,
    cot_ref,
    rmean_ref,
    rvar_ref,
    arrived,
):
    copies = [
        pltpu.make_async_copy(a, b, arrived.at[i])
        for i, (a, b) in enumerate(
            ((cot_hbm, cot_ref), (rmean_hbm, rmean_ref), (rvar_hbm, rvar_ref))
        )
    ]
    for copy in copies:
        copy.start()
    length, width = proj_ref.shape
    tiles = tiles_of(width)
    outs = tiles_of(out_ref.shape[1])
    mean, var, inverse = merged(stats_ref, length, sum_ref)
    gain, shift, decay = par_ref[0:1, :], par_ref[1:2, :], par_ref[2:3, :]
    real = out_ref.shape[1]
    count = float(stats_ref.shape[0] * length)
    fill_drive(proj_ref, drive, mean, inverse, gain, shift, tiles)
    clear(state, tiles)
    solve(drive, state, decay, tiles)
    put_states(state, out_ref, outs)
    fill_sigma(drive, state, decay, tiles, length)
    for copy in copies:
        copy.wait()
    for row, m, v in ((0, first_ref[0:1, :], first_ref[1:2, :]), (1, mean, var)):
        nmean_ref[row : row + 1, :] = (1.0 - MOMENTUM) * rmean_ref[row : row + 1, :] + MOMENTUM * m[:, :real]
        nvar_ref[row : row + 1, :] = (1.0 - MOMENTUM) * rvar_ref[row : row + 1, :] + (
            MOMENTUM * v[:, :real]
        ) * (count / (count - 1.0))
    for j, _, w in outs:
        if w < LANE:
            grad[j] = jnp.zeros(grad.shape[1:], F32)

    def load_cot(i, _):
        rows = pl.ds(pl.multiple_of(i * 16, 16), 16)
        for j, c, w in outs:
            grad[j, rows, :w] = cot_ref[rows, c : c + w].astype(F32)
        return 0

    lax.fori_loop(0, length // 16, load_cot, 0, unroll=4)
    solve_back(grad, drive, decay, tiles)
    finish_back(grad, state, proj_ref, mean, inverse, tiles, gb_ref, sums_ref)


def back_kernel(
    keep_ref, got_ref, proj_ref, wide_ref, sum_ref, par_ref, gb_ref, sums_ref, own_ref, drive, state, grad
):
    length, width = proj_ref.shape
    tiles = tiles_of(width)
    mean, inverse = sum_ref[0:1, :], sum_ref[2:3, :]
    gain, shift, decay = par_ref[0:1, :], par_ref[1:2, :], par_ref[2:3, :]
    fill_drive(proj_ref, drive, mean, inverse, gain, shift, tiles)
    clear(state, tiles)

    def load(i, _):
        rows = pl.ds(pl.multiple_of(i * 16, 16), 16)
        for j, c, _w in tiles:
            at = slice(c, c + LANE)
            grad[j, rows, :] = keep_ref[rows, at] + got_ref[rows, at].astype(F32)
            state[j, pl.ds(pl.multiple_of(8 + i * 16, 8), 16), :] = wide_ref[rows, at]
        return 0

    lax.fori_loop(0, length // 16, load, 0, unroll=4)
    fill_sigma(drive, state, decay, tiles, length)
    solve_back(grad, drive, decay, tiles)
    finish_back(grad, state, proj_ref, mean, inverse, tiles, gb_ref, sums_ref)
    scale = gain * inverse
    average = sums_ref[0, 0:1, :] * (1.0 / length)

    def put_own(i, _):
        rows = pl.ds(pl.multiple_of(i * 16, 16), 16)
        own_ref[rows, :] = (scale * (gb_ref[rows, :] - average)).astype(BF16)
        return 0

    lax.fori_loop(0, length // 16, put_own, 0, unroll=4)


def total_of(sums_ref):
    peers = sums_ref.shape[0]
    out = sums_ref[0]
    for p in range(1, peers):
        out = out + sums_ref[p]
    return out


def grad_kernel(sums_ref, gb_ref, proj_ref, sum_ref, par_ref, g_ref, total_ref):
    length, _ = proj_ref.shape
    total = total_of(sums_ref)
    total_ref[...] = total
    count = float(sums_ref.shape[0] * length)
    mean, inverse = sum_ref[0:1, :], sum_ref[2:3, :]
    scale = par_ref[0:1, :] * inverse
    base = total[0:1, :] * (1.0 / count)
    lean = total[1:2, :] * (1.0 / count) * inverse

    total_ref[7:8, :] = scale * (
        sums_ref[lax.axis_index("seq"), 0:1, :]
        - length * base
        - length * (sum_ref[3:4, :] - mean) * lean
    )

    def body(i, _):
        rows = pl.ds(pl.multiple_of(i * 16, 16), 16)
        g_ref[rows, :] = (
            scale * (gb_ref[rows, :] - base - (proj_ref[rows, :] - mean) * lean)
        ).astype(BF16)
        return 0

    lax.fori_loop(0, length // 16, body, 0, unroll=4)


def send_kernel(g_ref, mate_ref, w_ref, wmate_ref, out_ref):
    here = lax.axis_index("neur")
    for c in range(0, out_ref.shape[1], 256):
        at = slice(c, c + 256)
        out_ref[:, at] = (
            dot_nt(g_ref[...], w_ref[here ^ 2, at, :]) + dot_nt(mate_ref[...], wmate_ref[1, at, :])
        ).astype(BF16)


def keep_kernel(g_ref, mate_ref, w_ref, wmate_ref, out_ref):
    here = lax.axis_index("neur")
    for c in range(0, out_ref.shape[1], 256):
        at = slice(c, c + 256)
        out_ref[:, at] = dot_nt(g_ref[...], w_ref[here, at, :]) + dot_nt(
            mate_ref[...], wmate_ref[0, at, :]
        )


def split(row):
    high = row.astype(BF16)
    return high, (row - high.astype(F32)).astype(BF16)


def dot_tn(a, b):
    return lax.dot_general(a, b, (((0,), (0,)), ((), ())), preferred_element_type=F32)


def outer(a, b):
    (a_high, a_low), (b_high, b_low) = split(a), split(b)
    return dot_tn(
        jnp.concatenate([a_high, a_high, a_low, a_low]), jnp.concatenate([b_high, b_low, b_high, b_low])
    )


def weight_kernel(parted, own_ref, mate_ref, far_ref, cross_ref, g_ref, sum_ref, total_ref, *refs):
    outs, hold = (refs[:-1], refs[-1]) if parted else ((), refs[0])
    place = seat() if parted else 0
    _, half, width = hold.shape
    for k, x_ref in enumerate((own_ref, mate_ref, far_ref, cross_ref)):
        real = x_ref.shape[1]
        mean = sum_ref[4 + k : 5 + k, :real]
        part = (dot_tn(x_ref[...], g_ref[...]) - outer(mean, total_ref[7:8, :])).astype(BF16)
        hold[(2 * k) ^ place] = part[:half]
        rest = part[half:]
        hold[(2 * k + 1) ^ place, : rest.shape[0], :] = rest
        if not parted:
            hold[2 * k + 1, rest.shape[0] :, :] = jnp.zeros((half - rest.shape[0], width), BF16)
    if parted:
        left, right = slice(0, half), slice(half, width)
        for out, shares, at in zip(
            outs, ((0, 1, 2, 3), (4, 5, 6, 7), (0, 1, 4, 5), (2, 3, 6, 7)), (left, left, right, right)
        ):
            for i, r in enumerate(shares):
                out[i] = hold[r, :, at]


def halve_kernel(left_ref, got_left_ref, right_ref, got_right_ref, *outs):
    for n, (keep, got) in enumerate(((left_ref, got_left_ref), (right_ref, got_right_ref))):
        mine, give = outs[2 * n : 2 * n + 2]
        for i in range(2):
            mine[i] = wide_sum(keep[i], got[i])
            give[i] = half_sum(keep[i + 2], got[i + 2])


def settle_kernel(
    length,
    left_ref,
    got_left_ref,
    right_ref,
    got_right_ref,
    lean_left_ref,
    lean_got_left_ref,
    lean_right_ref,
    lean_got_right_ref,
    sums_ref,
    stats_ref,
    sum_ref,
    par_ref,
    *outs,
):
    peers = sums_ref.shape[0]
    total = total_of(sums_ref)
    base = total[0:1, :] * (1.0 / (peers * length))
    scale = par_ref[0:1, :] * sum_ref[2:3, :]
    lean = scale * total[1:2, :] * (1.0 / (peers * length))
    place, here = lax.axis_index("seq"), seat()
    half = left_ref.shape[1]
    for n, (keep, got, lean_keep, lean_got, other, shares, at) in enumerate((
        (left_ref, got_left_ref, lean_left_ref, lean_got_left_ref, place ^ LEVEL[4], (0, 1, 2, 3), slice(0, half)),
        (right_ref, got_right_ref, lean_right_ref, lean_got_right_ref, place ^ LEVEL[2], (0, 1, 4, 5), slice(half, 2 * half)),
    )):
        mine, give = outs[2 * n : 2 * n + 2]
        columns = [
            (scale * (sums_ref[p, 0:1, :] * (1.0 / length) - base) * length)[:, at] for p in (place, other)
        ]
        for i, r in enumerate(shares):
            share = here ^ r
            row, low = share >> 1, pl.multiple_of((share & 1) * half, 128)
            middle = sum_ref[pl.ds(4 + row, 1), pl.ds(low, half)]
            value = wide_sum(keep[i], got[i]) - lean[:, at] * wide_sum(lean_keep[i], lean_got[i])
            for p, column in zip((place, other), columns):
                value = value + outer(stats_ref[p, pl.ds(2 + row, 1), pl.ds(low, half)] - middle, column)
            if i < 2:
                mine[i] = value
            else:
                give[i - 2] = value.astype(BF16)


def quarter_kernel(left_ref, got_left_ref, right_ref, got_right_ref, mine_ref, give_ref):
    edge = left_ref.shape[2]
    for keep, got, at in (
        (left_ref, got_left_ref, slice(0, edge)),
        (right_ref, got_right_ref, slice(edge, 2 * edge)),
    ):
        mine_ref[:, at] = wide_sum(keep[0], got[0])
        give_ref[:, at] = half_sum(keep[1], got[1])


def spread_kernel(parted, *refs):
    if parted:
        shares, out_ref, hold = refs[:-2], refs[-2], refs[-1]
        for r, share in enumerate(shares):
            hold[r] = share[...]
    else:
        hold, out_ref = refs
    place, here = seat() if parted else 0, lax.axis_index("neur")
    half = hold.shape[1]
    block = out_ref.shape[0] // 4
    width = out_ref.shape[1]
    for b in range(4):
        for h in range(2):
            low, high = b * block + h * half, min(b * block + h * half + half, (b + 1) * block)
            which = (((here ^ b) * 2) + h) ^ place
            out_ref[low:high, :] = hold[which, : high - low, :width].astype(F32)


def wide_sum(a, b):
    return a.astype(F32) + b.astype(F32)


def half_sum(a, b):
    return wide_sum(a, b).astype(BF16)


def swap(x, bit, axis="seq"):
    n = lax.axis_size(axis)
    return lax.ppermute(x, axis, [(i, i ^ bit) for i in range(n)])


LEVEL = {4: 1, 2: 2, 1: 4}


def seat():
    place = lax.axis_index("seq")
    return ((place & 1) << 2) | (place & 2) | ((place >> 2) & 1)


def gather_first(v):
    return {0: v, 4: swap(v, LEVEL[4]), 2: swap(v, LEVEL[2]), 1: swap(v, LEVEL[1])}


def gather_rest(out):
    out = dict(out)
    out[2], out[4] = lax.optimization_barrier((out[2], out[4]))
    out[6] = swap(out[2], LEVEL[4])
    out[5] = swap(out[1], LEVEL[4])
    out[3] = swap(out[1], LEVEL[2])
    out[3], out[6] = lax.optimization_barrier((out[3], out[6]))
    out[7] = swap(out[3], LEVEL[4])
    return [out[r] for r in range(8)]


def per_device(devices_seq, *args):
    (
        tokens,
        w_first,
        gain_first,
        shift_first,
        decay_first,
        w_second,
        gain_second,
        shift_second,
        decay_second,
        cotangent,
        running_mean,
        running_var,
    ) = args
    _, length, real = tokens.shape
    width = -(-real // LANE) * LANE
    tiles = len(tiles_of(width))
    peers = devices_seq
    here = lax.axis_index("neur")
    tokens, cotangent = tokens[0], cotangent[0]

    scans = [
        pltpu.VMEM((tiles, length, LANE), F32),
        pltpu.VMEM((tiles, length + 8, LANE), F32),
    ]
    grads = [pltpu.VMEM((tiles, length, LANE), F32)]

    def share(stats):
        return lax.all_to_all(stats, "seq", 0, 0, tiled=True)

    def project(own, w, rows, *gives, aside=None):
        far = swap(own, 2, "neur")
        mate = swap(own, 1, "neur")
        w = lax.optimization_barrier((w, own))[0]
        w4, give, par = call(
            block_kernel,
            [shape(4, width, width, dtype=BF16), shape(2, width, width, dtype=BF16), shape(8, width)],
        )(w, *(row[None] for row in rows))
        part, means = call(project_early, [shape(length, width), shape(8, width)])(own, mate, w4)
        gives = [swap(lax.optimization_barrier((g, own))[0], 1, "neur") for g in gives + (give,)] if gives else give
        extra = aside(mate) if aside else ()
        far, part, par, gives, extra = lax.optimization_barrier((far, part, par, gives, extra))
        cross = swap(far, 1, "neur")
        part, means = call(project_middle, [shape(length, width), shape(8, width)])(part, means, far, w4)
        proj, stats = call(project_late, [shape(length, width), shape(peers, 8, width)])(
            part, means, cross, w4
        )
        return (own, mate, far, cross), proj, share(stats), w4, gives, par, extra

    def gradient(sums, gb, proj, summary, par):
        return call(grad_kernel, [shape(length, width, dtype=BF16), shape(8, width)])(
            sums, gb, proj, summary, par
        )

    def send(g, mate, w4, wm):
        out = call(send_kernel, shape(length, width, dtype=BF16))(g, mate, w4, wm)
        out, g, mate = lax.optimization_barrier((out, g, mate))
        got = swap(out, 2, "neur")
        keep = call(keep_kernel, shape(length, width))(g, mate, w4, wm)
        return keep, got

    half = width // 2

    def parts_shape(*lead):
        return shape(*lead, half, width, dtype=BF16)

    def weight_parts(*operands):
        if peers != 8:
            return call(functools.partial(weight_kernel, False), parts_shape(8))(*operands)
        return call(
            functools.partial(weight_kernel, True),
            [shape(4, half, half, dtype=BF16)] * 4,
            [pltpu.VMEM((8, half, width), BF16)],
        )(*operands)

    def weights(shares):
        if peers != 8:
            return call(functools.partial(spread_kernel, False), shape(4 * real, real))(shares)
        return call(
            functools.partial(spread_kernel, True),
            shape(4 * real, real),
            [pltpu.VMEM((8, half, width), BF16)],
        )(*shares)

    def together(*values):
        return lax.optimization_barrier(values)

    first_x, first_proj, first_stats, first_w, give, first_par, _ = project(
        tokens, w_first, (gain_first, shift_first, decay_first)
    )
    first_out, first_wide, first_sum = call(
        forward_kernel,
        [shape(length, real, dtype=BF16), shape(length, width), shape(8, width)],
        scans,
    )(first_stats, first_proj, first_par)

    def after(x, *earlier):
        return lax.optimization_barrier((x, earlier))[0]

    def leaning(mate):
        if peers != 8:
            return ()
        norm, norm_total = call(norm_kernel, [shape(length, width, dtype=BF16), shape(8, width)])(
            first_proj, after(first_sum, mate)
        )
        left, give_left, right, give_right = weight_parts(*first_x, norm, first_sum, norm_total)
        return left, swap(give_left, LEVEL[4]), right, swap(give_right, LEVEL[2])

    second_x, second_proj, second_stats, second_w, (first_mate, second_mate), second_par, lean = project(
        first_out, w_second, (gain_second, shift_second, decay_second), give, aside=leaning
    )
    second_out, second_gb, second_sums, second_sum, new_mean, new_var = call(
        turn_kernel,
        [
            shape(length, real, dtype=BF16),
            shape(length, width),
            shape(peers, 8, width),
            shape(8, width),
            shape(2, real),
            shape(2, real),
        ],
        scans
        + grads
        + [
            pltpu.VMEM((length, real), BF16),
            pltpu.VMEM((2, real), F32),
            pltpu.VMEM((2, real), F32),
            pltpu.SemaphoreType.DMA((3,)),
        ],
        in_specs=[pl.BlockSpec(memory_space=pltpu.VMEM)] * 4 + [pl.BlockSpec(memory_space=pl.ANY)] * 3,
    )(second_stats, second_proj, second_par, first_sum, cotangent, running_mean, running_var)

    second_sums = share(second_sums)
    second_g, second_total = gradient(second_sums, second_gb, second_proj, second_sum, second_par)
    mate = swap(second_g, 1, "neur")
    pairs = [shape(2, half, half), shape(2, half, half, dtype=BF16)] * 2
    rest = [shape(half, width), parts_shape()]
    second_parts = weight_parts(*second_x, second_g, second_sum, second_total)
    mate, second_parts = together(mate, second_parts)
    keep, got = send(second_g, mate, second_w, second_mate)
    if peers == 8:
        left, give_left, right, give_right = second_parts
        parcel = after((swap(give_left, LEVEL[4]), swap(give_right, LEVEL[2])), keep)
        left, give_left, right, give_right = call(halve_kernel, pairs)(left, parcel[0], right, parcel[1])
        keep, got, left = together(keep, got, left)
        parcel = swap(give_left, LEVEL[2]), swap(give_right, LEVEL[4])
    first_gb, first_sums, first_own = call(
        back_kernel,
        [shape(length, width), shape(peers, 8, width), shape(length, width, dtype=BF16)],
        scans + grads,
    )(keep, got, first_proj, first_wide, first_sum, first_par)
    if peers == 8:
        second_mine, give = call(quarter_kernel, rest)(left, parcel[0], right, parcel[1])
        first_sums, second_mine, give = together(first_sums, second_mine, give)
        left, give_left, right, give_right = weight_parts(
            *first_x, first_own, first_sum, jnp.zeros((8, width), F32)
        )
        parcel = swap(give_left, LEVEL[4]), swap(give_right, LEVEL[2])
    first_sums = share(first_sums)
    if peers == 8:
        first_sums, last, parcel = together(first_sums, swap(give, LEVEL[1]), parcel)
    first_g, first_total = gradient(first_sums, first_gb, first_proj, first_sum, first_par)
    mate = swap(first_g, 1, "neur")
    if peers == 8:
        left, give_left, right, give_right = call(functools.partial(settle_kernel, length), pairs)(
            left, parcel[0], right, parcel[1], *lean, first_sums, first_stats, first_sum, first_par
        )
        parcel = swap(give_left, LEVEL[2]), swap(give_right, LEVEL[4])
        mate, left = together(mate, left)
        keep, got = send(first_g, mate, first_w, first_mate)
        second_share = gather_first(half_sum(second_mine, last))
        mine, give = call(quarter_kernel, rest)(left, parcel[0], right, parcel[1])
        keep, first_share = together(keep, half_sum(mine, swap(give, LEVEL[1])))
        second_share = gather_rest(second_share)
        first_share = gather_rest(gather_first(first_share))
    else:
        first_parts = weight_parts(*first_x, first_g, first_sum, first_total)
        keep, got = send(first_g, mate, first_w, first_mate)
        second_share, first_share = lax.psum((second_parts, first_parts), "seq")
    grad_w_first = weights(first_share)
    grad_w_second = weights(second_share)
    input_grad = (keep + got.astype(F32))[:, :real]

    def pair(row):
        return jnp.stack([first_total[row, :real], second_total[row, :real]])

    return (
        first_out[None],
        second_out[None],
        input_grad[None],
        grad_w_first,
        grad_w_second,
        pair(1),
        pair(0),
        pair(2),
        new_mean,
        new_var,
    )


def solution(mesh):
    rows, line, flat = P("seq", None, "neur"), P("neur"), P(None, "neur")
    return jax.shard_map(
        functools.partial(per_device, mesh.shape["seq"]),
        mesh=mesh,
        in_specs=(rows, flat, line, line, line, flat, line, line, line, rows, flat, flat),
        out_specs=(rows, rows, rows) + (flat,) * 7,
        check_vma=False,
    )
```

```python
import functools
import math

import jax
import jax.numpy as jnp
from jax import lax
from jax.experimental import pallas as pl
from jax.experimental.pallas import tpu as pltpu
from jax.sharding import PartitionSpec as P

EPSILON = 1e-05
MOMENTUM = 0.1
LANE = 128
CHUNKS = 32
GROUPS = CHUNKS // 8
TOLERANCE = 2e-5
LOG2E = math.log2(math.e)
LN2 = math.log(2.0)
F32 = jnp.float32
BF16 = jnp.bfloat16
VMEM_BYTES = 16 * 1024 * 1024


def call(kernel, outs, scratch=(), **specs):
    return pl.pallas_call(
        kernel,
        **specs,
        out_shape=outs,
        scratch_shapes=list(scratch),
        compiler_params=pltpu.CompilerParams(vmem_limit_bytes=VMEM_BYTES),
    )


def shape(*dims, dtype=F32):
    return jax.ShapeDtypeStruct(dims, dtype)


def tiles_of(width):
    return [(j, j * LANE, min(LANE, width - j * LANE)) for j in range(-(-width // LANE))]


def dot(a, b):
    return jnp.dot(a, b, preferred_element_type=F32)


def dot_nt(a, b):
    return lax.dot_general(a, b, (((1,), (1,)), ((), ())), preferred_element_type=F32)


def block_kernel(w_ref, gain_ref, shift_ref, decay_ref, out_ref, mate_ref, par_ref):
    here = lax.axis_index("neur")
    blocks, width, _ = out_ref.shape
    real = w_ref.shape[0] // blocks
    out_ref[...] = jnp.zeros(out_ref.shape, BF16)
    for b in range(blocks):
        out_ref[b, :real, : w_ref.shape[1]] = w_ref[b * real : (b + 1) * real, :]
    for i, k in enumerate((1, 3)):
        mate_ref[i] = out_ref[here ^ k]
    par_ref[...] = jnp.zeros(par_ref.shape, F32)
    for i, row_ref in enumerate((gain_ref, shift_ref, decay_ref)):
        par_ref[i : i + 1, : row_ref.shape[1]] = row_ref[...]


def means_of(x_ref):
    length = x_ref.shape[0]
    return dot(jnp.ones((16, length), BF16), x_ref[...])[:1] * (1.0 / length)


def project_early(own_ref, mate_ref, w_ref, part_ref, means_ref):
    here = lax.axis_index("neur")
    k = own_ref.shape[1]
    means_ref[...] = jnp.zeros(means_ref.shape, F32)
    means_ref[0:1, :k] = means_of(own_ref)
    means_ref[1:2, :k] = means_of(mate_ref)
    for c in range(0, part_ref.shape[1], 256):
        part_ref[:, c : c + 256] = dot(own_ref[...], w_ref[here, :k, c : c + 256]) + dot(
            mate_ref[...], w_ref[here ^ 1, :k, c : c + 256]
        )


def project_middle(part_ref, means_ref, far_ref, w_ref, out_ref, out_means_ref):
    here = lax.axis_index("neur")
    k = far_ref.shape[1]
    out_means_ref[...] = means_ref[...]
    out_means_ref[2:3, :k] = means_of(far_ref)
    for c in range(0, part_ref.shape[1], 256):
        out_ref[:, c : c + 256] = part_ref[:, c : c + 256] + dot(
            far_ref[...], w_ref[here ^ 2, :k, c : c + 256]
        )


def project_late(part_ref, means_ref, cross_ref, w_ref, proj_ref, stats_ref):
    here = lax.axis_index("neur")
    k = cross_ref.shape[1]
    peers, _, width = stats_ref.shape
    cross = means_of(cross_ref)
    for p in range(peers):
        stats_ref[p, 2:8, :] = means_ref[0:6, :]
        stats_ref[p, 5:6, :k] = cross
    length = proj_ref.shape[0]
    for c in range(0, part_ref.shape[1], 256):
        y = part_ref[:, c : c + 256] + dot(cross_ref[...], w_ref[here ^ 3, :k, c : c + 256])
        proj_ref[:, c : c + 256] = y
        mean = jnp.sum(y, axis=0, keepdims=True) * (1.0 / length)
        off = y - mean
        spread = jnp.sum(off * off, axis=0, keepdims=True)
        for p in range(stats_ref.shape[0]):
            stats_ref[p, 0:1, c : c + 256] = mean
            stats_ref[p, 1:2, c : c + 256] = spread


def merged(stats_ref, length, sum_ref):
    peers = stats_ref.shape[0]
    means = [stats_ref[p, 0:1, :] for p in range(peers)]
    mean = sum(means[1:], means[0]) * (1.0 / peers)
    total = None
    for p in range(peers):
        off = means[p] - mean
        term = stats_ref[p, 1:2, :] + off * off * float(length)
        total = term if total is None else total + term
    var = total * (1.0 / (peers * length))
    inverse = lax.rsqrt(var + EPSILON)
    features = stats_ref[0, 2:6, :]
    for p in range(1, peers):
        features = features + stats_ref[p, 2:6, :]
    sum_ref[0:1, :] = mean
    sum_ref[1:2, :] = var
    sum_ref[2:3, :] = inverse
    sum_ref[3:4, :] = stats_ref[lax.axis_index("seq"), 0:1, :]
    sum_ref[4:8, :] = features * (1.0 / peers)
    return mean, var, inverse


def spread_rows(row, tiles):
    return [jnp.broadcast_to(row[:, c : c + LANE], (8, LANE)) for _, c, _ in tiles]


def load_step(ref, step, tiles, lead=0):
    steps = (ref.shape[1] - lead) // CHUNKS
    return [
        ref[j, pl.ds(lead + step + g * 8 * steps, 8, stride=steps), :]
        for j, _, _ in tiles
        for g in range(GROUPS)
    ]


def store_step(ref, step, tiles, values, lead=0):
    steps = (ref.shape[1] - lead) // CHUNKS
    i = 0
    for j, _, _ in tiles:
        for g in range(GROUPS):
            ref[j, pl.ds(lead + step + g * 8 * steps, 8, stride=steps), :] = values[i]
            i += 1


def rows_before(x, k, fill):
    at = lax.broadcasted_iota(jnp.int32, x.shape, 0)
    return jnp.where(at >= k, pltpu.roll(x, k, axis=0), fill)


def rows_after(x, k, fill):
    at = lax.broadcasted_iota(jnp.int32, x.shape, 0)
    return jnp.where(at < 8 - k, pltpu.roll(x, 8 - k, axis=0), fill)


def whole_row(x, i):
    return jnp.broadcast_to(x[i : i + 1, :], x.shape)


def chain(base, slope, floor=None, back=False):
    shifted, last, first = (rows_after, 0, 7) if back else (rows_before, 7, 0)
    starts = [None] * GROUPS
    carry = jnp.zeros((8, LANE), F32)
    for g in reversed(range(GROUPS)) if back else range(GROUPS):
        b, q, f = base[g], slope[g], None if floor is None else floor[g]
        for k in (1, 2, 4):
            early = shifted(b, k, 0.0)
            if f is not None:
                f = jnp.maximum(f, b + q * shifted(f, k, 0.0))
            b = b + q * early
            q = q * shifted(q, k, 1.0)
        ends = b + q * carry
        if f is not None:
            ends = jnp.maximum(ends, f)
        starts[g] = jnp.where(
            lax.broadcasted_iota(jnp.int32, ends.shape, 0) == first, carry, shifted(ends, 1, 0.0)
        )
        carry = whole_row(ends, last)
    return starts


def by_tile(tiles, run, *lists):
    out = []
    for n in range(len(tiles)):
        out += run(*(x[n * GROUPS : (n + 1) * GROUPS] for x in lists))
    return out


def handed_on(ends):
    out, carry = [], jnp.zeros((8, LANE), F32)
    for x in ends:
        out.append(jnp.where(lax.broadcasted_iota(jnp.int32, x.shape, 0) == 0, carry, rows_before(x, 1, 0.0)))
        carry = whole_row(x, 7)
    return out


def power(x, n):
    out = None
    while n:
        if n & 1:
            out = x if out is None else out * x
        x = x * x
        n >>= 1
    return out


def softplus2(before):
    return [jnp.where(b > 25.0, b * LN2, jnp.log(1.0 + jnp.exp2(b))) for b in before]


def run_bounds(drive_ref, decay, tiles, steps):
    u = [d for d in decay for _ in range(GROUPS)]
    u2 = [d * LOG2E for d in u]

    def body(step, carry):
        state, line = carry
        drive = load_step(drive_ref, step, tiles)
        line = [d + a * v for d, a, v in zip(drive, u, line)]
        state = softplus2([d + a * v for d, a, v in zip(drive, u2, state)])
        return state, line

    zero = [jnp.zeros((8, LANE), F32) for _ in u]
    state, line = lax.fori_loop(0, steps, body, (zero, zero), unroll=11)
    return state, [a * LN2 for a in line]


def run_chunks(drive_ref, state_ref, start, decay, tiles, steps):
    u2 = [d * LOG2E for d in decay for _ in range(GROUPS)]

    def body(step, carry):
        state, slope = carry
        drive = load_step(drive_ref, step, tiles)
        before = [d + u * s for d, u, s in zip(drive, u2, state)]
        state = softplus2(before)
        slope = [a + (b - s * LOG2E) for a, b, s in zip(slope, before, state)]
        store_step(state_ref, step, tiles, state, lead=8)
        return state, slope

    zero = [jnp.zeros((8, LANE), F32) for _ in start]
    state, slope = lax.fori_loop(0, steps, body, (start, zero), unroll=True)
    top = [power(d, steps) for d in decay for _ in range(GROUPS)]
    return state, [t * jnp.exp2(a) for t, a in zip(top, slope)]


def solve(drive_ref, state_ref, decay_row, tiles):
    steps = drive_ref.shape[1] // CHUNKS
    decay = spread_rows(decay_row, tiles)
    top = [power(d, steps) for d in decay for _ in range(GROUPS)]
    low, line = run_bounds(drive_ref, decay, tiles, steps)
    start = by_tile(tiles, lambda f, b, q: chain(b, q, f), low, line, top)

    def again(carry):
        count, worst, _ = carry
        return jnp.logical_and(worst > 0.0, count < CHUNKS + 1)

    def newton(carry):
        count, _, start = carry
        end, slope = run_chunks(drive_ref, state_ref, start, decay, tiles, steps)
        miss = [e - s for e, s in zip(by_tile(tiles, handed_on, end), start)]
        worst = None
        for m, s in zip(miss, start):
            over = jnp.abs(m) - TOLERANCE * jnp.maximum(s, 1.0)
            worst = over if worst is None else jnp.maximum(worst, over)

        def step(miss, slope, start):
            after = [
                jnp.where(
                    lax.broadcasted_iota(jnp.int32, m.shape, 0) == 7,
                    whole_row(miss[g + 1], 0) if g + 1 < GROUPS else 0.0,
                    rows_after(m, 1, 0.0),
                )
                for g, m in enumerate(miss)
            ]
            return [s + c for s, c in zip(start, chain(after, slope))]

        return count + 1, jnp.max(worst), by_tile(tiles, step, miss, slope, start)

    lax.while_loop(again, newton, (jnp.int32(0), jnp.float32(1.0), start))


def run_back(grad_ref, sigma_ref, start, decay, tiles, steps, store):
    u = [d for d in decay for _ in range(GROUPS)]

    def body(i, carry):
        z, prod = carry
        step = steps - 1 - i
        gs = load_step(grad_ref, step, tiles)
        sig = load_step(sigma_ref, step, tiles)
        z = [s * (g + a * v) for s, g, a, v in zip(sig, gs, u, z)]
        if store:
            store_step(grad_ref, step, tiles, z)
            return z, prod
        return z, [p * (s * a) for p, s, a in zip(prod, sig, u)]

    ones = [] if store else [jnp.ones((8, LANE), F32) for _ in start]
    return lax.fori_loop(0, steps, body, (start, ones), unroll=11)


def solve_back(grad_ref, sigma_ref, decay_row, tiles):
    steps = grad_ref.shape[1] // CHUNKS
    decay = spread_rows(decay_row, tiles)
    zero = [jnp.zeros((8, LANE), F32)] * (len(tiles) * GROUPS)
    end, slope = run_back(grad_ref, sigma_ref, zero, decay, tiles, steps, False)
    start = by_tile(tiles, lambda b, q: chain(b, q, back=True), end, slope)
    run_back(grad_ref, sigma_ref, start, decay, tiles, steps, True)


BLOCK = 88


def row_blocks(length, body):
    @pl.loop(0, length // BLOCK)
    def _(i):
        body(pl.ds(pl.multiple_of(i * BLOCK, 8), BLOCK))


def fill_drive(proj_ref, drive_ref, mean, inverse, gain, shift, tiles):
    scale = inverse * gain * LOG2E
    offset = shift * LOG2E

    def body(rows):
        for j, c, _ in tiles:
            at = slice(c, c + LANE)
            drive_ref[j, rows, :] = (proj_ref[rows, at] - mean[:, at]) * scale[:, at] + offset[:, at]

    row_blocks(proj_ref.shape[0], body)


def fill_sigma(drive_ref, prev_ref, decay_row, tiles, length):
    u2 = decay_row * LOG2E

    def body(i, _):
        for j, c, _w in tiles:
            rows = pl.ds(pl.multiple_of(i * BLOCK, 8), BLOCK)
            before = drive_ref[j, rows, :] + u2[:, c : c + LANE] * prev_ref[j, pl.ds(i * BLOCK + 7, BLOCK), :]
            drive_ref[j, rows, :] = 1.0 / (1.0 + jnp.exp2(-before))
        return 0

    lax.fori_loop(0, length // BLOCK, body, 0)


def finish_back(grad_ref, state_ref, proj_ref, mean, inverse, tiles, gb_ref, sums_ref):
    length, width = proj_ref.shape
    zero = tuple(jnp.zeros((1, LANE), F32) for _ in tiles)

    def body(i, carry):
        shift, gain, decay = (list(x) for x in carry)
        rows = pl.ds(pl.multiple_of(i * BLOCK, 8), BLOCK)
        for j, c, _w in tiles:
            at = slice(c, c + LANE)
            gb = grad_ref[j, rows, :]
            gb_ref[rows, at] = gb
            shift[j] = shift[j] + jnp.sum(gb, axis=0, keepdims=True)
            gain[j] = gain[j] + jnp.sum(gb * (proj_ref[rows, at] - mean[:, at]), axis=0, keepdims=True)
            decay[j] = decay[j] + jnp.sum(
                gb * state_ref[j, pl.ds(i * BLOCK + 7, BLOCK), :], axis=0, keepdims=True
            )
        return tuple(shift), tuple(gain), tuple(decay)

    shift, gain, decay = lax.fori_loop(0, length // BLOCK, body, (zero, zero, zero))
    for j, c, _ in tiles:
        at = slice(c, c + LANE)
        scaled = gain[j] * inverse[:, at]
        for p in range(sums_ref.shape[0]):
            sums_ref[p, 0:1, at] = shift[j]
            sums_ref[p, 1:2, at] = scaled
            sums_ref[p, 2:3, at] = decay[j]


def clear(state_ref, tiles):
    for j, _, _ in tiles:
        state_ref[j, 0:8, :] = jnp.zeros((8, LANE), F32)


def put_states(state_ref, out_ref, tiles, wide_ref=None):
    def body(i, _):
        rows = pl.ds(pl.multiple_of(i * 16, 16), 16)
        for j, c, w in tiles:
            s = state_ref[j, pl.ds(pl.multiple_of(8 + i * 16, 8), 16), :]
            out_ref[rows, c : c + w] = s[:, :w].astype(BF16)
            if wide_ref is not None:
                wide_ref[rows, c : c + LANE] = s
        return 0

    lax.fori_loop(0, out_ref.shape[0] // 16, body, 0, unroll=4)


def forward_kernel(stats_ref, proj_ref, par_ref, out_ref, wide_ref, sum_ref, drive, state):
    length, width = proj_ref.shape
    tiles = tiles_of(width)
    outs = tiles_of(out_ref.shape[1])
    mean, var, inverse = merged(stats_ref, length, sum_ref)
    gain, shift, decay = par_ref[0:1, :], par_ref[1:2, :], par_ref[2:3, :]
    fill_drive(proj_ref, drive, mean, inverse, gain, shift, tiles)
    clear(state, tiles)
    solve(drive, state, decay, tiles)
    put_states(state, out_ref, outs, wide_ref)


def norm_kernel(proj_ref, sum_ref, norm_ref, total_ref):
    length = proj_ref.shape[0]
    mean, inverse = sum_ref[0:1, :], sum_ref[2:3, :]
    total_ref[...] = jnp.zeros(total_ref.shape, F32)
    total_ref[7:8, :] = length * (sum_ref[3:4, :] - mean) * inverse

    def body(i, _):
        rows = pl.ds(pl.multiple_of(i * 16, 16), 16)
        norm_ref[rows, :] = ((proj_ref[rows, :] - mean) * inverse).astype(BF16)
        return 0

    lax.fori_loop(0, length // 16, body, 0, unroll=4)


def turn_kernel(
    stats_ref,
    proj_ref,
    par_ref,
    first_ref,
    cot_hbm,
    rmean_hbm,
    rvar_hbm,
    out_ref,
    gb_ref,
    sums_ref,
    sum_ref,
    nmean_ref,
    nvar_ref,
    drive,
    state,
    grad,
    cot_ref,
    rmean_ref,
    rvar_ref,
    arrived,
):
    copies = [
        pltpu.make_async_copy(a, b, arrived.at[i])
        for i, (a, b) in enumerate(
            ((cot_hbm, cot_ref), (rmean_hbm, rmean_ref), (rvar_hbm, rvar_ref))
        )
    ]
    for copy in copies:
        copy.start()
    length, width = proj_ref.shape
    tiles = tiles_of(width)
    outs = tiles_of(out_ref.shape[1])
    mean, var, inverse = merged(stats_ref, length, sum_ref)
    gain, shift, decay = par_ref[0:1, :], par_ref[1:2, :], par_ref[2:3, :]
    real = out_ref.shape[1]
    count = float(stats_ref.shape[0] * length)
    fill_drive(proj_ref, drive, mean, inverse, gain, shift, tiles)
    clear(state, tiles)
    solve(drive, state, decay, tiles)
    put_states(state, out_ref, outs)
    fill_sigma(drive, state, decay, tiles, length)
    for copy in copies:
        copy.wait()
    for row, m, v in ((0, first_ref[0:1, :], first_ref[1:2, :]), (1, mean, var)):
        nmean_ref[row : row + 1, :] = (1.0 - MOMENTUM) * rmean_ref[row : row + 1, :] + MOMENTUM * m[:, :real]
        nvar_ref[row : row + 1, :] = (1.0 - MOMENTUM) * rvar_ref[row : row + 1, :] + (
            MOMENTUM * v[:, :real]
        ) * (count / (count - 1.0))
    for j, _, w in outs:
        if w < LANE:
            grad[j] = jnp.zeros(grad.shape[1:], F32)

    def load_cot(i, _):
        rows = pl.ds(pl.multiple_of(i * 16, 16), 16)
        for j, c, w in outs:
            grad[j, rows, :w] = cot_ref[rows, c : c + w].astype(F32)
        return 0

    lax.fori_loop(0, length // 16, load_cot, 0, unroll=4)
    solve_back(grad, drive, decay, tiles)
    finish_back(grad, state, proj_ref, mean, inverse, tiles, gb_ref, sums_ref)


def back_kernel(
    keep_ref, got_ref, proj_ref, wide_ref, sum_ref, par_ref, gb_ref, sums_ref, own_ref, drive, state, grad
):
    length, width = proj_ref.shape
    tiles = tiles_of(width)
    mean, inverse = sum_ref[0:1, :], sum_ref[2:3, :]
    gain, shift, decay = par_ref[0:1, :], par_ref[1:2, :], par_ref[2:3, :]
    fill_drive(proj_ref, drive, mean, inverse, gain, shift, tiles)
    clear(state, tiles)

    def load(i, _):
        rows = pl.ds(pl.multiple_of(i * 16, 16), 16)
        for j, c, _w in tiles:
            at = slice(c, c + LANE)
            grad[j, rows, :] = keep_ref[rows, at] + got_ref[rows, at].astype(F32)
            state[j, pl.ds(pl.multiple_of(8 + i * 16, 8), 16), :] = wide_ref[rows, at]
        return 0

    lax.fori_loop(0, length // 16, load, 0, unroll=4)
    fill_sigma(drive, state, decay, tiles, length)
    solve_back(grad, drive, decay, tiles)
    finish_back(grad, state, proj_ref, mean, inverse, tiles, gb_ref, sums_ref)
    scale = gain * inverse
    average = sums_ref[0, 0:1, :] * (1.0 / length)

    def put_own(i, _):
        rows = pl.ds(pl.multiple_of(i * 16, 16), 16)
        own_ref[rows, :] = (scale * (gb_ref[rows, :] - average)).astype(BF16)
        return 0

    lax.fori_loop(0, length // 16, put_own, 0, unroll=4)


def total_of(sums_ref):
    peers = sums_ref.shape[0]
    out = sums_ref[0]
    for p in range(1, peers):
        out = out + sums_ref[p]
    return out


def grad_kernel(sums_ref, gb_ref, proj_ref, sum_ref, par_ref, g_ref, total_ref):
    length, _ = proj_ref.shape
    total = total_of(sums_ref)
    total_ref[...] = total
    count = float(sums_ref.shape[0] * length)
    mean, inverse = sum_ref[0:1, :], sum_ref[2:3, :]
    scale = par_ref[0:1, :] * inverse
    base = total[0:1, :] * (1.0 / count)
    lean = total[1:2, :] * (1.0 / count) * inverse

    total_ref[7:8, :] = scale * (
        sums_ref[lax.axis_index("seq"), 0:1, :]
        - length * base
        - length * (sum_ref[3:4, :] - mean) * lean
    )

    def body(i, _):
        rows = pl.ds(pl.multiple_of(i * 16, 16), 16)
        g_ref[rows, :] = (
            scale * (gb_ref[rows, :] - base - (proj_ref[rows, :] - mean) * lean)
        ).astype(BF16)
        return 0

    lax.fori_loop(0, length // 16, body, 0, unroll=4)


def send_kernel(g_ref, mate_ref, w_ref, wmate_ref, out_ref):
    here = lax.axis_index("neur")
    for c in range(0, out_ref.shape[1], 256):
        at = slice(c, c + 256)
        out_ref[:, at] = (
            dot_nt(g_ref[...], w_ref[here ^ 2, at, :]) + dot_nt(mate_ref[...], wmate_ref[1, at, :])
        ).astype(BF16)


def keep_kernel(g_ref, mate_ref, w_ref, wmate_ref, out_ref):
    here = lax.axis_index("neur")
    for c in range(0, out_ref.shape[1], 256):
        at = slice(c, c + 256)
        out_ref[:, at] = dot_nt(g_ref[...], w_ref[here, at, :]) + dot_nt(
            mate_ref[...], wmate_ref[0, at, :]
        )


def split(row):
    high = row.astype(BF16)
    return high, (row - high.astype(F32)).astype(BF16)


def dot_tn(a, b):
    return lax.dot_general(a, b, (((0,), (0,)), ((), ())), preferred_element_type=F32)


def outer(a, b):
    (a_high, a_low), (b_high, b_low) = split(a), split(b)
    return dot_tn(
        jnp.concatenate([a_high, a_high, a_low, a_low]), jnp.concatenate([b_high, b_low, b_high, b_low])
    )


def weight_kernel(parted, own_ref, mate_ref, far_ref, cross_ref, g_ref, sum_ref, total_ref, *refs):
    outs, hold = (refs[:-1], refs[-1]) if parted else ((), refs[0])
    place = seat() if parted else 0
    _, half, width = hold.shape
    for k, x_ref in enumerate((own_ref, mate_ref, far_ref, cross_ref)):
        real = x_ref.shape[1]
        mean = sum_ref[4 + k : 5 + k, :real]
        part = (dot_tn(x_ref[...], g_ref[...]) - outer(mean, total_ref[7:8, :])).astype(BF16)
        hold[(2 * k) ^ place] = part[:half]
        rest = part[half:]
        hold[(2 * k + 1) ^ place, : rest.shape[0], :] = rest
        if not parted:
            hold[2 * k + 1, rest.shape[0] :, :] = jnp.zeros((half - rest.shape[0], width), BF16)
    if parted:
        left, right = slice(0, half), slice(half, width)
        for out, shares, at in zip(
            outs, ((0, 1, 2, 3), (4, 5, 6, 7), (0, 1, 4, 5), (2, 3, 6, 7)), (left, left, right, right)
        ):
            for i, r in enumerate(shares):
                out[i] = hold[r, :, at]


def halve_kernel(left_ref, got_left_ref, right_ref, got_right_ref, *outs):
    for n, (keep, got) in enumerate(((left_ref, got_left_ref), (right_ref, got_right_ref))):
        mine, give = outs[2 * n : 2 * n + 2]
        for i in range(2):
            mine[i] = wide_sum(keep[i], got[i])
            give[i] = half_sum(keep[i + 2], got[i + 2])


def settle_kernel(
    length,
    left_ref,
    got_left_ref,
    right_ref,
    got_right_ref,
    lean_left_ref,
    lean_got_left_ref,
    lean_right_ref,
    lean_got_right_ref,
    sums_ref,
    stats_ref,
    sum_ref,
    par_ref,
    *outs,
):
    peers = sums_ref.shape[0]
    total = total_of(sums_ref)
    base = total[0:1, :] * (1.0 / (peers * length))
    scale = par_ref[0:1, :] * sum_ref[2:3, :]
    lean = scale * total[1:2, :] * (1.0 / (peers * length))
    place, here = lax.axis_index("seq"), seat()
    half = left_ref.shape[1]
    for n, (keep, got, lean_keep, lean_got, other, shares, at) in enumerate((
        (left_ref, got_left_ref, lean_left_ref, lean_got_left_ref, place ^ LEVEL[4], (0, 1, 2, 3), slice(0, half)),
        (right_ref, got_right_ref, lean_right_ref, lean_got_right_ref, place ^ LEVEL[2], (0, 1, 4, 5), slice(half, 2 * half)),
    )):
        mine, give = outs[2 * n : 2 * n + 2]
        columns = [
            (scale * (sums_ref[p, 0:1, :] * (1.0 / length) - base) * length)[:, at] for p in (place, other)
        ]
        for i, r in enumerate(shares):
            share = here ^ r
            row, low = share >> 1, pl.multiple_of((share & 1) * half, 128)
            middle = sum_ref[pl.ds(4 + row, 1), pl.ds(low, half)]
            value = wide_sum(keep[i], got[i]) - lean[:, at] * wide_sum(lean_keep[i], lean_got[i])
            for p, column in zip((place, other), columns):
                value = value + outer(stats_ref[p, pl.ds(2 + row, 1), pl.ds(low, half)] - middle, column)
            if i < 2:
                mine[i] = value
            else:
                give[i - 2] = value.astype(BF16)


def quarter_kernel(left_ref, got_left_ref, right_ref, got_right_ref, mine_ref, give_ref):
    edge = left_ref.shape[2]
    for keep, got, at in (
        (left_ref, got_left_ref, slice(0, edge)),
        (right_ref, got_right_ref, slice(edge, 2 * edge)),
    ):
        mine_ref[:, at] = wide_sum(keep[0], got[0])
        give_ref[:, at] = half_sum(keep[1], got[1])


def spread_kernel(parted, *refs):
    if parted:
        shares, out_ref, hold = refs[:-2], refs[-2], refs[-1]
        for r, share in enumerate(shares):
            hold[r] = share[...]
    else:
        hold, out_ref = refs
    place, here = seat() if parted else 0, lax.axis_index("neur")
    half = hold.shape[1]
    block = out_ref.shape[0] // 4
    width = out_ref.shape[1]
    for b in range(4):
        for h in range(2):
            low, high = b * block + h * half, min(b * block + h * half + half, (b + 1) * block)
            which = (((here ^ b) * 2) + h) ^ place
            out_ref[low:high, :] = hold[which, : high - low, :width].astype(F32)


def wide_sum(a, b):
    return a.astype(F32) + b.astype(F32)


def half_sum(a, b):
    return wide_sum(a, b).astype(BF16)


def swap(x, bit, axis="seq"):
    n = lax.axis_size(axis)
    return lax.ppermute(x, axis, [(i, i ^ bit) for i in range(n)])


LEVEL = {4: 1, 2: 2, 1: 4}


def seat():
    place = lax.axis_index("seq")
    return ((place & 1) << 2) | (place & 2) | ((place >> 2) & 1)


def gather_first(v):
    return {0: v, 4: swap(v, LEVEL[4]), 2: swap(v, LEVEL[2]), 1: swap(v, LEVEL[1])}


def gather_rest(out):
    out = dict(out)
    out[2], out[4] = lax.optimization_barrier((out[2], out[4]))
    out[6] = swap(out[2], LEVEL[4])
    out[5] = swap(out[1], LEVEL[4])
    out[3] = swap(out[1], LEVEL[2])
    out[3], out[6] = lax.optimization_barrier((out[3], out[6]))
    out[7] = swap(out[3], LEVEL[4])
    return [out[r] for r in range(8)]


def per_device(devices_seq, *args):
    (
        tokens,
        w_first,
        gain_first,
        shift_first,
        decay_first,
        w_second,
        gain_second,
        shift_second,
        decay_second,
        cotangent,
        running_mean,
        running_var,
    ) = args
    _, length, real = tokens.shape
    width = -(-real // LANE) * LANE
    tiles = len(tiles_of(width))
    peers = devices_seq
    here = lax.axis_index("neur")
    tokens, cotangent = tokens[0], cotangent[0]

    scans = [
        pltpu.VMEM((tiles, length, LANE), F32),
        pltpu.VMEM((tiles, length + 8, LANE), F32),
    ]
    grads = [pltpu.VMEM((tiles, length, LANE), F32)]

    def share(stats):
        return lax.all_to_all(stats, "seq", 0, 0, tiled=True)

    def project(own, w, rows, *gives, aside=None):
        far = swap(own, 2, "neur")
        mate = swap(own, 1, "neur")
        w = lax.optimization_barrier((w, own))[0]
        w4, give, par = call(
            block_kernel,
            [shape(4, width, width, dtype=BF16), shape(2, width, width, dtype=BF16), shape(8, width)],
        )(w, *(row[None] for row in rows))
        part, means = call(project_early, [shape(length, width), shape(8, width)])(own, mate, w4)
        gives = [swap(lax.optimization_barrier((g, own))[0], 1, "neur") for g in gives + (give,)] if gives else give
        extra = aside(mate) if aside else ()
        far, part, par, gives, extra = lax.optimization_barrier((far, part, par, gives, extra))
        cross = swap(far, 1, "neur")
        part, means = call(project_middle, [shape(length, width), shape(8, width)])(part, means, far, w4)
        proj, stats = call(project_late, [shape(length, width), shape(peers, 8, width)])(
            part, means, cross, w4
        )
        return (own, mate, far, cross), proj, share(stats), w4, gives, par, extra

    def gradient(sums, gb, proj, summary, par):
        return call(grad_kernel, [shape(length, width, dtype=BF16), shape(8, width)])(
            sums, gb, proj, summary, par
        )

    def send(g, mate, w4, wm):
        out = call(send_kernel, shape(length, width, dtype=BF16))(g, mate, w4, wm)
        out, g, mate = lax.optimization_barrier((out, g, mate))
        got = swap(out, 2, "neur")
        keep = call(keep_kernel, shape(length, width))(g, mate, w4, wm)
        return keep, got

    half = width // 2

    def parts_shape(*lead):
        return shape(*lead, half, width, dtype=BF16)

    def weight_parts(*operands):
        if peers != 8:
            return call(functools.partial(weight_kernel, False), parts_shape(8))(*operands)
        return call(
            functools.partial(weight_kernel, True),
            [shape(4, half, half, dtype=BF16)] * 4,
            [pltpu.VMEM((8, half, width), BF16)],
        )(*operands)

    def weights(shares):
        if peers != 8:
            return call(functools.partial(spread_kernel, False), shape(4 * real, real))(shares)
        return call(
            functools.partial(spread_kernel, True),
            shape(4 * real, real),
            [pltpu.VMEM((8, half, width), BF16)],
        )(*shares)

    def together(*values):
        return lax.optimization_barrier(values)

    first_x, first_proj, first_stats, first_w, give, first_par, _ = project(
        tokens, w_first, (gain_first, shift_first, decay_first)
    )
    first_out, first_wide, first_sum = call(
        forward_kernel,
        [shape(length, real, dtype=BF16), shape(length, width), shape(8, width)],
        scans,
    )(first_stats, first_proj, first_par)

    def after(x, *earlier):
        return lax.optimization_barrier((x, earlier))[0]

    def leaning(mate):
        if peers != 8:
            return ()
        norm, norm_total = call(norm_kernel, [shape(length, width, dtype=BF16), shape(8, width)])(
            first_proj, after(first_sum, mate)
        )
        left, give_left, right, give_right = weight_parts(*first_x, norm, first_sum, norm_total)
        return left, swap(give_left, LEVEL[4]), right, swap(give_right, LEVEL[2])

    second_x, second_proj, second_stats, second_w, (first_mate, second_mate), second_par, lean = project(
        first_out, w_second, (gain_second, shift_second, decay_second), give, aside=leaning
    )
    second_out, second_gb, second_sums, second_sum, new_mean, new_var = call(
        turn_kernel,
        [
            shape(length, real, dtype=BF16),
            shape(length, width),
            shape(peers, 8, width),
            shape(8, width),
            shape(2, real),
            shape(2, real),
        ],
        scans
        + grads
        + [
            pltpu.VMEM((length, real), BF16),
            pltpu.VMEM((2, real), F32),
            pltpu.VMEM((2, real), F32),
            pltpu.SemaphoreType.DMA((3,)),
        ],
        in_specs=[pl.BlockSpec(memory_space=pltpu.VMEM)] * 4 + [pl.BlockSpec(memory_space=pl.ANY)] * 3,
    )(second_stats, second_proj, second_par, first_sum, cotangent, running_mean, running_var)

    second_sums = share(second_sums)
    second_g, second_total = gradient(second_sums, second_gb, second_proj, second_sum, second_par)
    mate = swap(second_g, 1, "neur")
    pairs = [shape(2, half, half), shape(2, half, half, dtype=BF16)] * 2
    rest = [shape(half, width), parts_shape()]
    second_parts = weight_parts(*second_x, second_g, second_sum, second_total)
    mate, second_parts = together(mate, second_parts)
    keep, got = send(second_g, mate, second_w, second_mate)
    if peers == 8:
        left, give_left, right, give_right = second_parts
        parcel = after((swap(give_left, LEVEL[4]), swap(give_right, LEVEL[2])), keep)
        left, give_left, right, give_right = call(halve_kernel, pairs)(left, parcel[0], right, parcel[1])
        keep, got, left = together(keep, got, left)
        parcel = swap(give_left, LEVEL[2]), swap(give_right, LEVEL[4])
    first_gb, first_sums, first_own = call(
        back_kernel,
        [shape(length, width), shape(peers, 8, width), shape(length, width, dtype=BF16)],
        scans + grads,
    )(keep, got, first_proj, first_wide, first_sum, first_par)
    if peers == 8:
        second_mine, give = call(quarter_kernel, rest)(left, parcel[0], right, parcel[1])
        first_sums, second_mine, give = together(first_sums, second_mine, give)
        left, give_left, right, give_right = weight_parts(
            *first_x, first_own, first_sum, jnp.zeros((8, width), F32)
        )
        parcel = swap(give_left, LEVEL[4]), swap(give_right, LEVEL[2])
    first_sums = share(first_sums)
    if peers == 8:
        first_sums, last, parcel = together(first_sums, swap(give, LEVEL[1]), parcel)
    first_g, first_total = gradient(first_sums, first_gb, first_proj, first_sum, first_par)
    mate = swap(first_g, 1, "neur")
    if peers == 8:
        left, give_left, right, give_right = call(functools.partial(settle_kernel, length), pairs)(
            left, parcel[0], right, parcel[1], *lean, first_sums, first_stats, first_sum, first_par
        )
        parcel = swap(give_left, LEVEL[2]), swap(give_right, LEVEL[4])
        mate, left = together(mate, left)
        keep, got = send(first_g, mate, first_w, first_mate)
        second_share = gather_first(half_sum(second_mine, last))
        mine, give = call(quarter_kernel, rest)(left, parcel[0], right, parcel[1])
        keep, first_share = together(keep, half_sum(mine, swap(give, LEVEL[1])))
        second_share = gather_rest(second_share)
        first_share = gather_rest(gather_first(first_share))
    else:
        first_parts = weight_parts(*first_x, first_g, first_sum, first_total)
        keep, got = send(first_g, mate, first_w, first_mate)
        second_share, first_share = lax.psum((second_parts, first_parts), "seq")
    grad_w_first = weights(first_share)
    grad_w_second = weights(second_share)
    input_grad = (keep + got.astype(F32))[:, :real]

    def pair(row):
        return jnp.stack([first_total[row, :real], second_total[row, :real]])

    return (
        first_out[None],
        second_out[None],
        input_grad[None],
        grad_w_first,
        grad_w_second,
        pair(1),
        pair(0),
        pair(2),
        new_mean,
        new_var,
    )


def solution(mesh):
    rows, line, flat = P("seq", None, "neur"), P("neur"), P(None, "neur")
    return jax.shard_map(
        functools.partial(per_device, mesh.shape["seq"]),
        mesh=mesh,
        in_specs=(rows, flat, line, line, line, flat, line, line, line, rows, flat, flat),
        out_specs=(rows, rows, rows) + (flat,) * 7,
        check_vma=False,
    )
```

```python
import functools
import math

import jax
import jax.numpy as jnp
from jax import lax
from jax.experimental import pallas as pl
from jax.experimental.pallas import tpu as pltpu
from jax.sharding import PartitionSpec as P

EPSILON = 1e-05
MOMENTUM = 0.1
LANE = 128
CHUNKS = 32
GROUPS = CHUNKS // 8
TOLERANCE = 2e-5
LOG2E = math.log2(math.e)
LN2 = math.log(2.0)
F32 = jnp.float32
BF16 = jnp.bfloat16
VMEM_BYTES = 16 * 1024 * 1024


def call(kernel, outs, scratch=(), **specs):
    return pl.pallas_call(
        kernel,
        **specs,
        out_shape=outs,
        scratch_shapes=list(scratch),
        compiler_params=pltpu.CompilerParams(vmem_limit_bytes=VMEM_BYTES),
    )


def shape(*dims, dtype=F32):
    return jax.ShapeDtypeStruct(dims, dtype)


def tiles_of(width):
    return [(j, j * LANE, min(LANE, width - j * LANE)) for j in range(-(-width // LANE))]


def dot(a, b):
    return jnp.dot(a, b, preferred_element_type=F32)


def dot_nt(a, b):
    return lax.dot_general(a, b, (((1,), (1,)), ((), ())), preferred_element_type=F32)


def block_kernel(w_ref, gain_ref, shift_ref, decay_ref, out_ref, mate_ref, par_ref):
    here = lax.axis_index("neur")
    blocks, width, _ = out_ref.shape
    real = w_ref.shape[0] // blocks
    out_ref[...] = jnp.zeros(out_ref.shape, BF16)
    for b in range(blocks):
        out_ref[b, :real, : w_ref.shape[1]] = w_ref[b * real : (b + 1) * real, :]
    for i, k in enumerate((1, 3)):
        mate_ref[i] = out_ref[here ^ k]
    par_ref[...] = jnp.zeros(par_ref.shape, F32)
    for i, row_ref in enumerate((gain_ref, shift_ref, decay_ref)):
        par_ref[i : i + 1, : row_ref.shape[1]] = row_ref[...]


def means_of(x_ref):
    length = x_ref.shape[0]
    return dot(jnp.ones((16, length), BF16), x_ref[...])[:1] * (1.0 / length)


def project_early(own_ref, mate_ref, w_ref, part_ref, means_ref):
    here = lax.axis_index("neur")
    k = own_ref.shape[1]
    means_ref[...] = jnp.zeros(means_ref.shape, F32)
    means_ref[0:1, :k] = means_of(own_ref)
    means_ref[1:2, :k] = means_of(mate_ref)
    for c in range(0, part_ref.shape[1], 256):
        part_ref[:, c : c + 256] = dot(own_ref[...], w_ref[here, :k, c : c + 256]) + dot(
            mate_ref[...], w_ref[here ^ 1, :k, c : c + 256]
        )


def project_middle(part_ref, means_ref, far_ref, w_ref, out_ref, out_means_ref):
    here = lax.axis_index("neur")
    k = far_ref.shape[1]
    out_means_ref[...] = means_ref[...]
    out_means_ref[2:3, :k] = means_of(far_ref)
    for c in range(0, part_ref.shape[1], 256):
        out_ref[:, c : c + 256] = part_ref[:, c : c + 256] + dot(
            far_ref[...], w_ref[here ^ 2, :k, c : c + 256]
        )


def project_late(part_ref, means_ref, cross_ref, w_ref, proj_ref, stats_ref):
    here = lax.axis_index("neur")
    k = cross_ref.shape[1]
    peers, _, width = stats_ref.shape
    cross = means_of(cross_ref)
    for p in range(peers):
        stats_ref[p, 2:8, :] = means_ref[0:6, :]
        stats_ref[p, 5:6, :k] = cross
    length = proj_ref.shape[0]
    for c in range(0, part_ref.shape[1], 256):
        y = part_ref[:, c : c + 256] + dot(cross_ref[...], w_ref[here ^ 3, :k, c : c + 256])
        proj_ref[:, c : c + 256] = y
        mean = jnp.sum(y, axis=0, keepdims=True) * (1.0 / length)
        off = y - mean
        spread = jnp.sum(off * off, axis=0, keepdims=True)
        for p in range(stats_ref.shape[0]):
            stats_ref[p, 0:1, c : c + 256] = mean
            stats_ref[p, 1:2, c : c + 256] = spread


def merged(stats_ref, length, sum_ref):
    peers = stats_ref.shape[0]
    means = [stats_ref[p, 0:1, :] for p in range(peers)]
    mean = sum(means[1:], means[0]) * (1.0 / peers)
    total = None
    for p in range(peers):
        off = means[p] - mean
        term = stats_ref[p, 1:2, :] + off * off * float(length)
        total = term if total is None else total + term
    var = total * (1.0 / (peers * length))
    inverse = lax.rsqrt(var + EPSILON)
    features = stats_ref[0, 2:6, :]
    for p in range(1, peers):
        features = features + stats_ref[p, 2:6, :]
    sum_ref[0:1, :] = mean
    sum_ref[1:2, :] = var
    sum_ref[2:3, :] = inverse
    sum_ref[3:4, :] = stats_ref[lax.axis_index("seq"), 0:1, :]
    sum_ref[4:8, :] = features * (1.0 / peers)
    return mean, var, inverse


def spread_rows(row, tiles):
    return [jnp.broadcast_to(row[:, c : c + LANE], (8, LANE)) for _, c, _ in tiles]


def load_step(ref, step, tiles, lead=0):
    steps = (ref.shape[1] - lead) // CHUNKS
    return [
        ref[j, pl.ds(lead + step + g * 8 * steps, 8, stride=steps), :]
        for j, _, _ in tiles
        for g in range(GROUPS)
    ]


def store_step(ref, step, tiles, values, lead=0):
    steps = (ref.shape[1] - lead) // CHUNKS
    i = 0
    for j, _, _ in tiles:
        for g in range(GROUPS):
            ref[j, pl.ds(lead + step + g * 8 * steps, 8, stride=steps), :] = values[i]
            i += 1


def rows_before(x, k, fill):
    at = lax.broadcasted_iota(jnp.int32, x.shape, 0)
    return jnp.where(at >= k, pltpu.roll(x, k, axis=0), fill)


def rows_after(x, k, fill):
    at = lax.broadcasted_iota(jnp.int32, x.shape, 0)
    return jnp.where(at < 8 - k, pltpu.roll(x, 8 - k, axis=0), fill)


def whole_row(x, i):
    return jnp.broadcast_to(x[i : i + 1, :], x.shape)


def chain(base, slope, floor=None, back=False):
    shifted, last, first = (rows_after, 0, 7) if back else (rows_before, 7, 0)
    starts = [None] * GROUPS
    carry = jnp.zeros((8, LANE), F32)
    for g in reversed(range(GROUPS)) if back else range(GROUPS):
        b, q, f = base[g], slope[g], None if floor is None else floor[g]
        for k in (1, 2, 4):
            early = shifted(b, k, 0.0)
            if f is not None:
                f = jnp.maximum(f, b + q * shifted(f, k, 0.0))
            b = b + q * early
            q = q * shifted(q, k, 1.0)
        ends = b + q * carry
        if f is not None:
            ends = jnp.maximum(ends, f)
        starts[g] = jnp.where(
            lax.broadcasted_iota(jnp.int32, ends.shape, 0) == first, carry, shifted(ends, 1, 0.0)
        )
        carry = whole_row(ends, last)
    return starts


def by_tile(tiles, run, *lists):
    out = []
    for n in range(len(tiles)):
        out += run(*(x[n * GROUPS : (n + 1) * GROUPS] for x in lists))
    return out


def handed_on(ends):
    out, carry = [], jnp.zeros((8, LANE), F32)
    for x in ends:
        out.append(jnp.where(lax.broadcasted_iota(jnp.int32, x.shape, 0) == 0, carry, rows_before(x, 1, 0.0)))
        carry = whole_row(x, 7)
    return out


def power(x, n):
    out = None
    while n:
        if n & 1:
            out = x if out is None else out * x
        x = x * x
        n >>= 1
    return out


def softplus2(before):
    return [jnp.where(b > 25.0, b * LN2, jnp.log(1.0 + jnp.exp2(b))) for b in before]


def run_bounds(drive_ref, decay, tiles, steps):
    u = [d for d in decay for _ in range(GROUPS)]
    u2 = [d * LOG2E for d in u]

    def body(step, carry):
        state, line = carry
        drive = load_step(drive_ref, step, tiles)
        line = [d + a * v for d, a, v in zip(drive, u, line)]
        state = softplus2([d + a * v for d, a, v in zip(drive, u2, state)])
        return state, line

    zero = [jnp.zeros((8, LANE), F32) for _ in u]
    state, line = lax.fori_loop(0, steps, body, (zero, zero), unroll=True)
    return state, [a * LN2 for a in line]


def run_chunks(drive_ref, state_ref, start, decay, tiles, steps):
    u2 = [d * LOG2E for d in decay for _ in range(GROUPS)]

    def body(step, carry):
        state, slope = carry
        drive = load_step(drive_ref, step, tiles)
        before = [d + u * s for d, u, s in zip(drive, u2, state)]
        state = softplus2(before)
        slope = [a + (b - s * LOG2E) for a, b, s in zip(slope, before, state)]
        store_step(state_ref, step, tiles, state, lead=8)
        return state, slope

    zero = [jnp.zeros((8, LANE), F32) for _ in start]
    state, slope = lax.fori_loop(0, steps, body, (start, zero), unroll=True)
    top = [power(d, steps) for d in decay for _ in range(GROUPS)]
    return state, [t * jnp.exp2(a) for t, a in zip(top, slope)]


def solve(drive_ref, state_ref, decay_row, tiles):
    steps = drive_ref.shape[1] // CHUNKS
    decay = spread_rows(decay_row, tiles)
    top = [power(d, steps) for d in decay for _ in range(GROUPS)]
    low, line = run_bounds(drive_ref, decay, tiles, steps)
    start = by_tile(tiles, lambda f, b, q: chain(b, q, f), low, line, top)

    def again(carry):
        count, worst, _ = carry
        return jnp.logical_and(worst > 0.0, count < CHUNKS + 1)

    def newton(carry):
        count, _, start = carry
        end, slope = run_chunks(drive_ref, state_ref, start, decay, tiles, steps)
        miss = [e - s for e, s in zip(by_tile(tiles, handed_on, end), start)]
        worst = None
        for m, s in zip(miss, start):
            over = jnp.abs(m) - TOLERANCE * jnp.maximum(s, 1.0)
            worst = over if worst is None else jnp.maximum(worst, over)

        def step(miss, slope, start):
            after = [
                jnp.where(
                    lax.broadcasted_iota(jnp.int32, m.shape, 0) == 7,
                    whole_row(miss[g + 1], 0) if g + 1 < GROUPS else 0.0,
                    rows_after(m, 1, 0.0),
                )
                for g, m in enumerate(miss)
            ]
            return [s + c for s, c in zip(start, chain(after, slope))]

        return count + 1, jnp.max(worst), by_tile(tiles, step, miss, slope, start)

    lax.while_loop(again, newton, (jnp.int32(0), jnp.float32(1.0), start))


def run_back(grad_ref, sigma_ref, start, decay, tiles, steps, store):
    u = [d for d in decay for _ in range(GROUPS)]

    def body(i, carry):
        z, prod = carry
        step = steps - 1 - i
        gs = load_step(grad_ref, step, tiles)
        sig = load_step(sigma_ref, step, tiles)
        z = [s * (g + a * v) for s, g, a, v in zip(sig, gs, u, z)]
        if store:
            store_step(grad_ref, step, tiles, z)
            return z, prod
        return z, [p * (s * a) for p, s, a in zip(prod, sig, u)]

    ones = [] if store else [jnp.ones((8, LANE), F32) for _ in start]
    return lax.fori_loop(0, steps, body, (start, ones), unroll=True)


def solve_back(grad_ref, sigma_ref, decay_row, tiles):
    steps = grad_ref.shape[1] // CHUNKS
    decay = spread_rows(decay_row, tiles)
    zero = [jnp.zeros((8, LANE), F32)] * (len(tiles) * GROUPS)
    end, slope = run_back(grad_ref, sigma_ref, zero, decay, tiles, steps, False)
    start = by_tile(tiles, lambda b, q: chain(b, q, back=True), end, slope)
    run_back(grad_ref, sigma_ref, start, decay, tiles, steps, True)


BLOCK = 88


def row_blocks(length, body):
    @pl.loop(0, length // BLOCK)
    def _(i):
        body(pl.ds(pl.multiple_of(i * BLOCK, 8), BLOCK))


def fill_drive(proj_ref, drive_ref, mean, inverse, gain, shift, tiles):
    scale = inverse * gain * LOG2E
    offset = shift * LOG2E

    def body(rows):
        for j, c, _ in tiles:
            at = slice(c, c + LANE)
            drive_ref[j, rows, :] = (proj_ref[rows, at] - mean[:, at]) * scale[:, at] + offset[:, at]

    row_blocks(proj_ref.shape[0], body)


def fill_sigma(drive_ref, prev_ref, decay_row, tiles, length):
    u2 = decay_row * LOG2E

    def body(i, _):
        for j, c, _w in tiles:
            rows = pl.ds(pl.multiple_of(i * BLOCK, 8), BLOCK)
            before = drive_ref[j, rows, :] + u2[:, c : c + LANE] * prev_ref[j, pl.ds(i * BLOCK + 7, BLOCK), :]
            drive_ref[j, rows, :] = 1.0 / (1.0 + jnp.exp2(-before))
        return 0

    lax.fori_loop(0, length // BLOCK, body, 0)


def finish_back(grad_ref, state_ref, proj_ref, mean, inverse, tiles, gb_ref, sums_ref):
    length, width = proj_ref.shape
    zero = tuple(jnp.zeros((1, LANE), F32) for _ in tiles)

    def body(i, carry):
        shift, gain, decay = (list(x) for x in carry)
        rows = pl.ds(pl.multiple_of(i * BLOCK, 8), BLOCK)
        for j, c, _w in tiles:
            at = slice(c, c + LANE)
            gb = grad_ref[j, rows, :]
            gb_ref[rows, at] = gb
            shift[j] = shift[j] + jnp.sum(gb, axis=0, keepdims=True)
            gain[j] = gain[j] + jnp.sum(gb * (proj_ref[rows, at] - mean[:, at]), axis=0, keepdims=True)
            decay[j] = decay[j] + jnp.sum(
                gb * state_ref[j, pl.ds(i * BLOCK + 7, BLOCK), :], axis=0, keepdims=True
            )
        return tuple(shift), tuple(gain), tuple(decay)

    shift, gain, decay = lax.fori_loop(0, length // BLOCK, body, (zero, zero, zero))
    for j, c, _ in tiles:
        at = slice(c, c + LANE)
        scaled = gain[j] * inverse[:, at]
        for p in range(sums_ref.shape[0]):
            sums_ref[p, 0:1, at] = shift[j]
            sums_ref[p, 1:2, at] = scaled
            sums_ref[p, 2:3, at] = decay[j]


def clear(state_ref, tiles):
    for j, _, _ in tiles:
        state_ref[j, 0:8, :] = jnp.zeros((8, LANE), F32)


def put_states(state_ref, out_ref, tiles, wide_ref=None):
    def body(i, _):
        rows = pl.ds(pl.multiple_of(i * 16, 16), 16)
        for j, c, w in tiles:
            s = state_ref[j, pl.ds(pl.multiple_of(8 + i * 16, 8), 16), :]
            out_ref[rows, c : c + w] = s[:, :w].astype(BF16)
            if wide_ref is not None:
                wide_ref[rows, c : c + LANE] = s
        return 0

    lax.fori_loop(0, out_ref.shape[0] // 16, body, 0, unroll=4)


def forward_kernel(stats_ref, proj_ref, par_ref, out_ref, wide_ref, sum_ref, drive, state):
    length, width = proj_ref.shape
    tiles = tiles_of(width)
    outs = tiles_of(out_ref.shape[1])
    mean, var, inverse = merged(stats_ref, length, sum_ref)
    gain, shift, decay = par_ref[0:1, :], par_ref[1:2, :], par_ref[2:3, :]
    fill_drive(proj_ref, drive, mean, inverse, gain, shift, tiles)
    clear(state, tiles)
    solve(drive, state, decay, tiles)
    put_states(state, out_ref, outs, wide_ref)


def norm_kernel(proj_ref, sum_ref, norm_ref, total_ref):
    length = proj_ref.shape[0]
    mean, inverse = sum_ref[0:1, :], sum_ref[2:3, :]
    total_ref[...] = jnp.zeros(total_ref.shape, F32)
    total_ref[7:8, :] = length * (sum_ref[3:4, :] - mean) * inverse

    def body(i, _):
        rows = pl.ds(pl.multiple_of(i * 16, 16), 16)
        norm_ref[rows, :] = ((proj_ref[rows, :] - mean) * inverse).astype(BF16)
        return 0

    lax.fori_loop(0, length // 16, body, 0, unroll=4)


def turn_kernel(
    stats_ref,
    proj_ref,
    par_ref,
    first_ref,
    cot_hbm,
    rmean_hbm,
    rvar_hbm,
    out_ref,
    gb_ref,
    sums_ref,
    sum_ref,
    nmean_ref,
    nvar_ref,
    drive,
    state,
    grad,
    cot_ref,
    rmean_ref,
    rvar_ref,
    arrived,
):
    copies = [
        pltpu.make_async_copy(a, b, arrived.at[i])
        for i, (a, b) in enumerate(
            ((cot_hbm, cot_ref), (rmean_hbm, rmean_ref), (rvar_hbm, rvar_ref))
        )
    ]
    for copy in copies:
        copy.start()
    length, width = proj_ref.shape
    tiles = tiles_of(width)
    outs = tiles_of(out_ref.shape[1])
    mean, var, inverse = merged(stats_ref, length, sum_ref)
    gain, shift, decay = par_ref[0:1, :], par_ref[1:2, :], par_ref[2:3, :]
    real = out_ref.shape[1]
    count = float(stats_ref.shape[0] * length)
    fill_drive(proj_ref, drive, mean, inverse, gain, shift, tiles)
    clear(state, tiles)
    solve(drive, state, decay, tiles)
    put_states(state, out_ref, outs)
    fill_sigma(drive, state, decay, tiles, length)
    for copy in copies:
        copy.wait()
    for row, m, v in ((0, first_ref[0:1, :], first_ref[1:2, :]), (1, mean, var)):
        nmean_ref[row : row + 1, :] = (1.0 - MOMENTUM) * rmean_ref[row : row + 1, :] + MOMENTUM * m[:, :real]
        nvar_ref[row : row + 1, :] = (1.0 - MOMENTUM) * rvar_ref[row : row + 1, :] + (
            MOMENTUM * v[:, :real]
        ) * (count / (count - 1.0))
    for j, _, w in outs:
        if w < LANE:
            grad[j] = jnp.zeros(grad.shape[1:], F32)

    def load_cot(i, _):
        rows = pl.ds(pl.multiple_of(i * 16, 16), 16)
        for j, c, w in outs:
            grad[j, rows, :w] = cot_ref[rows, c : c + w].astype(F32)
        return 0

    lax.fori_loop(0, length // 16, load_cot, 0, unroll=4)
    solve_back(grad, drive, decay, tiles)
    finish_back(grad, state, proj_ref, mean, inverse, tiles, gb_ref, sums_ref)


def back_kernel(
    keep_ref, got_ref, proj_ref, wide_ref, sum_ref, par_ref, gb_ref, sums_ref, own_ref, drive, state, grad
):
    length, width = proj_ref.shape
    tiles = tiles_of(width)
    mean, inverse = sum_ref[0:1, :], sum_ref[2:3, :]
    gain, shift, decay = par_ref[0:1, :], par_ref[1:2, :], par_ref[2:3, :]
    fill_drive(proj_ref, drive, mean, inverse, gain, shift, tiles)
    clear(state, tiles)

    def load(i, _):
        rows = pl.ds(pl.multiple_of(i * 16, 16), 16)
        for j, c, _w in tiles:
            at = slice(c, c + LANE)
            grad[j, rows, :] = keep_ref[rows, at] + got_ref[rows, at].astype(F32)
            state[j, pl.ds(pl.multiple_of(8 + i * 16, 8), 16), :] = wide_ref[rows, at]
        return 0

    lax.fori_loop(0, length // 16, load, 0, unroll=4)
    fill_sigma(drive, state, decay, tiles, length)
    solve_back(grad, drive, decay, tiles)
    finish_back(grad, state, proj_ref, mean, inverse, tiles, gb_ref, sums_ref)
    scale = gain * inverse
    average = sums_ref[0, 0:1, :] * (1.0 / length)

    def put_own(i, _):
        rows = pl.ds(pl.multiple_of(i * 16, 16), 16)
        own_ref[rows, :] = (scale * (gb_ref[rows, :] - average)).astype(BF16)
        return 0

    lax.fori_loop(0, length // 16, put_own, 0, unroll=4)


def total_of(sums_ref):
    peers = sums_ref.shape[0]
    out = sums_ref[0]
    for p in range(1, peers):
        out = out + sums_ref[p]
    return out


def grad_kernel(sums_ref, gb_ref, proj_ref, sum_ref, par_ref, g_ref, total_ref):
    length, _ = proj_ref.shape
    total = total_of(sums_ref)
    total_ref[...] = total
    count = float(sums_ref.shape[0] * length)
    mean, inverse = sum_ref[0:1, :], sum_ref[2:3, :]
    scale = par_ref[0:1, :] * inverse
    base = total[0:1, :] * (1.0 / count)
    lean = total[1:2, :] * (1.0 / count) * inverse

    total_ref[7:8, :] = scale * (
        sums_ref[lax.axis_index("seq"), 0:1, :]
        - length * base
        - length * (sum_ref[3:4, :] - mean) * lean
    )

    def body(i, _):
        rows = pl.ds(pl.multiple_of(i * 16, 16), 16)
        g_ref[rows, :] = (
            scale * (gb_ref[rows, :] - base - (proj_ref[rows, :] - mean) * lean)
        ).astype(BF16)
        return 0

    lax.fori_loop(0, length // 16, body, 0, unroll=4)


def send_kernel(g_ref, mate_ref, w_ref, wmate_ref, out_ref):
    here = lax.axis_index("neur")
    for c in range(0, out_ref.shape[1], 256):
        at = slice(c, c + 256)
        out_ref[:, at] = (
            dot_nt(g_ref[...], w_ref[here ^ 2, at, :]) + dot_nt(mate_ref[...], wmate_ref[1, at, :])
        ).astype(BF16)


def keep_kernel(g_ref, mate_ref, w_ref, wmate_ref, out_ref):
    here = lax.axis_index("neur")
    for c in range(0, out_ref.shape[1], 256):
        at = slice(c, c + 256)
        out_ref[:, at] = dot_nt(g_ref[...], w_ref[here, at, :]) + dot_nt(
            mate_ref[...], wmate_ref[0, at, :]
        )


def split(row):
    high = row.astype(BF16)
    return high, (row - high.astype(F32)).astype(BF16)


def dot_tn(a, b):
    return lax.dot_general(a, b, (((0,), (0,)), ((), ())), preferred_element_type=F32)


def outer(a, b):
    (a_high, a_low), (b_high, b_low) = split(a), split(b)
    return dot_tn(
        jnp.concatenate([a_high, a_high, a_low, a_low]), jnp.concatenate([b_high, b_low, b_high, b_low])
    )


def weight_kernel(parted, own_ref, mate_ref, far_ref, cross_ref, g_ref, sum_ref, total_ref, *refs):
    outs, hold = (refs[:-1], refs[-1]) if parted else ((), refs[0])
    place = seat() if parted else 0
    _, half, width = hold.shape
    for k, x_ref in enumerate((own_ref, mate_ref, far_ref, cross_ref)):
        real = x_ref.shape[1]
        mean = sum_ref[4 + k : 5 + k, :real]
        part = (dot_tn(x_ref[...], g_ref[...]) - outer(mean, total_ref[7:8, :])).astype(BF16)
        hold[(2 * k) ^ place] = part[:half]
        rest = part[half:]
        hold[(2 * k + 1) ^ place, : rest.shape[0], :] = rest
        if not parted:
            hold[2 * k + 1, rest.shape[0] :, :] = jnp.zeros((half - rest.shape[0], width), BF16)
    if parted:
        left, right = slice(0, half), slice(half, width)
        for out, shares, at in zip(
            outs, ((0, 1, 2, 3), (4, 5, 6, 7), (0, 1, 4, 5), (2, 3, 6, 7)), (left, left, right, right)
        ):
            for i, r in enumerate(shares):
                out[i] = hold[r, :, at]


def halve_kernel(left_ref, got_left_ref, right_ref, got_right_ref, *outs):
    for n, (keep, got) in enumerate(((left_ref, got_left_ref), (right_ref, got_right_ref))):
        mine, give = outs[2 * n : 2 * n + 2]
        for i in range(2):
            mine[i] = wide_sum(keep[i], got[i])
            give[i] = half_sum(keep[i + 2], got[i + 2])


def settle_kernel(
    length,
    left_ref,
    got_left_ref,
    right_ref,
    got_right_ref,
    lean_left_ref,
    lean_got_left_ref,
    lean_right_ref,
    lean_got_right_ref,
    sums_ref,
    stats_ref,
    sum_ref,
    par_ref,
    *outs,
):
    peers = sums_ref.shape[0]
    total = total_of(sums_ref)
    base = total[0:1, :] * (1.0 / (peers * length))
    scale = par_ref[0:1, :] * sum_ref[2:3, :]
    lean = scale * total[1:2, :] * (1.0 / (peers * length))
    place, here = lax.axis_index("seq"), seat()
    half = left_ref.shape[1]
    for n, (keep, got, lean_keep, lean_got, other, shares, at) in enumerate((
        (left_ref, got_left_ref, lean_left_ref, lean_got_left_ref, place ^ LEVEL[4], (0, 1, 2, 3), slice(0, half)),
        (right_ref, got_right_ref, lean_right_ref, lean_got_right_ref, place ^ LEVEL[2], (0, 1, 4, 5), slice(half, 2 * half)),
    )):
        mine, give = outs[2 * n : 2 * n + 2]
        columns = [
            (scale * (sums_ref[p, 0:1, :] * (1.0 / length) - base) * length)[:, at] for p in (place, other)
        ]
        for i, r in enumerate(shares):
            share = here ^ r
            row, low = share >> 1, pl.multiple_of((share & 1) * half, 128)
            middle = sum_ref[pl.ds(4 + row, 1), pl.ds(low, half)]
            value = wide_sum(keep[i], got[i]) - lean[:, at] * wide_sum(lean_keep[i], lean_got[i])
            for p, column in zip((place, other), columns):
                value = value + outer(stats_ref[p, pl.ds(2 + row, 1), pl.ds(low, half)] - middle, column)
            if i < 2:
                mine[i] = value
            else:
                give[i - 2] = value.astype(BF16)


def quarter_kernel(left_ref, got_left_ref, right_ref, got_right_ref, mine_ref, give_ref):
    edge = left_ref.shape[2]
    for keep, got, at in (
        (left_ref, got_left_ref, slice(0, edge)),
        (right_ref, got_right_ref, slice(edge, 2 * edge)),
    ):
        mine_ref[:, at] = wide_sum(keep[0], got[0])
        give_ref[:, at] = half_sum(keep[1], got[1])


def spread_kernel(parted, *refs):
    if parted:
        shares, out_ref, hold = refs[:-2], refs[-2], refs[-1]
        for r, share in enumerate(shares):
            hold[r] = share[...]
    else:
        hold, out_ref = refs
    place, here = seat() if parted else 0, lax.axis_index("neur")
    half = hold.shape[1]
    block = out_ref.shape[0] // 4
    width = out_ref.shape[1]
    for b in range(4):
        for h in range(2):
            low, high = b * block + h * half, min(b * block + h * half + half, (b + 1) * block)
            which = (((here ^ b) * 2) + h) ^ place
            out_ref[low:high, :] = hold[which, : high - low, :width].astype(F32)


def wide_sum(a, b):
    return a.astype(F32) + b.astype(F32)


def half_sum(a, b):
    return wide_sum(a, b).astype(BF16)


def swap(x, bit, axis="seq"):
    n = lax.axis_size(axis)
    return lax.ppermute(x, axis, [(i, i ^ bit) for i in range(n)])


LEVEL = {4: 1, 2: 2, 1: 4}


def seat():
    place = lax.axis_index("seq")
    return ((place & 1) << 2) | (place & 2) | ((place >> 2) & 1)


def gather_first(v):
    return {0: v, 4: swap(v, LEVEL[4]), 2: swap(v, LEVEL[2]), 1: swap(v, LEVEL[1])}


def gather_rest(out):
    out = dict(out)
    out[2], out[4] = lax.optimization_barrier((out[2], out[4]))
    out[6] = swap(out[2], LEVEL[4])
    out[5] = swap(out[1], LEVEL[4])
    out[3] = swap(out[1], LEVEL[2])
    out[3], out[6] = lax.optimization_barrier((out[3], out[6]))
    out[7] = swap(out[3], LEVEL[4])
    return [out[r] for r in range(8)]


def per_device(devices_seq, *args):
    (
        tokens,
        w_first,
        gain_first,
        shift_first,
        decay_first,
        w_second,
        gain_second,
        shift_second,
        decay_second,
        cotangent,
        running_mean,
        running_var,
    ) = args
    _, length, real = tokens.shape
    width = -(-real // LANE) * LANE
    tiles = len(tiles_of(width))
    peers = devices_seq
    here = lax.axis_index("neur")
    tokens, cotangent = tokens[0], cotangent[0]

    scans = [
        pltpu.VMEM((tiles, length, LANE), F32),
        pltpu.VMEM((tiles, length + 8, LANE), F32),
    ]
    grads = [pltpu.VMEM((tiles, length, LANE), F32)]

    def share(stats):
        return lax.all_to_all(stats, "seq", 0, 0, tiled=True)

    def project(own, w, rows, *gives, aside=None):
        far = swap(own, 2, "neur")
        mate = swap(own, 1, "neur")
        w = lax.optimization_barrier((w, own))[0]
        w4, give, par = call(
            block_kernel,
            [shape(4, width, width, dtype=BF16), shape(2, width, width, dtype=BF16), shape(8, width)],
        )(w, *(row[None] for row in rows))
        part, means = call(project_early, [shape(length, width), shape(8, width)])(own, mate, w4)
        gives = [swap(lax.optimization_barrier((g, own))[0], 1, "neur") for g in gives + (give,)] if gives else give
        extra = aside(mate) if aside else ()
        far, part, par, gives, extra = lax.optimization_barrier((far, part, par, gives, extra))
        cross = swap(far, 1, "neur")
        part, means = call(project_middle, [shape(length, width), shape(8, width)])(part, means, far, w4)
        proj, stats = call(project_late, [shape(length, width), shape(peers, 8, width)])(
            part, means, cross, w4
        )
        return (own, mate, far, cross), proj, share(stats), w4, gives, par, extra

    def gradient(sums, gb, proj, summary, par):
        return call(grad_kernel, [shape(length, width, dtype=BF16), shape(8, width)])(
            sums, gb, proj, summary, par
        )

    def send(g, mate, w4, wm):
        out = call(send_kernel, shape(length, width, dtype=BF16))(g, mate, w4, wm)
        out, g, mate = lax.optimization_barrier((out, g, mate))
        got = swap(out, 2, "neur")
        keep = call(keep_kernel, shape(length, width))(g, mate, w4, wm)
        return keep, got

    half = width // 2

    def parts_shape(*lead):
        return shape(*lead, half, width, dtype=BF16)

    def weight_parts(*operands):
        if peers != 8:
            return call(functools.partial(weight_kernel, False), parts_shape(8))(*operands)
        return call(
            functools.partial(weight_kernel, True),
            [shape(4, half, half, dtype=BF16)] * 4,
            [pltpu.VMEM((8, half, width), BF16)],
        )(*operands)

    def weights(shares):
        if peers != 8:
            return call(functools.partial(spread_kernel, False), shape(4 * real, real))(shares)
        return call(
            functools.partial(spread_kernel, True),
            shape(4 * real, real),
            [pltpu.VMEM((8, half, width), BF16)],
        )(*shares)

    def together(*values):
        return lax.optimization_barrier(values)

    first_x, first_proj, first_stats, first_w, give, first_par, _ = project(
        tokens, w_first, (gain_first, shift_first, decay_first)
    )
    first_out, first_wide, first_sum = call(
        forward_kernel,
        [shape(length, real, dtype=BF16), shape(length, width), shape(8, width)],
        scans,
    )(first_stats, first_proj, first_par)

    def after(x, *earlier):
        return lax.optimization_barrier((x, earlier))[0]

    def leaning(mate):
        if peers != 8:
            return ()
        norm, norm_total = call(norm_kernel, [shape(length, width, dtype=BF16), shape(8, width)])(
            first_proj, after(first_sum, mate)
        )
        left, give_left, right, give_right = weight_parts(*first_x, norm, first_sum, norm_total)
        return left, swap(give_left, LEVEL[4]), right, swap(give_right, LEVEL[2])

    second_x, second_proj, second_stats, second_w, (first_mate, second_mate), second_par, lean = project(
        first_out, w_second, (gain_second, shift_second, decay_second), give, aside=leaning
    )
    second_out, second_gb, second_sums, second_sum, new_mean, new_var = call(
        turn_kernel,
        [
            shape(length, real, dtype=BF16),
            shape(length, width),
            shape(peers, 8, width),
            shape(8, width),
            shape(2, real),
            shape(2, real),
        ],
        scans
        + grads
        + [
            pltpu.VMEM((length, real), BF16),
            pltpu.VMEM((2, real), F32),
            pltpu.VMEM((2, real), F32),
            pltpu.SemaphoreType.DMA((3,)),
        ],
        in_specs=[pl.BlockSpec(memory_space=pltpu.VMEM)] * 4 + [pl.BlockSpec(memory_space=pl.ANY)] * 3,
    )(second_stats, second_proj, second_par, first_sum, cotangent, running_mean, running_var)

    second_sums = share(second_sums)
    second_g, second_total = gradient(second_sums, second_gb, second_proj, second_sum, second_par)
    mate = swap(second_g, 1, "neur")
    pairs = [shape(2, half, half), shape(2, half, half, dtype=BF16)] * 2
    rest = [shape(half, width), parts_shape()]
    second_parts = weight_parts(*second_x, second_g, second_sum, second_total)
    mate, second_parts = together(mate, second_parts)
    keep, got = send(second_g, mate, second_w, second_mate)
    if peers == 8:
        left, give_left, right, give_right = second_parts
        parcel = after((swap(give_left, LEVEL[4]), swap(give_right, LEVEL[2])), keep)
        left, give_left, right, give_right = call(halve_kernel, pairs)(left, parcel[0], right, parcel[1])
        keep, got, left = together(keep, got, left)
        parcel = swap(give_left, LEVEL[2]), swap(give_right, LEVEL[4])
    first_gb, first_sums, first_own = call(
        back_kernel,
        [shape(length, width), shape(peers, 8, width), shape(length, width, dtype=BF16)],
        scans + grads,
    )(keep, got, first_proj, first_wide, first_sum, first_par)
    if peers == 8:
        second_mine, give = call(quarter_kernel, rest)(left, parcel[0], right, parcel[1])
        first_sums, second_mine, give = together(first_sums, second_mine, give)
        left, give_left, right, give_right = weight_parts(
            *first_x, first_own, first_sum, jnp.zeros((8, width), F32)
        )
        parcel = swap(give_left, LEVEL[4]), swap(give_right, LEVEL[2])
    first_sums = share(first_sums)
    if peers == 8:
        first_sums, last, parcel = together(first_sums, swap(give, LEVEL[1]), parcel)
    first_g, first_total = gradient(first_sums, first_gb, first_proj, first_sum, first_par)
    mate = swap(first_g, 1, "neur")
    if peers == 8:
        left, give_left, right, give_right = call(functools.partial(settle_kernel, length), pairs)(
            left, parcel[0], right, parcel[1], *lean, first_sums, first_stats, first_sum, first_par
        )
        parcel = swap(give_left, LEVEL[2]), swap(give_right, LEVEL[4])
        mate, left = together(mate, left)
        keep, got = send(first_g, mate, first_w, first_mate)
        second_share = gather_first(half_sum(second_mine, last))
        mine, give = call(quarter_kernel, rest)(left, parcel[0], right, parcel[1])
        keep, first_share = together(keep, half_sum(mine, swap(give, LEVEL[1])))
        second_share = gather_rest(second_share)
        first_share = gather_rest(gather_first(first_share))
    else:
        first_parts = weight_parts(*first_x, first_g, first_sum, first_total)
        keep, got = send(first_g, mate, first_w, first_mate)
        second_share, first_share = lax.psum((second_parts, first_parts), "seq")
    grad_w_first = weights(first_share)
    grad_w_second = weights(second_share)
    input_grad = (keep + got.astype(F32))[:, :real]

    def pair(row):
        return jnp.stack([first_total[row, :real], second_total[row, :real]])

    return (
        first_out[None],
        second_out[None],
        input_grad[None],
        grad_w_first,
        grad_w_second,
        pair(1),
        pair(0),
        pair(2),
        new_mean,
        new_var,
    )


def solution(mesh):
    rows, line, flat = P("seq", None, "neur"), P("neur"), P(None, "neur")
    return jax.shard_map(
        functools.partial(per_device, mesh.shape["seq"]),
        mesh=mesh,
        in_specs=(rows, flat, line, line, line, flat, line, line, line, rows, flat, flat),
        out_specs=(rows, rows, rows) + (flat,) * 7,
        check_vma=False,
    )
```

```python
import functools
import math

import jax
import jax.numpy as jnp
from jax import lax
from jax.experimental import pallas as pl
from jax.experimental.pallas import tpu as pltpu
from jax.sharding import PartitionSpec as P

EPSILON = 1e-05
MOMENTUM = 0.1
LANE = 128
CHUNKS = 32
GROUPS = CHUNKS // 8
TOLERANCE = 2e-5
LOG2E = math.log2(math.e)
LN2 = math.log(2.0)
F32 = jnp.float32
BF16 = jnp.bfloat16
VMEM_BYTES = 16 * 1024 * 1024


def call(kernel, outs, scratch=(), **specs):
    return pl.pallas_call(
        kernel,
        **specs,
        out_shape=outs,
        scratch_shapes=list(scratch),
        compiler_params=pltpu.CompilerParams(vmem_limit_bytes=VMEM_BYTES),
    )


def shape(*dims, dtype=F32):
    return jax.ShapeDtypeStruct(dims, dtype)


def tiles_of(width):
    return [(j, j * LANE, min(LANE, width - j * LANE)) for j in range(-(-width // LANE))]


def dot(a, b):
    return jnp.dot(a, b, preferred_element_type=F32)


def dot_nt(a, b):
    return lax.dot_general(a, b, (((1,), (1,)), ((), ())), preferred_element_type=F32)


def block_kernel(w_ref, gain_ref, shift_ref, decay_ref, out_ref, mate_ref, par_ref):
    here = lax.axis_index("neur")
    blocks, width, _ = out_ref.shape
    real = w_ref.shape[0] // blocks
    out_ref[...] = jnp.zeros(out_ref.shape, BF16)
    for b in range(blocks):
        out_ref[b, :real, : w_ref.shape[1]] = w_ref[b * real : (b + 1) * real, :]
    for i, k in enumerate((1, 3)):
        mate_ref[i] = out_ref[here ^ k]
    par_ref[...] = jnp.zeros(par_ref.shape, F32)
    for i, row_ref in enumerate((gain_ref, shift_ref, decay_ref)):
        par_ref[i : i + 1, : row_ref.shape[1]] = row_ref[...]


def means_of(x_ref):
    length = x_ref.shape[0]
    return dot(jnp.ones((16, length), BF16), x_ref[...])[:1] * (1.0 / length)


def project_early(own_ref, mate_ref, w_ref, part_ref, means_ref):
    here = lax.axis_index("neur")
    k = own_ref.shape[1]
    means_ref[...] = jnp.zeros(means_ref.shape, F32)
    means_ref[0:1, :k] = means_of(own_ref)
    means_ref[1:2, :k] = means_of(mate_ref)
    for c in range(0, part_ref.shape[1], 256):
        part_ref[:, c : c + 256] = dot(own_ref[...], w_ref[here, :k, c : c + 256]) + dot(
            mate_ref[...], w_ref[here ^ 1, :k, c : c + 256]
        )


def project_middle(part_ref, means_ref, far_ref, w_ref, out_ref, out_means_ref):
    here = lax.axis_index("neur")
    k = far_ref.shape[1]
    out_means_ref[...] = means_ref[...]
    out_means_ref[2:3, :k] = means_of(far_ref)
    for c in range(0, part_ref.shape[1], 256):
        out_ref[:, c : c + 256] = part_ref[:, c : c + 256] + dot(
            far_ref[...], w_ref[here ^ 2, :k, c : c + 256]
        )


def project_late(part_ref, means_ref, cross_ref, w_ref, proj_ref, stats_ref):
    here = lax.axis_index("neur")
    k = cross_ref.shape[1]
    peers, _, width = stats_ref.shape
    cross = means_of(cross_ref)
    for p in range(peers):
        stats_ref[p, 2:8, :] = means_ref[0:6, :]
        stats_ref[p, 5:6, :k] = cross
    length = proj_ref.shape[0]
    for c in range(0, part_ref.shape[1], 256):
        y = part_ref[:, c : c + 256] + dot(cross_ref[...], w_ref[here ^ 3, :k, c : c + 256])
        proj_ref[:, c : c + 256] = y
        mean = jnp.sum(y, axis=0, keepdims=True) * (1.0 / length)
        off = y - mean
        spread = jnp.sum(off * off, axis=0, keepdims=True)
        for p in range(stats_ref.shape[0]):
            stats_ref[p, 0:1, c : c + 256] = mean
            stats_ref[p, 1:2, c : c + 256] = spread


def merged(stats_ref, length, sum_ref):
    peers = stats_ref.shape[0]
    means = [stats_ref[p, 0:1, :] for p in range(peers)]
    mean = sum(means[1:], means[0]) * (1.0 / peers)
    total = None
    for p in range(peers):
        off = means[p] - mean
        term = stats_ref[p, 1:2, :] + off * off * float(length)
        total = term if total is None else total + term
    var = total * (1.0 / (peers * length))
    inverse = lax.rsqrt(var + EPSILON)
    features = stats_ref[0, 2:6, :]
    for p in range(1, peers):
        features = features + stats_ref[p, 2:6, :]
    sum_ref[0:1, :] = mean
    sum_ref[1:2, :] = var
    sum_ref[2:3, :] = inverse
    sum_ref[3:4, :] = stats_ref[lax.axis_index("seq"), 0:1, :]
    sum_ref[4:8, :] = features * (1.0 / peers)
    return mean, var, inverse


def spread_rows(row, tiles):
    return [jnp.broadcast_to(row[:, c : c + LANE], (8, LANE)) for _, c, _ in tiles]


def load_step(ref, step, tiles, lead=0):
    steps = (ref.shape[1] - lead) // CHUNKS
    return [
        ref[j, pl.ds(lead + step + g * 8 * steps, 8, stride=steps), :]
        for j, _, _ in tiles
        for g in range(GROUPS)
    ]


def store_step(ref, step, tiles, values, lead=0):
    steps = (ref.shape[1] - lead) // CHUNKS
    i = 0
    for j, _, _ in tiles:
        for g in range(GROUPS):
            ref[j, pl.ds(lead + step + g * 8 * steps, 8, stride=steps), :] = values[i]
            i += 1


def rows_before(x, k, fill):
    at = lax.broadcasted_iota(jnp.int32, x.shape, 0)
    return jnp.where(at >= k, pltpu.roll(x, k, axis=0), fill)


def rows_after(x, k, fill):
    at = lax.broadcasted_iota(jnp.int32, x.shape, 0)
    return jnp.where(at < 8 - k, pltpu.roll(x, 8 - k, axis=0), fill)


def whole_row(x, i):
    return jnp.broadcast_to(x[i : i + 1, :], x.shape)


def chain(base, slope, floor=None, back=False):
    shifted, last, first = (rows_after, 0, 7) if back else (rows_before, 7, 0)
    starts = [None] * GROUPS
    carry = jnp.zeros((8, LANE), F32)
    for g in reversed(range(GROUPS)) if back else range(GROUPS):
        b, q, f = base[g], slope[g], None if floor is None else floor[g]
        for k in (1, 2, 4):
            early = shifted(b, k, 0.0)
            if f is not None:
                f = jnp.maximum(f, b + q * shifted(f, k, 0.0))
            b = b + q * early
            q = q * shifted(q, k, 1.0)
        ends = b + q * carry
        if f is not None:
            ends = jnp.maximum(ends, f)
        starts[g] = jnp.where(
            lax.broadcasted_iota(jnp.int32, ends.shape, 0) == first, carry, shifted(ends, 1, 0.0)
        )
        carry = whole_row(ends, last)
    return starts


def by_tile(tiles, run, *lists):
    out = []
    for n in range(len(tiles)):
        out += run(*(x[n * GROUPS : (n + 1) * GROUPS] for x in lists))
    return out


def handed_on(ends):
    out, carry = [], jnp.zeros((8, LANE), F32)
    for x in ends:
        out.append(jnp.where(lax.broadcasted_iota(jnp.int32, x.shape, 0) == 0, carry, rows_before(x, 1, 0.0)))
        carry = whole_row(x, 7)
    return out


def power(x, n):
    out = None
    while n:
        if n & 1:
            out = x if out is None else out * x
        x = x * x
        n >>= 1
    return out


def softplus2(before):
    return [jnp.where(b > 25.0, b * LN2, jnp.log(1.0 + jnp.exp2(b))) for b in before]


def run_bounds(drive_ref, decay, tiles, steps):
    u = [d for d in decay for _ in range(GROUPS)]
    u2 = [d * LOG2E for d in u]

    def body(step, carry):
        state, line = carry
        drive = load_step(drive_ref, step, tiles)
        line = [d + a * v for d, a, v in zip(drive, u, line)]
        state = softplus2([d + a * v for d, a, v in zip(drive, u2, state)])
        return state, line

    zero = [jnp.zeros((8, LANE), F32) for _ in u]
    state, line = lax.fori_loop(0, steps, body, (zero, zero), unroll=True)
    return state, [a * LN2 for a in line]


def run_chunks(drive_ref, state_ref, start, decay, tiles, steps):
    u2 = [d * LOG2E for d in decay for _ in range(GROUPS)]

    def body(step, carry):
        state, slope = carry
        drive = load_step(drive_ref, step, tiles)
        before = [d + u * s for d, u, s in zip(drive, u2, state)]
        state = softplus2(before)
        slope = [a + (b - s * LOG2E) for a, b, s in zip(slope, before, state)]
        store_step(state_ref, step, tiles, state, lead=8)
        return state, slope

    zero = [jnp.zeros((8, LANE), F32) for _ in start]
    state, slope = lax.fori_loop(0, steps, body, (start, zero), unroll=True)
    top = [power(d, steps) for d in decay for _ in range(GROUPS)]
    return state, [t * jnp.exp2(a) for t, a in zip(top, slope)]


def solve(drive_ref, state_ref, decay_row, tiles):
    steps = drive_ref.shape[1] // CHUNKS
    decay = spread_rows(decay_row, tiles)
    top = [power(d, steps) for d in decay for _ in range(GROUPS)]
    low, line = run_bounds(drive_ref, decay, tiles, steps)
    start = by_tile(tiles, lambda f, b, q: chain(b, q, f), low, line, top)

    def again(carry):
        count, worst, _ = carry
        return jnp.logical_and(worst > 0.0, count < CHUNKS + 1)

    def newton(carry):
        count, _, start = carry
        end, slope = run_chunks(drive_ref, state_ref, start, decay, tiles, steps)
        miss = [e - s for e, s in zip(by_tile(tiles, handed_on, end), start)]
        worst = None
        for m, s in zip(miss, start):
            over = jnp.abs(m) - TOLERANCE * jnp.maximum(s, 1.0)
            worst = over if worst is None else jnp.maximum(worst, over)

        def step(miss, slope, start):
            after = [
                jnp.where(
                    lax.broadcasted_iota(jnp.int32, m.shape, 0) == 7,
                    whole_row(miss[g + 1], 0) if g + 1 < GROUPS else 0.0,
                    rows_after(m, 1, 0.0),
                )
                for g, m in enumerate(miss)
            ]
            return [s + c for s, c in zip(start, chain(after, slope))]

        return count + 1, jnp.max(worst), by_tile(tiles, step, miss, slope, start)

    lax.while_loop(again, newton, (jnp.int32(0), jnp.float32(1.0), start))


def run_back(grad_ref, sigma_ref, start, decay, tiles, steps, store):
    u = [d for d in decay for _ in range(GROUPS)]

    def body(i, carry):
        z, prod = carry
        step = steps - 1 - i
        gs = load_step(grad_ref, step, tiles)
        sig = load_step(sigma_ref, step, tiles)
        z = [s * (g + a * v) for s, g, a, v in zip(sig, gs, u, z)]
        if store:
            store_step(grad_ref, step, tiles, z)
            return z, prod
        return z, [p * (s * a) for p, s, a in zip(prod, sig, u)]

    ones = [] if store else [jnp.ones((8, LANE), F32) for _ in start]
    return lax.fori_loop(0, steps, body, (start, ones), unroll=True)


def solve_back(grad_ref, sigma_ref, decay_row, tiles):
    steps = grad_ref.shape[1] // CHUNKS
    decay = spread_rows(decay_row, tiles)
    zero = [jnp.zeros((8, LANE), F32)] * (len(tiles) * GROUPS)
    end, slope = run_back(grad_ref, sigma_ref, zero, decay, tiles, steps, False)
    start = by_tile(tiles, lambda b, q: chain(b, q, back=True), end, slope)
    run_back(grad_ref, sigma_ref, start, decay, tiles, steps, True)


BLOCK = 88


def row_blocks(length, body):
    @pl.loop(0, length // BLOCK)
    def _(i):
        body(pl.ds(pl.multiple_of(i * BLOCK, 8), BLOCK))


def fill_drive(proj_ref, drive_ref, mean, inverse, gain, shift, tiles):
    scale = inverse * gain * LOG2E
    offset = shift * LOG2E

    def body(rows):
        for j, c, _ in tiles:
            at = slice(c, c + LANE)
            drive_ref[j, rows, :] = (proj_ref[rows, at] - mean[:, at]) * scale[:, at] + offset[:, at]

    row_blocks(proj_ref.shape[0], body)


def fill_sigma(drive_ref, prev_ref, decay_row, tiles, length):
    u2 = decay_row * LOG2E

    def body(i, _):
        for j, c, _w in tiles:
            rows = pl.ds(pl.multiple_of(i * BLOCK, 8), BLOCK)
            before = drive_ref[j, rows, :] + u2[:, c : c + LANE] * prev_ref[j, pl.ds(i * BLOCK + 7, BLOCK), :]
            drive_ref[j, rows, :] = 1.0 / (1.0 + jnp.exp2(-before))
        return 0

    lax.fori_loop(0, length // BLOCK, body, 0, unroll=2)


def finish_back(grad_ref, state_ref, proj_ref, mean, inverse, tiles, gb_ref, sums_ref):
    length, width = proj_ref.shape
    zero = tuple(jnp.zeros((1, LANE), F32) for _ in tiles)

    def body(i, carry):
        shift, gain, decay = (list(x) for x in carry)
        rows = pl.ds(pl.multiple_of(i * BLOCK, 8), BLOCK)
        for j, c, _w in tiles:
            at = slice(c, c + LANE)
            gb = grad_ref[j, rows, :]
            gb_ref[rows, at] = gb
            shift[j] = shift[j] + jnp.sum(gb, axis=0, keepdims=True)
            gain[j] = gain[j] + jnp.sum(gb * (proj_ref[rows, at] - mean[:, at]), axis=0, keepdims=True)
            decay[j] = decay[j] + jnp.sum(
                gb * state_ref[j, pl.ds(i * BLOCK + 7, BLOCK), :], axis=0, keepdims=True
            )
        return tuple(shift), tuple(gain), tuple(decay)

    shift, gain, decay = lax.fori_loop(0, length // BLOCK, body, (zero, zero, zero), unroll=2)
    for j, c, _ in tiles:
        at = slice(c, c + LANE)
        scaled = gain[j] * inverse[:, at]
        for p in range(sums_ref.shape[0]):
            sums_ref[p, 0:1, at] = shift[j]
            sums_ref[p, 1:2, at] = scaled
            sums_ref[p, 2:3, at] = decay[j]


def clear(state_ref, tiles):
    for j, _, _ in tiles:
        state_ref[j, 0:8, :] = jnp.zeros((8, LANE), F32)


def put_states(state_ref, out_ref, tiles, wide_ref=None):
    def body(i, _):
        rows = pl.ds(pl.multiple_of(i * 16, 16), 16)
        for j, c, w in tiles:
            s = state_ref[j, pl.ds(pl.multiple_of(8 + i * 16, 8), 16), :]
            out_ref[rows, c : c + w] = s[:, :w].astype(BF16)
            if wide_ref is not None:
                wide_ref[rows, c : c + LANE] = s
        return 0

    lax.fori_loop(0, out_ref.shape[0] // 16, body, 0, unroll=4)


def forward_kernel(stats_ref, proj_ref, par_ref, out_ref, wide_ref, sum_ref, drive, state):
    length, width = proj_ref.shape
    tiles = tiles_of(width)
    outs = tiles_of(out_ref.shape[1])
    mean, var, inverse = merged(stats_ref, length, sum_ref)
    gain, shift, decay = par_ref[0:1, :], par_ref[1:2, :], par_ref[2:3, :]
    fill_drive(proj_ref, drive, mean, inverse, gain, shift, tiles)
    clear(state, tiles)
    solve(drive, state, decay, tiles)
    put_states(state, out_ref, outs, wide_ref)


def norm_kernel(proj_ref, sum_ref, norm_ref, total_ref):
    length = proj_ref.shape[0]
    mean, inverse = sum_ref[0:1, :], sum_ref[2:3, :]
    total_ref[...] = jnp.zeros(total_ref.shape, F32)
    total_ref[7:8, :] = length * (sum_ref[3:4, :] - mean) * inverse

    def body(i, _):
        rows = pl.ds(pl.multiple_of(i * 16, 16), 16)
        norm_ref[rows, :] = ((proj_ref[rows, :] - mean) * inverse).astype(BF16)
        return 0

    lax.fori_loop(0, length // 16, body, 0, unroll=4)


def turn_kernel(
    stats_ref,
    proj_ref,
    par_ref,
    first_ref,
    cot_hbm,
    rmean_hbm,
    rvar_hbm,
    out_ref,
    gb_ref,
    sums_ref,
    sum_ref,
    nmean_ref,
    nvar_ref,
    drive,
    state,
    grad,
    cot_ref,
    rmean_ref,
    rvar_ref,
    arrived,
):
    copies = [
        pltpu.make_async_copy(a, b, arrived.at[i])
        for i, (a, b) in enumerate(
            ((cot_hbm, cot_ref), (rmean_hbm, rmean_ref), (rvar_hbm, rvar_ref))
        )
    ]
    for copy in copies:
        copy.start()
    length, width = proj_ref.shape
    tiles = tiles_of(width)
    outs = tiles_of(out_ref.shape[1])
    mean, var, inverse = merged(stats_ref, length, sum_ref)
    gain, shift, decay = par_ref[0:1, :], par_ref[1:2, :], par_ref[2:3, :]
    real = out_ref.shape[1]
    count = float(stats_ref.shape[0] * length)
    fill_drive(proj_ref, drive, mean, inverse, gain, shift, tiles)
    clear(state, tiles)
    solve(drive, state, decay, tiles)
    put_states(state, out_ref, outs)
    fill_sigma(drive, state, decay, tiles, length)
    for copy in copies:
        copy.wait()
    for row, m, v in ((0, first_ref[0:1, :], first_ref[1:2, :]), (1, mean, var)):
        nmean_ref[row : row + 1, :] = (1.0 - MOMENTUM) * rmean_ref[row : row + 1, :] + MOMENTUM * m[:, :real]
        nvar_ref[row : row + 1, :] = (1.0 - MOMENTUM) * rvar_ref[row : row + 1, :] + (
            MOMENTUM * v[:, :real]
        ) * (count / (count - 1.0))
    for j, _, w in outs:
        if w < LANE:
            grad[j] = jnp.zeros(grad.shape[1:], F32)

    def load_cot(i, _):
        rows = pl.ds(pl.multiple_of(i * 16, 16), 16)
        for j, c, w in outs:
            grad[j, rows, :w] = cot_ref[rows, c : c + w].astype(F32)
        return 0

    lax.fori_loop(0, length // 16, load_cot, 0, unroll=4)
    solve_back(grad, drive, decay, tiles)
    finish_back(grad, state, proj_ref, mean, inverse, tiles, gb_ref, sums_ref)


def back_kernel(
    keep_ref, got_ref, proj_ref, wide_ref, sum_ref, par_ref, gb_ref, sums_ref, own_ref, drive, state, grad
):
    length, width = proj_ref.shape
    tiles = tiles_of(width)
    mean, inverse = sum_ref[0:1, :], sum_ref[2:3, :]
    gain, shift, decay = par_ref[0:1, :], par_ref[1:2, :], par_ref[2:3, :]
    fill_drive(proj_ref, drive, mean, inverse, gain, shift, tiles)
    clear(state, tiles)

    def load(i, _):
        rows = pl.ds(pl.multiple_of(i * 16, 16), 16)
        for j, c, _w in tiles:
            at = slice(c, c + LANE)
            grad[j, rows, :] = keep_ref[rows, at] + got_ref[rows, at].astype(F32)
            state[j, pl.ds(pl.multiple_of(8 + i * 16, 8), 16), :] = wide_ref[rows, at]
        return 0

    lax.fori_loop(0, length // 16, load, 0, unroll=4)
    fill_sigma(drive, state, decay, tiles, length)
    solve_back(grad, drive, decay, tiles)
    finish_back(grad, state, proj_ref, mean, inverse, tiles, gb_ref, sums_ref)
    scale = gain * inverse
    average = sums_ref[0, 0:1, :] * (1.0 / length)

    def put_own(i, _):
        rows = pl.ds(pl.multiple_of(i * 16, 16), 16)
        own_ref[rows, :] = (scale * (gb_ref[rows, :] - average)).astype(BF16)
        return 0

    lax.fori_loop(0, length // 16, put_own, 0, unroll=4)


def total_of(sums_ref):
    peers = sums_ref.shape[0]
    out = sums_ref[0]
    for p in range(1, peers):
        out = out + sums_ref[p]
    return out


def grad_kernel(sums_ref, gb_ref, proj_ref, sum_ref, par_ref, g_ref, total_ref):
    length, _ = proj_ref.shape
    total = total_of(sums_ref)
    total_ref[...] = total
    count = float(sums_ref.shape[0] * length)
    mean, inverse = sum_ref[0:1, :], sum_ref[2:3, :]
    scale = par_ref[0:1, :] * inverse
    base = total[0:1, :] * (1.0 / count)
    lean = total[1:2, :] * (1.0 / count) * inverse

    total_ref[7:8, :] = scale * (
        sums_ref[lax.axis_index("seq"), 0:1, :]
        - length * base
        - length * (sum_ref[3:4, :] - mean) * lean
    )

    def body(i, _):
        rows = pl.ds(pl.multiple_of(i * 16, 16), 16)
        g_ref[rows, :] = (
            scale * (gb_ref[rows, :] - base - (proj_ref[rows, :] - mean) * lean)
        ).astype(BF16)
        return 0

    lax.fori_loop(0, length // 16, body, 0, unroll=4)


def send_kernel(g_ref, mate_ref, w_ref, wmate_ref, out_ref):
    here = lax.axis_index("neur")
    for c in range(0, out_ref.shape[1], 256):
        at = slice(c, c + 256)
        out_ref[:, at] = (
            dot_nt(g_ref[...], w_ref[here ^ 2, at, :]) + dot_nt(mate_ref[...], wmate_ref[1, at, :])
        ).astype(BF16)


def keep_kernel(g_ref, mate_ref, w_ref, wmate_ref, out_ref):
    here = lax.axis_index("neur")
    for c in range(0, out_ref.shape[1], 256):
        at = slice(c, c + 256)
        out_ref[:, at] = dot_nt(g_ref[...], w_ref[here, at, :]) + dot_nt(
            mate_ref[...], wmate_ref[0, at, :]
        )


def split(row):
    high = row.astype(BF16)
    return high, (row - high.astype(F32)).astype(BF16)


def dot_tn(a, b):
    return lax.dot_general(a, b, (((0,), (0,)), ((), ())), preferred_element_type=F32)


def outer(a, b):
    (a_high, a_low), (b_high, b_low) = split(a), split(b)
    return dot_tn(
        jnp.concatenate([a_high, a_high, a_low, a_low]), jnp.concatenate([b_high, b_low, b_high, b_low])
    )


def weight_kernel(parted, own_ref, mate_ref, far_ref, cross_ref, g_ref, sum_ref, total_ref, *refs):
    outs, hold = (refs[:-1], refs[-1]) if parted else ((), refs[0])
    place = seat() if parted else 0
    _, half, width = hold.shape
    for k, x_ref in enumerate((own_ref, mate_ref, far_ref, cross_ref)):
        real = x_ref.shape[1]
        mean = sum_ref[4 + k : 5 + k, :real]
        part = (dot_tn(x_ref[...], g_ref[...]) - outer(mean, total_ref[7:8, :])).astype(BF16)
        hold[(2 * k) ^ place] = part[:half]
        rest = part[half:]
        hold[(2 * k + 1) ^ place, : rest.shape[0], :] = rest
        if not parted:
            hold[2 * k + 1, rest.shape[0] :, :] = jnp.zeros((half - rest.shape[0], width), BF16)
    if parted:
        left, right = slice(0, half), slice(half, width)
        for out, shares, at in zip(
            outs, ((0, 1, 2, 3), (4, 5, 6, 7), (0, 1, 4, 5), (2, 3, 6, 7)), (left, left, right, right)
        ):
            for i, r in enumerate(shares):
                out[i] = hold[r, :, at]


def halve_kernel(left_ref, got_left_ref, right_ref, got_right_ref, *outs):
    for n, (keep, got) in enumerate(((left_ref, got_left_ref), (right_ref, got_right_ref))):
        mine, give = outs[2 * n : 2 * n + 2]
        for i in range(2):
            mine[i] = wide_sum(keep[i], got[i])
            give[i] = half_sum(keep[i + 2], got[i + 2])


def settle_kernel(
    length,
    left_ref,
    got_left_ref,
    right_ref,
    got_right_ref,
    lean_left_ref,
    lean_got_left_ref,
    lean_right_ref,
    lean_got_right_ref,
    sums_ref,
    stats_ref,
    sum_ref,
    par_ref,
    *outs,
):
    peers = sums_ref.shape[0]
    total = total_of(sums_ref)
    base = total[0:1, :] * (1.0 / (peers * length))
    scale = par_ref[0:1, :] * sum_ref[2:3, :]
    lean = scale * total[1:2, :] * (1.0 / (peers * length))
    place, here = lax.axis_index("seq"), seat()
    half = left_ref.shape[1]
    for n, (keep, got, lean_keep, lean_got, other, shares, at) in enumerate((
        (left_ref, got_left_ref, lean_left_ref, lean_got_left_ref, place ^ LEVEL[4], (0, 1, 2, 3), slice(0, half)),
        (right_ref, got_right_ref, lean_right_ref, lean_got_right_ref, place ^ LEVEL[2], (0, 1, 4, 5), slice(half, 2 * half)),
    )):
        mine, give = outs[2 * n : 2 * n + 2]
        columns = [
            (scale * (sums_ref[p, 0:1, :] * (1.0 / length) - base) * length)[:, at] for p in (place, other)
        ]
        for i, r in enumerate(shares):
            share = here ^ r
            row, low = share >> 1, pl.multiple_of((share & 1) * half, 128)
            middle = sum_ref[pl.ds(4 + row, 1), pl.ds(low, half)]
            value = wide_sum(keep[i], got[i]) - lean[:, at] * wide_sum(lean_keep[i], lean_got[i])
            for p, column in zip((place, other), columns):
                value = value + outer(stats_ref[p, pl.ds(2 + row, 1), pl.ds(low, half)] - middle, column)
            if i < 2:
                mine[i] = value
            else:
                give[i - 2] = value.astype(BF16)


def quarter_kernel(left_ref, got_left_ref, right_ref, got_right_ref, mine_ref, give_ref):
    edge = left_ref.shape[2]
    for keep, got, at in (
        (left_ref, got_left_ref, slice(0, edge)),
        (right_ref, got_right_ref, slice(edge, 2 * edge)),
    ):
        mine_ref[:, at] = wide_sum(keep[0], got[0])
        give_ref[:, at] = half_sum(keep[1], got[1])


def spread_kernel(parted, *refs):
    if parted:
        shares, out_ref, hold = refs[:-2], refs[-2], refs[-1]
        for r, share in enumerate(shares):
            hold[r] = share[...]
    else:
        hold, out_ref = refs
    place, here = seat() if parted else 0, lax.axis_index("neur")
    half = hold.shape[1]
    block = out_ref.shape[0] // 4
    width = out_ref.shape[1]
    for b in range(4):
        for h in range(2):
            low, high = b * block + h * half, min(b * block + h * half + half, (b + 1) * block)
            which = (((here ^ b) * 2) + h) ^ place
            out_ref[low:high, :] = hold[which, : high - low, :width].astype(F32)


def wide_sum(a, b):
    return a.astype(F32) + b.astype(F32)


def half_sum(a, b):
    return wide_sum(a, b).astype(BF16)


def swap(x, bit, axis="seq"):
    n = lax.axis_size(axis)
    return lax.ppermute(x, axis, [(i, i ^ bit) for i in range(n)])


LEVEL = {4: 1, 2: 2, 1: 4}


def seat():
    place = lax.axis_index("seq")
    return ((place & 1) << 2) | (place & 2) | ((place >> 2) & 1)


def gather_first(v):
    return {0: v, 4: swap(v, LEVEL[4]), 2: swap(v, LEVEL[2]), 1: swap(v, LEVEL[1])}


def gather_rest(out):
    out = dict(out)
    out[2], out[4] = lax.optimization_barrier((out[2], out[4]))
    out[6] = swap(out[2], LEVEL[4])
    out[5] = swap(out[1], LEVEL[4])
    out[3] = swap(out[1], LEVEL[2])
    out[3], out[6] = lax.optimization_barrier((out[3], out[6]))
    out[7] = swap(out[3], LEVEL[4])
    return [out[r] for r in range(8)]


def per_device(devices_seq, *args):
    (
        tokens,
        w_first,
        gain_first,
        shift_first,
        decay_first,
        w_second,
        gain_second,
        shift_second,
        decay_second,
        cotangent,
        running_mean,
        running_var,
    ) = args
    _, length, real = tokens.shape
    width = -(-real // LANE) * LANE
    tiles = len(tiles_of(width))
    peers = devices_seq
    here = lax.axis_index("neur")
    tokens, cotangent = tokens[0], cotangent[0]

    scans = [
        pltpu.VMEM((tiles, length, LANE), F32),
        pltpu.VMEM((tiles, length + 8, LANE), F32),
    ]
    grads = [pltpu.VMEM((tiles, length, LANE), F32)]

    def share(stats):
        return lax.all_to_all(stats, "seq", 0, 0, tiled=True)

    def project(own, w, rows, *gives, aside=None):
        far = swap(own, 2, "neur")
        mate = swap(own, 1, "neur")
        w = lax.optimization_barrier((w, own))[0]
        w4, give, par = call(
            block_kernel,
            [shape(4, width, width, dtype=BF16), shape(2, width, width, dtype=BF16), shape(8, width)],
        )(w, *(row[None] for row in rows))
        part, means = call(project_early, [shape(length, width), shape(8, width)])(own, mate, w4)
        gives = [swap(lax.optimization_barrier((g, own))[0], 1, "neur") for g in gives + (give,)] if gives else give
        extra = aside(mate) if aside else ()
        far, part, par, gives, extra = lax.optimization_barrier((far, part, par, gives, extra))
        cross = swap(far, 1, "neur")
        part, means = call(project_middle, [shape(length, width), shape(8, width)])(part, means, far, w4)
        proj, stats = call(project_late, [shape(length, width), shape(peers, 8, width)])(
            part, means, cross, w4
        )
        return (own, mate, far, cross), proj, share(stats), w4, gives, par, extra

    def gradient(sums, gb, proj, summary, par):
        return call(grad_kernel, [shape(length, width, dtype=BF16), shape(8, width)])(
            sums, gb, proj, summary, par
        )

    def send(g, mate, w4, wm):
        out = call(send_kernel, shape(length, width, dtype=BF16))(g, mate, w4, wm)
        out, g, mate = lax.optimization_barrier((out, g, mate))
        got = swap(out, 2, "neur")
        keep = call(keep_kernel, shape(length, width))(g, mate, w4, wm)
        return keep, got

    half = width // 2

    def parts_shape(*lead):
        return shape(*lead, half, width, dtype=BF16)

    def weight_parts(*operands):
        if peers != 8:
            return call(functools.partial(weight_kernel, False), parts_shape(8))(*operands)
        return call(
            functools.partial(weight_kernel, True),
            [shape(4, half, half, dtype=BF16)] * 4,
            [pltpu.VMEM((8, half, width), BF16)],
        )(*operands)

    def weights(shares):
        if peers != 8:
            return call(functools.partial(spread_kernel, False), shape(4 * real, real))(shares)
        return call(
            functools.partial(spread_kernel, True),
            shape(4 * real, real),
            [pltpu.VMEM((8, half, width), BF16)],
        )(*shares)

    def together(*values):
        return lax.optimization_barrier(values)

    first_x, first_proj, first_stats, first_w, give, first_par, _ = project(
        tokens, w_first, (gain_first, shift_first, decay_first)
    )
    first_out, first_wide, first_sum = call(
        forward_kernel,
        [shape(length, real, dtype=BF16), shape(length, width), shape(8, width)],
        scans,
    )(first_stats, first_proj, first_par)

    def after(x, *earlier):
        return lax.optimization_barrier((x, earlier))[0]

    def leaning(mate):
        if peers != 8:
            return ()
        norm, norm_total = call(norm_kernel, [shape(length, width, dtype=BF16), shape(8, width)])(
            first_proj, after(first_sum, mate)
        )
        left, give_left, right, give_right = weight_parts(*first_x, norm, first_sum, norm_total)
        return left, swap(give_left, LEVEL[4]), right, swap(give_right, LEVEL[2])

    second_x, second_proj, second_stats, second_w, (first_mate, second_mate), second_par, lean = project(
        first_out, w_second, (gain_second, shift_second, decay_second), give, aside=leaning
    )
    second_out, second_gb, second_sums, second_sum, new_mean, new_var = call(
        turn_kernel,
        [
            shape(length, real, dtype=BF16),
            shape(length, width),
            shape(peers, 8, width),
            shape(8, width),
            shape(2, real),
            shape(2, real),
        ],
        scans
        + grads
        + [
            pltpu.VMEM((length, real), BF16),
            pltpu.VMEM((2, real), F32),
            pltpu.VMEM((2, real), F32),
            pltpu.SemaphoreType.DMA((3,)),
        ],
        in_specs=[pl.BlockSpec(memory_space=pltpu.VMEM)] * 4 + [pl.BlockSpec(memory_space=pl.ANY)] * 3,
    )(second_stats, second_proj, second_par, first_sum, cotangent, running_mean, running_var)

    second_sums = share(second_sums)
    second_g, second_total = gradient(second_sums, second_gb, second_proj, second_sum, second_par)
    mate = swap(second_g, 1, "neur")
    pairs = [shape(2, half, half), shape(2, half, half, dtype=BF16)] * 2
    rest = [shape(half, width), parts_shape()]
    second_parts = weight_parts(*second_x, second_g, second_sum, second_total)
    mate, second_parts = together(mate, second_parts)
    keep, got = send(second_g, mate, second_w, second_mate)
    if peers == 8:
        left, give_left, right, give_right = second_parts
        parcel = after((swap(give_left, LEVEL[4]), swap(give_right, LEVEL[2])), keep)
        left, give_left, right, give_right = call(halve_kernel, pairs)(left, parcel[0], right, parcel[1])
        keep, got, left = together(keep, got, left)
        parcel = swap(give_left, LEVEL[2]), swap(give_right, LEVEL[4])
    first_gb, first_sums, first_own = call(
        back_kernel,
        [shape(length, width), shape(peers, 8, width), shape(length, width, dtype=BF16)],
        scans + grads,
    )(keep, got, first_proj, first_wide, first_sum, first_par)
    if peers == 8:
        second_mine, give = call(quarter_kernel, rest)(left, parcel[0], right, parcel[1])
        first_sums, second_mine, give = together(first_sums, second_mine, give)
        left, give_left, right, give_right = weight_parts(
            *first_x, first_own, first_sum, jnp.zeros((8, width), F32)
        )
        parcel = swap(give_left, LEVEL[4]), swap(give_right, LEVEL[2])
    first_sums = share(first_sums)
    if peers == 8:
        first_sums, last, parcel = together(first_sums, swap(give, LEVEL[1]), parcel)
    first_g, first_total = gradient(first_sums, first_gb, first_proj, first_sum, first_par)
    mate = swap(first_g, 1, "neur")
    if peers == 8:
        left, give_left, right, give_right = call(functools.partial(settle_kernel, length), pairs)(
            left, parcel[0], right, parcel[1], *lean, first_sums, first_stats, first_sum, first_par
        )
        parcel = swap(give_left, LEVEL[2]), swap(give_right, LEVEL[4])
        mate, left = together(mate, left)
        keep, got = send(first_g, mate, first_w, first_mate)
        second_share = gather_first(half_sum(second_mine, last))
        mine, give = call(quarter_kernel, rest)(left, parcel[0], right, parcel[1])
        keep, first_share = together(keep, half_sum(mine, swap(give, LEVEL[1])))
        second_share = gather_rest(second_share)
        first_share = gather_rest(gather_first(first_share))
    else:
        first_parts = weight_parts(*first_x, first_g, first_sum, first_total)
        keep, got = send(first_g, mate, first_w, first_mate)
        second_share, first_share = lax.psum((second_parts, first_parts), "seq")
    grad_w_first = weights(first_share)
    grad_w_second = weights(second_share)
    input_grad = (keep + got.astype(F32))[:, :real]

    def pair(row):
        return jnp.stack([first_total[row, :real], second_total[row, :real]])

    return (
        first_out[None],
        second_out[None],
        input_grad[None],
        grad_w_first,
        grad_w_second,
        pair(1),
        pair(0),
        pair(2),
        new_mean,
        new_var,
    )


def solution(mesh):
    rows, line, flat = P("seq", None, "neur"), P("neur"), P(None, "neur")
    return jax.shard_map(
        functools.partial(per_device, mesh.shape["seq"]),
        mesh=mesh,
        in_specs=(rows, flat, line, line, line, flat, line, line, line, rows, flat, flat),
        out_specs=(rows, rows, rows) + (flat,) * 7,
        check_vma=False,
    )
```
